128 devices in a mesh: section: 2 (over z_hi), dp: 2 (over z_lo), tensor: 32 (over y, x, core).
Axes of the slice: x: 4, y: 4, z: 4 (z_hi: 2, z_lo: 2; z = z_hi * 2 + z_lo), core: 2. Of those that a mesh axis runs over, the one named last changes fastest.
Arguments:
- in_codes: bfloat16 [512, 16384], P(('section', 'dp'), 'tensor'), may hold values from -1 to 1
- in_scales: float32 [2, 128], P('section'), may hold values from 0.25 to 1
- query_weight: bfloat16 [2, 16384, 8192], P('section', None, 'tensor'), may hold values from -0.046875 to 0.046875
- kv_weight: bfloat16 [2, 16384, 2, 4, 128], P('section', None, None, None, 'tensor'), may hold values from -0.046875 to 0.046875
- out_weight: bfloat16 [2, 8192, 16384], P('section', 'tensor'), may hold values from -0.125 to 0.125
- kv_cache: bfloat16 [32, 4, 2, 128, 128], P(('section', 'dp')), may hold values from -2000 to 2000
- prefix_len: int32 [32], P(('section', 'dp')), may hold values from 32 to 128, as said below
- draft_parent: int32 [32, 16], P(('section', 'dp')), may hold values from 0 to 14, as said below
Outputs:
- next_codes: bfloat16 [512, 16384], P(('section', 'dp'), 'tensor')
- next_scales: float32 [2, 128], P('section')
The draws below stay inside these ranges and needn't reach their ends.
Inputs may be any that keep to these rules, and one draw needn't show every extreme that they name: `prefix_len`: some request of every draw has exactly 128 live positions and some exactly 32. `draft_parent`: token 0 names itself; every other token names an earlier token of its request.
All inputs are finite; a program needn't handle non-finite values. Where the reference program divides by a largest or mean magnitude, that divisor is 1e-20 or more.
Results may differ from the reference program's by a relative error of at most 0.014.
The reference program's roundings to bfloat16 on the way count: a program that leaves them out, or rounds other values in their place, can miss the bound.
Values may be sent and summed in bfloat16 or wider, within the bound.
No kernel may reach another device: no remote copies, remote signals or barrier semaphores. Data moves between devices by JAX's collectives and lax.ppermute only.
A program may use at most 128 MiB of HBM per device.

```python
import math
import jax
import jax.numpy as jnp
from jax import lax

D = 16384
HD = 128
GROUP = 16
RB = 128
BLOCK = 16
LEN = 128
HEADS = 64
KV_HEADS = 4
LAYERS = 2
REQS = 32
ROWS_ALL = 512
N_TENSOR = 32


def draw_in_codes(key, part):
    key = jax.random.fold_in(key, 11)
    rows_section = ROWS_ALL // LAYERS
    ramp = (jnp.arange(ROWS_ALL) % rows_section).astype(jnp.float32) / max(rows_section - 1, 1)
    values = jax.random.uniform(key, (ROWS_ALL, D), jnp.float32, -1.0, 1.0)
    factor = jnp.power(3.0, ramp - 1.0)
    return (values * factor[:, None]).astype(jnp.bfloat16)


def draw_kv_cache(key, part):
    key = jax.random.fold_in(key, 23)
    noise_key = jax.random.fold_in(key, 0)
    shape_all = (REQS, KV_HEADS, 2, LEN, HD)
    entries = jnp.clip(jax.random.normal(noise_key, shape_all, jnp.float32), -4.0, 4.0)
    return entries.astype(jnp.bfloat16)


def draw_prefix_len(key, part):
    key = jax.random.fold_in(key, 37)
    key_length, key_long, key_short = jax.random.split(key, 3)
    lengths = jax.random.randint(key_length, (REQS,), LEN // 4, LEN + 1)
    longest = jax.random.randint(key_long, (), 0, REQS)
    shortest = (longest + 1 + jax.random.randint(key_short, (), 0, REQS - 1)) % REQS
    index_all = jnp.arange(REQS)
    lengths = jnp.where(index_all == longest, LEN, lengths)
    lengths = jnp.where(index_all == shortest, LEN // 4, lengths)
    return lengths.astype(jnp.int32)


def draw_draft_parent(key, part):
    key = jax.random.fold_in(key, 41)
    limits = jnp.maximum(jnp.arange(BLOCK), 1)
    parents = jax.random.randint(key, (REQS, BLOCK), 0, limits[None, :])
    return parents.astype(jnp.int32)


def spiked(result, key, source, target, blocks, factor):
    def block_of(dim):
        return (jnp.arange(result.shape[dim]) // (result.shape[dim] // blocks)).reshape((-1,) + (1,) * (result.ndim - 1 - dim))

    near = jax.random.permutation(key, blocks)[block_of(target)]
    far = (block_of(target) + blocks // 2) % blocks
    return jnp.where((block_of(source) == near) | (block_of(source) == far), factor * result, result)


def block_scale(stream_key, extent, cuts, least, largest):
    level = 1.0
    for dim, shards_of in cuts:
        draws = jax.random.uniform(jax.random.fold_in(jax.random.fold_in(stream_key, 6), dim), (shards_of,), jnp.float32, least / len(cuts), largest / len(cuts))
        level = level * jnp.repeat(jnp.exp(draws), extent[dim] // shards_of).reshape((-1,) + (1,) * (len(extent) - 1 - dim))
    return level


def normal_values(key, shape, spread, limit, cuts=(), kind=jnp.bfloat16):
    values = jax.random.normal(key, shape, jnp.float32) * spread
    if len(cuts) > 0:
        values = block_scale(key, shape, cuts, -0.22, 0.18) * values
    return jnp.clip(values, min=-limit, max=limit).astype(kind)


def heavy_noise(stream_key, dims, scale, bound, cuts, heavy, kind=jnp.bfloat16):
    drawn = scale * jax.random.normal(stream_key, dims, jnp.float32)
    if cuts:
        drawn = drawn * block_scale(stream_key, dims, cuts, -0.22, 0.18)
    return jnp.clip(spiked(drawn, jax.random.fold_in(stream_key, 3), *heavy), -bound, bound).astype(kind)


def setup_inputs(seed: int = 0) -> dict:
    arg_keys = jax.random.split(jax.random.key(seed), 9)
    in_codes = draw_in_codes(jax.random.fold_in(arg_keys[8], 71), 0)
    in_scales = jnp.clip(jnp.exp(math.log(1.0) - 1.3862944 * jax.random.uniform(arg_keys[1], (LAYERS, D // RB), jnp.float32) ** block_scale(arg_keys[1], (LAYERS, D // RB), ((0, 2),), -0.2, 0.2)), 0.25, 1.0)
    query_weight = normal_values(arg_keys[2], (LAYERS, D, HEADS * HD), D ** -0.5, 0.046875, ((0, 2), (2, 32)))
    kv_weight = normal_values(arg_keys[3], (LAYERS, D, 2, KV_HEADS, HD), D ** -0.5, 0.046875, ((0, 2), (4, 32)))
    out_weight = heavy_noise(arg_keys[4], (LAYERS, HEADS * HD, D), (HEADS * HD) ** -0.5, 0.125, ((0, 2), (1, 32)), (1, 2, 32, 2.75))
    kv_cache = draw_kv_cache(jax.random.fold_in(arg_keys[8], 71), 0)
    prefix_len = draw_prefix_len(jax.random.fold_in(arg_keys[8], 71), 0)
    draft_parent = draw_draft_parent(jax.random.fold_in(arg_keys[8], 71), 0)
    return {"in_codes": in_codes, "in_scales": in_scales, "query_weight": query_weight, "kv_weight": kv_weight, "out_weight": out_weight, "kv_cache": kv_cache, "prefix_len": prefix_len, "draft_parent": draft_parent}


rope_base = 500000.0
tiny_value = 1e-06

def hadamard(order_size):
    row_index = lax.broadcasted_iota(jnp.int32, (order_size, order_size), 0)
    col_index = lax.broadcasted_iota(jnp.int32, (order_size, order_size), 1)
    common = row_index & col_index
    parity = jnp.zeros((order_size, order_size), jnp.int32)
    for bit_place in range(order_size.bit_length()):
        parity = parity + (common >> bit_place & 1)
    return jnp.where(parity % 2 == 0, 1.0, -1.0).astype(jnp.float32)

def decode_codes(code_rows, scales, rotation):
    block_size = rotation.shape[0]
    product_rows = jnp.dot(code_rows.reshape(-1, block_size), rotation.astype(jnp.bfloat16), preferred_element_type=jnp.float32)
    product_rows = product_rows.reshape(code_rows.shape[0], -1, block_size)
    factor = scales * (1.0 / math.sqrt(block_size))
    return (product_rows * factor[None, :, None]).reshape(code_rows.shape)

def rotate_rows(values, rotation):
    block_size = rotation.shape[0]
    product_rows = jnp.dot(values.reshape(-1, block_size), rotation, precision=lax.Precision.HIGHEST, preferred_element_type=jnp.float32)
    return product_rows.reshape(values.shape) * (1.0 / math.sqrt(block_size))

def rotate_pairs(values, position):
    half_size = values.shape[-1] // 2
    exponent = jnp.arange(half_size, dtype=jnp.float32) / half_size
    frequency = jnp.power(rope_base, -exponent)
    angles = position[..., None] * frequency
    cosine = jnp.cos(angles)
    sine_part = jnp.sin(angles)
    first_half = values[..., :half_size]
    second_half = values[..., half_size:]
    return jnp.concatenate([first_half * cosine - second_half * sine_part, second_half * cosine + first_half * sine_part], -1)

def ancestor_table(draft_parent):
    count_reqs, block_len = draft_parent.shape
    target = lax.broadcasted_iota(jnp.int32, (count_reqs, block_len, block_len), 2)
    source = lax.broadcasted_iota(jnp.int32, (count_reqs, block_len, block_len), 1)
    ancestry = ((target == draft_parent[:, :, None]) | (target == source)).astype(jnp.float32)
    for square_step in range(block_len.bit_length()):
        ancestry = jnp.minimum(jnp.einsum('rij,rjk->rik', ancestry, ancestry, precision=lax.Precision.HIGHEST), 1.0)
    return ancestry

def attend_exact(queries, cache_pair, keys_new, values_new, lengths, ancestry):
    count_reqs, block_len, heads_here, head_size = queries.shape
    highest = lax.Precision.HIGHEST
    score_scale = 1.0 / math.sqrt(head_size)
    merged = queries.reshape(count_reqs, block_len * heads_here, head_size).astype(jnp.float32)
    old_scores = jnp.einsum('rqd,rjd->rqj', merged, cache_pair[:, 0].astype(jnp.float32), precision=highest) * score_scale
    new_scores = jnp.einsum('rqd,rud->rqu', merged, keys_new.astype(jnp.float32), precision=highest) * score_scale
    positions = lax.broadcasted_iota(jnp.int32, old_scores.shape, 2)
    live_old = positions < lengths[:, None, None]
    live_new = jnp.repeat(ancestry > 0.5, heads_here, axis=1)
    row_max = jnp.maximum(lax.optimization_barrier(jnp.max(jnp.where(live_old, old_scores, -jnp.inf), -1)), lax.optimization_barrier(jnp.max(jnp.where(live_new, new_scores, -jnp.inf), -1)))
    old_exp = jnp.where(live_old, jnp.exp(old_scores - row_max[..., None]), 0.0)
    new_exp = jnp.where(live_new, jnp.exp(new_scores - row_max[..., None]), 0.0)
    denominator = lax.optimization_barrier(jnp.sum(old_exp, -1)) + lax.optimization_barrier(jnp.sum(new_exp, -1))
    old_weight = (old_exp / denominator[..., None]).astype(jnp.bfloat16)
    new_weight = (new_exp / denominator[..., None]).astype(jnp.bfloat16)
    blended = jnp.einsum('rqj,rjd->rqd', old_weight.astype(jnp.float32), cache_pair[:, 1].astype(jnp.float32), precision=highest)
    blended = blended + jnp.einsum('rqu,rud->rqd', new_weight.astype(jnp.float32), values_new.astype(jnp.float32), precision=highest)
    return blended.reshape(count_reqs, block_len, heads_here * head_size).astype(jnp.bfloat16)

def reference(in_codes, in_scales, query_weight, kv_weight, out_weight, kv_cache, prefix_len, draft_parent):
    rotation = hadamard(RB)
    reqs_section = REQS // LAYERS
    rows_section = reqs_section * BLOCK
    group_width = HEADS // N_TENSOR * HD
    codes_list = []
    scales_list = []
    for layer_index in range(LAYERS):
        in_block = in_codes[layer_index * rows_section:(layer_index + 1) * rows_section]
        decoded_full = decode_codes(in_block, in_scales[layer_index], rotation)
        layer_in = decoded_full.astype(jnp.bfloat16)
        queries = jnp.dot(layer_in, query_weight[layer_index], preferred_element_type=jnp.float32)
        draft_kv = jnp.dot(layer_in, kv_weight[layer_index].reshape(D, -1), preferred_element_type=jnp.float32).astype(jnp.bfloat16)
        draft_kv = draft_kv.reshape(rows_section, 2, KV_HEADS * HD)
        lengths = prefix_len[layer_index * reqs_section:(layer_index + 1) * reqs_section]
        parents = draft_parent[layer_index * reqs_section:(layer_index + 1) * reqs_section]
        ancestry = ancestor_table(parents)
        tree_depth = lax.optimization_barrier(jnp.sum(ancestry, -1)) - 1.0
        position = lengths.astype(jnp.float32)[:, None] + tree_depth
        queries = rotate_pairs(queries.reshape(reqs_section, BLOCK, HEADS, HD), position[:, :, None]).astype(jnp.bfloat16)
        draft_keys = rotate_pairs(draft_kv[:, 0].astype(jnp.float32).reshape(reqs_section, BLOCK, KV_HEADS, HD), position[:, :, None]).astype(jnp.bfloat16)
        draft_values = draft_kv[:, 1].reshape(reqs_section, BLOCK, KV_HEADS, HD)
        cache_block = kv_cache[layer_index * reqs_section:(layer_index + 1) * reqs_section]
        pieces = []
        for kv_rank in range(KV_HEADS):
            head_queries = queries[:, :, kv_rank * GROUP:(kv_rank + 1) * GROUP]
            pieces.append(attend_exact(head_queries, cache_block[:, kv_rank], draft_keys[:, :, kv_rank], draft_values[:, :, kv_rank], lengths, ancestry))
        attended = jnp.concatenate(pieces, 2).reshape(rows_section, HEADS * HD)
        summed = jnp.zeros((rows_section, D), jnp.float32)
        for head_group in range(N_TENSOR):
            partial_value = jnp.dot(attended[:, head_group * group_width:(head_group + 1) * group_width], out_weight[layer_index, head_group * group_width:(head_group + 1) * group_width], preferred_element_type=jnp.float32)
            rotated = rotate_rows(partial_value, rotation).reshape(rows_section, -1, RB)
            part_scale = lax.optimization_barrier(jnp.max(jnp.abs(rotated), -1)) + tiny_value
            part_codes = (rotated / part_scale[..., None]).astype(jnp.bfloat16)
            summed = summed + (part_codes.astype(jnp.float32) * part_scale[..., None]).reshape(rows_section, D)
        output_rows = decoded_full + rotate_rows(summed, rotation)
        rotated_out = rotate_rows(output_rows, rotation).reshape(rows_section, -1, RB)
        out_scale = lax.optimization_barrier(jnp.max(jnp.abs(rotated_out), axis=(0, 2))) + tiny_value
        out_codes = (rotated_out / out_scale[None, :, None]).reshape(rows_section, D).astype(jnp.bfloat16)
        codes_list.append(out_codes)
        scales_list.append(out_scale)
    next_codes = jnp.concatenate([codes_list[-1]] + codes_list[:-1], 0)
    next_scales = jnp.stack([scales_list[-1]] + scales_list[:-1], 0)
    return (next_codes, next_scales)
```

```python
import math

import jax
import jax.numpy as jnp
import numpy as np
from jax import lax
from jax.experimental import pallas as pl
from jax.experimental.pallas import tpu as pltpu
from jax.sharding import Mesh, PartitionSpec as P

HD = 128
RB = 128
CHIPS = 16
ROPE_BASE = 500000.0
TINY = 1e-06
TENSOR = ("y", "x", "core")
VMEM_LIMIT = 48 * 1024 * 1024
F32 = jnp.float32
BF16 = jnp.bfloat16
NT = (((1,), (1,)), ((), ()))


def hadamard():
    index = np.arange(RB)
    common = index[:, None] & index[None, :]
    parity = np.zeros((RB, RB), np.int32)
    for place in range(7):
        parity = parity + (common >> place & 1)
    return np.where(parity % 2 == 0, 1.0, -1.0).astype(np.float32)


def ancestor_table(draft_parent):
    count, size = draft_parent.shape
    target = lax.broadcasted_iota(jnp.int32, (count, size, size), 2)
    source = lax.broadcasted_iota(jnp.int32, (count, size, size), 1)
    table = ((target == draft_parent[:, :, None]) | (target == source)).astype(F32)
    for _ in range(4):
        table = jnp.minimum(jnp.einsum("rij,rjk->rik", table, table), 1.0)
    return table


def swapped(block, axis):
    return lax.ppermute(block, axis, [(0, 1), (1, 0)])


def params(**more):
    return pltpu.CompilerParams(vmem_limit_bytes=VMEM_LIMIT, **more)


def decode_kernel(core_ref, scale_ref, codes_ref, rotation_ref, kv_ref, rows_ref, kv_out_ref):
    step = pl.program_id(0)
    core = core_ref[0]
    total = jnp.zeros(kv_out_ref.shape, F32)
    for k in range(codes_ref.shape[0]):
        first = ((step * codes_ref.shape[0] + k) * 2 + core) * 4
        for half in range(2):
            product = jnp.dot(
                codes_ref[k, :, half * 256 : half * 256 + 256],
                rotation_ref[...],
                preferred_element_type=F32,
            )
            for b in range(2):
                factor = scale_ref[first + half * 2 + b] * F32(1.0 / math.sqrt(RB))
                at = k * 512 + half * 256 + b * 128
                rows_ref[:, at : at + 128] = (product[:, b * 128 : b * 128 + 128] * factor).astype(
                    BF16
                )
    total = lax.dot_general(kv_ref[...], rows_ref[...], NT, preferred_element_type=F32)

    @pl.when(step == 0)
    def _():
        kv_out_ref[...] = total

    @pl.when(step > 0)
    def _():
        kv_out_ref[...] += total


def decode(core, scales, codes, rotation, kv_weight):
    steps, each = 4, 4
    return pl.pallas_call(
        decode_kernel,
        grid_spec=pltpu.PrefetchScalarGridSpec(
            num_scalar_prefetch=2,
            grid=(steps,),
            in_specs=[
                pl.BlockSpec((each, 128, 512), lambda i, c, s: (i, 0, 0)),
                pl.BlockSpec((256, 256), lambda i, c, s: (0, 0)),
                pl.BlockSpec((64, each * 512), lambda i, c, s: (0, i)),
            ],
            out_specs=[
                pl.BlockSpec((128, each * 512), lambda i, c, s: (0, i)),
                pl.BlockSpec((64, 128), lambda i, c, s: (0, 0)),
            ],
        ),
        out_shape=[
            jax.ShapeDtypeStruct((128, 8192), BF16),
            jax.ShapeDtypeStruct((64, 128), F32),
        ],
        compiler_params=params(),
        cost_estimate=pl.CostEstimate(
            flops=2 * 128 * 8192 * 320, bytes_accessed=5 << 20, transcendentals=0
        ),
        name="decode",
    )(core, scales, codes, rotation, kv_weight)


def query_kernel(core_ref, rows_ref, own_ref, other_ref, own_out, other_out):
    own = jnp.zeros(own_out.shape, F32)
    other = jnp.zeros(own_out.shape, F32)
    for k in range(own_ref.shape[0]):
        rows = rows_ref[:, k * 512 : k * 512 + 512]
        own += jnp.dot(rows, own_ref[k, 0], preferred_element_type=F32)
        other += jnp.dot(rows, other_ref[k, 0], preferred_element_type=F32)

    @pl.when(pl.program_id(0) == 0)
    def _():
        own_out[...] = own
        other_out[...] = other

    @pl.when(pl.program_id(0) > 0)
    def _():
        own_out[...] += own
        other_out[...] += other


def project(core, rows, own_weight, other_weight):
    steps, each = 4, 4
    return pl.pallas_call(
        query_kernel,
        grid_spec=pltpu.PrefetchScalarGridSpec(
            num_scalar_prefetch=1,
            grid=(steps,),
            in_specs=[
                pl.BlockSpec((128, each * 512), lambda i, c: (0, i)),
                pl.BlockSpec((each, 1, 512, 256), lambda i, c: (i, c[0], 0, 0)),
                pl.BlockSpec((each, 1, 512, 256), lambda i, c: (i, c[0], 0, 0)),
            ],
            out_specs=[pl.BlockSpec((128, 256), lambda i, c: (0, 0))] * 2,
        ),
        out_shape=[jax.ShapeDtypeStruct((128, 256), F32)] * 2,
        compiler_params=params(),
        cost_estimate=pl.CostEstimate(
            flops=2 * 128 * 8192 * 512, bytes_accessed=10 << 20, transcendentals=0
        ),
        name="query",
    )(core, rows, own_weight, other_weight)


def attend_kernel(
    head_ref, length_ref, own_ref, recv_ref, kv_ref, cos_t, sin_t, cos_q, sin_q, mask_ref, cache_ref, out_ref
):
    score_scale = F32(1.0 / math.sqrt(HD))
    parts = [kv_ref[2 * j] + kv_ref[2 * j + 1] for j in range(CHIPS)]
    keys = jnp.concatenate([p[:8] for p in parts], 0).astype(BF16).astype(F32)
    values = jnp.concatenate([p[8:] for p in parts], 0).astype(BF16)
    low, high = keys[:64], keys[64:]
    keys = jnp.concatenate(
        [low * cos_t[...] - high * sin_t[...], high * cos_t[...] + low * sin_t[...]], 0
    ).astype(BF16)
    heads = []
    for h in range(2):
        q = own_ref[:, h * 128 : h * 128 + 128] + recv_ref[:, h * 128 : h * 128 + 128]
        q = q * cos_q[...] + pltpu.roll(q, 64, 1) * sin_q[...]
        heads.append(q.astype(BF16))
    fresh = [
        jnp.dot(q, keys, preferred_element_type=F32) * score_scale for q in heads
    ]
    lane = lax.broadcasted_iota(jnp.int32, (32, 128), 1)
    for r in range(8):
        rows = slice(r * 16, r * 16 + 16)
        q = jnp.concatenate([heads[0][rows], heads[1][rows]], 0)
        old = (
            lax.dot_general(q, cache_ref[r, 0, 0], NT, preferred_element_type=F32) * score_scale
        )
        new = jnp.concatenate([fresh[0][rows], fresh[1][rows]], 0)
        mask = jnp.concatenate([mask_ref[rows, :]] * 2, 0)
        old = jnp.where(lane < length_ref[r], old, -jnp.inf)
        new = jnp.where(mask > 0.5, new, -jnp.inf)
        peak = jnp.maximum(
            jnp.max(old, -1, keepdims=True), jnp.max(new, -1, keepdims=True)
        )
        old = jnp.exp(old - peak)
        new = jnp.exp(new - peak)
        total = jnp.sum(old, -1, keepdims=True) + jnp.sum(new, -1, keepdims=True)
        old = (old / total).astype(BF16)
        new = (new / total).astype(BF16)
        mixed = jnp.dot(old, cache_ref[r, 0, 1], preferred_element_type=F32)
        mixed = mixed + lax.dot_general(new, values, NT, preferred_element_type=F32)
        mixed = mixed.astype(BF16)
        out_ref[rows, 0:128] = mixed[:16]
        out_ref[rows, 128:256] = mixed[16:]


def attend(head, lengths, own, recv, kv, cos_t, sin_t, cos_q, sin_q, mask, cache):
    def whole(array):
        return pl.BlockSpec(array.shape, lambda i, h, n: (0,) * array.ndim)

    arrays = (own, recv, kv, cos_t, sin_t, cos_q, sin_q, mask)
    return pl.pallas_call(
        attend_kernel,
        grid_spec=pltpu.PrefetchScalarGridSpec(
            num_scalar_prefetch=2,
            grid=(1,),
            in_specs=[whole(a) for a in arrays]
            + [pl.BlockSpec((8, 1, 2, 128, 128), lambda i, h, n: (0, h[0], 0, 0, 0))],
            out_specs=pl.BlockSpec((128, 256), lambda i, h, n: (0, 0)),
        ),
        out_shape=jax.ShapeDtypeStruct((128, 256), BF16),
        compiler_params=params(),
        cost_estimate=pl.CostEstimate(
            flops=2 * 256 * 128 * 512, bytes_accessed=2 << 20, transcendentals=65536
        ),
        name="attend",
    )(head, lengths, *arrays, cache)


def partial_kernel(core_ref, mine_ref, theirs_ref, own_a, own_b, other_a, other_b, rotation_ref, out_ref):
    unit = F32(1.0 / math.sqrt(RB))
    for k, (own, other) in enumerate(((own_a, other_a), (own_b, other_b))):
        for half in range(2):
            at = half * 256
            groups = (
                jnp.dot(mine_ref[...], own[:, at : at + 256], preferred_element_type=F32),
                jnp.dot(theirs_ref[...], other[:, at : at + 256], preferred_element_type=F32),
            )
            for b in range(2):
                terms = []
                for group in groups:
                    block = group[:, b * 128 : b * 128 + 128]
                    coarse = block.astype(BF16)
                    fine = (block - coarse.astype(F32)).astype(BF16)
                    turned = lax.dot_general(
                        rotation_ref[...],
                        jnp.concatenate([coarse, fine], 1),
                        NT,
                        preferred_element_type=F32,
                    )
                    scale = jnp.max(jnp.abs(turned), 0, keepdims=True) * unit + TINY
                    codes = (turned * (unit / scale)).astype(BF16)
                    terms.append(codes.astype(F32) * scale)
                row = at + b * 128
                out_ref[k, row : row + 128, :] = (terms[0] + terms[1]).astype(BF16)


def partials(core, mine, theirs, own_weight, other_weight, rotation):
    return pl.pallas_call(
        partial_kernel,
        grid_spec=pltpu.PrefetchScalarGridSpec(
            num_scalar_prefetch=1,
            grid=(8,),
            in_specs=[
                pl.BlockSpec((128, 256), lambda i, c: (0, 0)),
                pl.BlockSpec((128, 256), lambda i, c: (0, 0)),
                pl.BlockSpec((256, 512), lambda i, c: (0, 4 * i + c[0])),
                pl.BlockSpec((256, 512), lambda i, c: (0, 4 * i + 2 + c[0])),
                pl.BlockSpec((256, 512), lambda i, c: (0, 4 * i + c[0])),
                pl.BlockSpec((256, 512), lambda i, c: (0, 4 * i + 2 + c[0])),
                pl.BlockSpec((128, 256), lambda i, c: (0, 0)),
            ],
            out_specs=pl.BlockSpec((2, 512, 128), lambda i, c: (i, 0, 0)),
        ),
        out_shape=jax.ShapeDtypeStruct((CHIPS, 512, 128), BF16),
        compiler_params=params(),
        cost_estimate=pl.CostEstimate(
            flops=2 * 128 * 8192 * 1024, bytes_accessed=12 << 20, transcendentals=0
        ),
        name="partials",
    )(core, mine, theirs, own_weight, own_weight, other_weight, other_weight, rotation)


def on_device(
    in_codes, in_scales, query_weight, kv_weight, out_weight, kv_cache, prefix_len, draft_parent
):
    core = lax.axis_index("core")
    head = lax.axis_index("y")
    rank = lax.axis_index(TENSOR)
    core_at = core.reshape(1)
    signs = hadamard()
    scales = in_scales[0]

    spread = jnp.broadcast_to(in_codes[None], (CHIPS, 128, 512))
    codes = lax.all_to_all(spread, ("y", "x"), 0, 0, tiled=True)

    wq = query_weight[0].reshape(CHIPS, 2, 512, 256)
    wq_other = swapped(query_weight, "core")[0].reshape(CHIPS, 2, 512, 256)
    wkv = kv_weight[0].transpose(2, 1, 3, 0).reshape(4, 2, 4, CHIPS, 2, 512)
    wkv_own = lax.dynamic_index_in_dim(wkv, core, 4, keepdims=False)
    wkv_other = swapped(lax.dynamic_index_in_dim(wkv, 1 - core, 4, keepdims=False), "core")
    first = jnp.where(core == 0, wkv_own, wkv_other)
    second = jnp.where(core == 0, wkv_other, wkv_own)
    wkv_both = jnp.stack([first, second], 2).reshape(64, 8192)
    wo = out_weight[0]
    wo_other = swapped(out_weight, "core")[0]

    ancestry = ancestor_table(draft_parent)
    position = prefix_len.astype(F32)[:, None] + (jnp.sum(ancestry, -1) - 1.0)
    frequency = jnp.power(ROPE_BASE, -(jnp.arange(64, dtype=F32) / 64))
    angles = position.reshape(128, 1) * frequency
    cosine, sine = jnp.cos(angles), jnp.sin(angles)
    cos_q = jnp.concatenate([cosine, cosine], 1)
    sin_q = jnp.concatenate([-sine, sine], 1)
    same = jnp.eye(8, dtype=F32)
    mask = (ancestry[:, :, None, :] * same[:, None, :, None]).reshape(128, 128)

    blocks = np.kron(np.eye(2, dtype=np.float32), signs)
    rows, kv_part = decode(core_at, scales, codes, jnp.asarray(blocks, BF16), wkv_both)
    kv = lax.all_to_all(
        jnp.broadcast_to(kv_part.reshape(4, 1, 16, 128), (4, 8, 16, 128)).reshape(32, 16, 128),
        TENSOR,
        0,
        0,
        tiled=True,
    )
    own, other = project(core_at, rows, wq, wq_other)
    recv = swapped(other, "core")
    attended = attend(
        head.reshape(1), prefix_len, own, recv, kv, cosine.T, sine.T, cos_q, sin_q, mask, kv_cache
    )
    theirs = swapped(attended, "core")
    twice = jnp.asarray(np.concatenate([signs, signs], 1), BF16)
    pieces = partials(core_at, attended, theirs, wo, wo_other, twice)
    pieces = lax.all_to_all(pieces, ("y", "x"), 0, 0, tiled=True)

    here = lax.dynamic_slice_in_dim(scales, rank * 4, 4)
    turned_in = in_codes.T.astype(F32) * jnp.repeat(here, RB)[:, None]
    turned = jnp.sum(pieces.astype(F32), 0) + turned_in
    peak = jnp.max(jnp.abs(turned.reshape(4, RB, 128)), (1, 2))
    everyone = lax.all_to_all(
        jnp.broadcast_to(peak[None], (64, 4)), ("dp",) + TENSOR, 0, 0, tiled=True
    )
    out_scale = jnp.max(everyone.reshape(2, 128), 0) + TINY
    both = jnp.maximum(peak, swapped(peak, "dp")) + TINY
    out_codes = (turned.T / jnp.repeat(both, RB)[None, :]).astype(BF16)
    next_codes = swapped(out_codes, "section")
    next_scales = swapped(out_scale[None], "section")
    return (next_codes, next_scales)


def solution(mesh):
    fine = Mesh(mesh.devices.reshape(2, 2, 4, 4, 2), ("section", "dp", "y", "x", "core"))
    rows = ("section", "dp")
    placed = (
        P(rows, TENSOR),
        P("section", None),
        P("section", None, TENSOR),
        P("section", None, None, None, TENSOR),
        P("section", TENSOR, None),
        P(rows, None, None, None, None),
        P(rows),
        P(rows, None),
    )
    return jax.shard_map(
        on_device,
        mesh=fine,
        in_specs=placed,
        out_specs=(P(rows, TENSOR), P("section", None)),
        check_vma=False,
    )
```

```python
import functools
import math

import jax
import jax.numpy as jnp
import numpy as np
from jax import lax
from jax.experimental import pallas as pl
from jax.experimental.pallas import tpu as pltpu
from jax.sharding import Mesh, PartitionSpec as P

HD = 128
RB = 128
CHIPS = 16
ROPE_BASE = 500000.0
TINY = 1e-06
TENSOR = ("y", "x", "core")
VMEM_LIMIT = 48 * 1024 * 1024
F32 = jnp.float32
BF16 = jnp.bfloat16
NT = (((1,), (1,)), ((), ()))


def hadamard():
    index = np.arange(RB)
    common = index[:, None] & index[None, :]
    parity = np.zeros((RB, RB), np.int32)
    for place in range(7):
        parity = parity + (common >> place & 1)
    return np.where(parity % 2 == 0, 1.0, -1.0).astype(np.float32)


def ancestor_table(draft_parent):
    count, size = draft_parent.shape
    target = lax.broadcasted_iota(jnp.int32, (count, size, size), 2)
    source = lax.broadcasted_iota(jnp.int32, (count, size, size), 1)
    table = ((target == draft_parent[:, :, None]) | (target == source)).astype(F32)
    for _ in range(4):
        table = jnp.minimum(jnp.einsum("rij,rjk->rik", table, table), 1.0)
    return table


def swapped(block, axis):
    return lax.ppermute(block, axis, [(0, 1), (1, 0)])


def shifted(block, axis, by):
    return lax.ppermute(block, axis, [(i, (i + by) % 4) for i in range(4)])


def params(**more):
    return pltpu.CompilerParams(vmem_limit_bytes=VMEM_LIMIT, **more)


def chip_a(place, hop, j):
    return lax.rem(place[1] + 4 - hop, 4) * 4 + lax.rem(place[2] + 4 - j, 4)


def chip_b(place, hop, j):
    return lax.rem(place[1] + 4 - j, 4) * 4 + lax.rem(place[2] + 4 - hop, 4)


def decode_kernel(
    hop, place, scale_ref, a_ref, b_ref, rotation_ref, kv_a, kv_b, kv_in, rows_ref, kv_out
):
    j = pl.program_id(0)
    chips = (chip_a(place, hop, j), chip_b(place, hop, j))
    total = jnp.zeros(kv_out.shape, F32)
    for half, (codes, weight) in enumerate(((a_ref, kv_a), (b_ref, kv_b))):
        first = (chips[half] * 2 + place[0]) * 4 + half * 2
        product = jnp.dot(codes[0], rotation_ref[...], preferred_element_type=F32)
        for b in range(2):
            factor = scale_ref[first + b] * F32(1.0 / math.sqrt(RB))
            at = half * 256 + b * 128
            rows_ref[:, at : at + 128] = (product[:, b * 128 : b * 128 + 128] * factor).astype(
                BF16
            )
        total += lax.dot_general(
            weight[...],
            rows_ref[:, half * 256 : half * 256 + 256],
            NT,
            preferred_element_type=F32,
        )

    @pl.when(j == 0)
    def _():
        kv_out[...] = kv_in[...] + total

    @pl.when(j > 0)
    def _():
        kv_out[...] += total


def decode(hop, place, scales, a, b, rotation, kv_weight, kv_in):
    return pl.pallas_call(
        functools.partial(decode_kernel, hop),
        grid_spec=pltpu.PrefetchScalarGridSpec(
            num_scalar_prefetch=2,
            grid=(4,),
            in_specs=[
                pl.BlockSpec((1, 128, 256), lambda j, p, s: (j, 0, 0)),
                pl.BlockSpec((1, 128, 256), lambda j, p, s: (j, 0, 0)),
                pl.BlockSpec((256, 256), lambda j, p, s: (0, 0)),
                pl.BlockSpec((64, 256), lambda j, p, s: (0, chip_a(p, hop, j) * 2)),
                pl.BlockSpec((64, 256), lambda j, p, s: (0, chip_b(p, hop, j) * 2 + 1)),
                pl.BlockSpec((64, 128), lambda j, p, s: (0, 0)),
            ],
            out_specs=[
                pl.BlockSpec((128, 512), lambda j, p, s: (0, j)),
                pl.BlockSpec((64, 128), lambda j, p, s: (0, 0)),
            ],
        ),
        out_shape=[
            jax.ShapeDtypeStruct((128, 2048), BF16),
            jax.ShapeDtypeStruct((64, 128), F32),
        ],
        compiler_params=params(),
        cost_estimate=pl.CostEstimate(
            flops=2 * 128 * 2048 * 320, bytes_accessed=5 << 18, transcendentals=0
        ),
        name="decode",
    )(place, scales, a, b, rotation, kv_weight, kv_weight, kv_in)


def query_kernel(place, rows, own_a, own_b, other_a, other_b, own_in, other_in, own_out, other_out):
    sums = []
    for first, second in ((own_a, own_b), (other_a, other_b)):
        sums.append(
            jnp.dot(rows[:, :256], first[...], preferred_element_type=F32)
            + jnp.dot(rows[:, 256:], second[...], preferred_element_type=F32)
        )

    @pl.when(pl.program_id(0) == 0)
    def _():
        own_out[...] = own_in[...] + sums[0]
        other_out[...] = other_in[...] + sums[1]

    @pl.when(pl.program_id(0) > 0)
    def _():
        own_out[...] += sums[0]
        other_out[...] += sums[1]


def project(hop, place, rows, own_weight, other_weight, own_in, other_in):
    at_a = pl.BlockSpec((256, 256), lambda j, p: ((chip_a(p, hop, j) * 2 + p[0]) * 2, 0))
    at_b = pl.BlockSpec((256, 256), lambda j, p: ((chip_b(p, hop, j) * 2 + p[0]) * 2 + 1, 0))
    still = pl.BlockSpec((128, 256), lambda j, p: (0, 0))
    return pl.pallas_call(
        query_kernel,
        grid_spec=pltpu.PrefetchScalarGridSpec(
            num_scalar_prefetch=1,
            grid=(4,),
            in_specs=[
                pl.BlockSpec((128, 512), lambda j, p: (0, j)),
                at_a,
                at_b,
                at_a,
                at_b,
                still,
                still,
            ],
            out_specs=[still, still],
        ),
        out_shape=[jax.ShapeDtypeStruct((128, 256), F32)] * 2,
        compiler_params=params(),
        cost_estimate=pl.CostEstimate(
            flops=2 * 128 * 2048 * 512, bytes_accessed=10 << 18, transcendentals=0
        ),
        name="query",
    )(place, rows, own_weight, own_weight, other_weight, other_weight, own_in, other_in)


def attend_kernel(
    head_ref, length_ref, own_ref, recv_ref, kv_ref, cos_t, sin_t, cos_q, sin_q, mask_ref, cache_ref, out_ref
):
    score_scale = F32(1.0 / math.sqrt(HD))
    parts = [kv_ref[2 * j] + kv_ref[2 * j + 1] for j in range(CHIPS)]
    keys = jnp.concatenate([p[:8] for p in parts], 0).astype(BF16).astype(F32)
    values = jnp.concatenate([p[8:] for p in parts], 0).astype(BF16)
    low, high = keys[:64], keys[64:]
    keys = jnp.concatenate(
        [low * cos_t[...] - high * sin_t[...], high * cos_t[...] + low * sin_t[...]], 0
    ).astype(BF16)
    heads = []
    for h in range(2):
        q = own_ref[:, h * 128 : h * 128 + 128] + recv_ref[:, h * 128 : h * 128 + 128]
        q = q * cos_q[...] + pltpu.roll(q, 64, 1) * sin_q[...]
        heads.append(q.astype(BF16))
    fresh = [
        jnp.dot(q, keys, preferred_element_type=F32) * score_scale for q in heads
    ]
    lane = lax.broadcasted_iota(jnp.int32, (32, 128), 1)
    for r in range(8):
        rows = slice(r * 16, r * 16 + 16)
        q = jnp.concatenate([heads[0][rows], heads[1][rows]], 0)
        old = (
            lax.dot_general(q, cache_ref[r, 0, 0], NT, preferred_element_type=F32) * score_scale
        )
        new = jnp.concatenate([fresh[0][rows], fresh[1][rows]], 0)
        mask = jnp.concatenate([mask_ref[rows, :]] * 2, 0)
        old = jnp.where(lane < length_ref[r], old, -jnp.inf)
        new = jnp.where(mask > 0.5, new, -jnp.inf)
        peak = jnp.maximum(
            jnp.max(old, -1, keepdims=True), jnp.max(new, -1, keepdims=True)
        )
        old = jnp.exp(old - peak)
        new = jnp.exp(new - peak)
        total = jnp.sum(old, -1, keepdims=True) + jnp.sum(new, -1, keepdims=True)
        old = (old / total).astype(BF16)
        new = (new / total).astype(BF16)
        mixed = jnp.dot(old, cache_ref[r, 0, 1], preferred_element_type=F32)
        mixed = mixed + lax.dot_general(new, values, NT, preferred_element_type=F32)
        mixed = mixed.astype(BF16)
        out_ref[rows, 0:128] = mixed[:16]
        out_ref[rows, 128:256] = mixed[16:]


def attend(head, lengths, own, recv, kv, cos_t, sin_t, cos_q, sin_q, mask, cache):
    def whole(array):
        return pl.BlockSpec(array.shape, lambda i, h, n: (0,) * array.ndim)

    arrays = (own, recv, kv, cos_t, sin_t, cos_q, sin_q, mask)
    return pl.pallas_call(
        attend_kernel,
        grid_spec=pltpu.PrefetchScalarGridSpec(
            num_scalar_prefetch=2,
            grid=(1,),
            in_specs=[whole(a) for a in arrays]
            + [pl.BlockSpec((8, 1, 2, 128, 128), lambda i, h, n: (0, h[0], 0, 0, 0))],
            out_specs=pl.BlockSpec((128, 256), lambda i, h, n: (0, 0)),
        ),
        out_shape=jax.ShapeDtypeStruct((128, 256), BF16),
        compiler_params=params(),
        cost_estimate=pl.CostEstimate(
            flops=2 * 256 * 128 * 512, bytes_accessed=2 << 20, transcendentals=65536
        ),
        name="attend",
    )(head, lengths, *arrays, cache)


def partial_kernel(
    place, mine, theirs, own_a, own_b, other_a, other_b, rotation_ref, out_a, out_b
):
    unit = F32(1.0 / math.sqrt(RB))
    for own, other, out_ref in ((own_a, other_a, out_a), (own_b, other_b, out_b)):
        groups = (
            jnp.dot(mine[...], own[...], preferred_element_type=F32),
            jnp.dot(theirs[...], other[...], preferred_element_type=F32),
        )
        for b in range(2):
            terms = []
            for group in groups:
                block = group[:, b * 128 : b * 128 + 128]
                coarse = block.astype(BF16)
                fine = (block - coarse.astype(F32)).astype(BF16)
                turned = lax.dot_general(
                    rotation_ref[...],
                    jnp.concatenate([coarse, fine], 1),
                    NT,
                    preferred_element_type=F32,
                )
                scale = jnp.max(jnp.abs(turned), 0, keepdims=True) * unit + TINY
                codes = (turned * (unit / scale)).astype(BF16)
                terms.append(codes.astype(F32) * scale)
            out_ref[0, b * 128 : b * 128 + 128, :] = (terms[0] + terms[1]).astype(out_ref.dtype)


def partials(hop, place, mine, theirs, own_weight, other_weight, rotation):
    def at_a(i, p):
        chip = lax.rem(p[1] + i, 4) * 4 + lax.rem(p[2] + hop, 4)
        return (0, (chip * 2 + p[0]) * 2)

    def at_b(i, p):
        chip = lax.rem(p[1] + hop, 4) * 4 + lax.rem(p[2] + i, 4)
        return (0, (chip * 2 + p[0]) * 2 + 1)

    kind = F32 if hop == 0 else BF16
    return pl.pallas_call(
        partial_kernel,
        grid_spec=pltpu.PrefetchScalarGridSpec(
            num_scalar_prefetch=1,
            grid=(4,),
            in_specs=[
                pl.BlockSpec((128, 256), lambda i, p: (0, 0)),
                pl.BlockSpec((128, 256), lambda i, p: (0, 0)),
                pl.BlockSpec((256, 256), at_a),
                pl.BlockSpec((256, 256), at_b),
                pl.BlockSpec((256, 256), at_a),
                pl.BlockSpec((256, 256), at_b),
                pl.BlockSpec((128, 256), lambda i, p: (0, 0)),
            ],
            out_specs=[pl.BlockSpec((1, 256, 128), lambda i, p: (i, 0, 0))] * 2,
        ),
        out_shape=[jax.ShapeDtypeStruct((4, 256, 128), kind)] * 2,
        compiler_params=params(),
        cost_estimate=pl.CostEstimate(
            flops=2 * 128 * 2048 * 1024, bytes_accessed=3 << 20, transcendentals=0
        ),
        name="partials",
    )(place, mine, theirs, own_weight, own_weight, other_weight, other_weight, rotation)


def on_device(
    in_codes, in_scales, query_weight, kv_weight, out_weight, kv_cache, prefix_len, draft_parent
):
    core = lax.axis_index("core")
    head = lax.axis_index("y")
    rank = lax.axis_index(TENSOR)
    place = jnp.stack([core, head, lax.axis_index("x")])
    signs = hadamard()
    scales = in_scales[0]

    first_a, first_b = in_codes[:, :256], in_codes[:, 256:]
    stack_a = jnp.stack([first_a] + [shifted(first_a, "x", k) for k in (1, 2, 3)])
    stack_b = jnp.stack([first_b] + [shifted(first_b, "y", k) for k in (1, 2, 3)])
    arrived = {0: (stack_a, stack_b)}
    for k in (1, 3, 2):
        arrived[k] = (shifted(stack_a, "y", k), shifted(stack_b, "x", k))

    wq = query_weight[0]
    wq_other = swapped(query_weight, "core")[0]
    wkv = kv_weight[0].transpose(2, 1, 3, 0).reshape(4, 2, 4, CHIPS, 2, 512)
    wkv_own = lax.dynamic_index_in_dim(wkv, core, 4, keepdims=False)
    wkv_other = swapped(lax.dynamic_index_in_dim(wkv, 1 - core, 4, keepdims=False), "core")
    first = jnp.where(core == 0, wkv_own, wkv_other)
    second = jnp.where(core == 0, wkv_other, wkv_own)
    wkv_both = jnp.stack([first, second], 2).reshape(64, 8192)
    wo = out_weight[0]
    wo_other = swapped(out_weight, "core")[0]

    ancestry = ancestor_table(draft_parent)
    position = prefix_len.astype(F32)[:, None] + (jnp.sum(ancestry, -1) - 1.0)
    frequency = jnp.power(ROPE_BASE, -(jnp.arange(64, dtype=F32) / 64))
    angles = position.reshape(128, 1) * frequency
    cosine, sine = jnp.cos(angles), jnp.sin(angles)
    cos_q = jnp.concatenate([cosine, cosine], 1)
    sin_q = jnp.concatenate([-sine, sine], 1)
    same = jnp.eye(8, dtype=F32)
    mask = (ancestry[:, :, None, :] * same[:, None, :, None]).reshape(128, 128)

    blocks = np.kron(np.eye(2, dtype=np.float32), signs)
    rotation = jnp.asarray(blocks, BF16)
    kv_part = jnp.zeros((64, 128), F32)
    own = other = jnp.zeros((128, 256), F32)
    for k in (0, 1, 3, 2):
        rows, kv_part = decode(k, place, scales, *arrived[k], rotation, wkv_both, kv_part)
        own, other = project(k, place, rows, wq, wq_other, own, other)
    kv = lax.all_to_all(
        jnp.broadcast_to(kv_part.reshape(4, 1, 16, 128), (4, 8, 16, 128)).reshape(32, 16, 128),
        TENSOR,
        0,
        0,
        tiled=True,
    )
    recv = swapped(other, "core")
    attended = attend(
        head.reshape(1), prefix_len, own, recv, kv, cosine.T, sine.T, cos_q, sin_q, mask, kv_cache
    )
    theirs = swapped(attended, "core")
    twice = jnp.asarray(np.concatenate([signs, signs], 1), BF16)
    sent = {}
    for k in (2, 1, 3, 0):
        sent[k] = partials(k, place, attended, theirs, wo, wo_other, twice)
    sum_a = sent[0][0]
    sum_b = sent[0][1]
    for k in (2, 1, 3):
        sum_a = sum_a + shifted(sent[k][0], "x", k).astype(F32)
        sum_b = sum_b + shifted(sent[k][1], "y", k).astype(F32)
    last_a, last_b = sum_a[0], sum_b[0]
    for k in (2, 1, 3):
        last_a = last_a + shifted(sum_a[k].astype(BF16), "y", k).astype(F32)
        last_b = last_b + shifted(sum_b[k].astype(BF16), "x", k).astype(F32)

    here = lax.dynamic_slice_in_dim(scales, rank * 4, 4)
    turned_in = in_codes.T.astype(F32) * jnp.repeat(here, RB)[:, None]
    turned = jnp.concatenate([last_a, last_b], 0) + turned_in
    peak = jnp.max(jnp.abs(turned.reshape(4, RB, 128)), (1, 2))
    next_peak = jnp.maximum(
        swapped(peak, "section"),
        lax.ppermute(peak, ("section", "dp"), [(0, 3), (1, 2), (2, 1), (3, 0)]),
    )
    next_rows = swapped(turned, "section").T
    scale_here = next_peak + TINY
    next_scales = lax.all_to_all(
        jnp.broadcast_to(scale_here[None], (32, 4)), TENSOR, 0, 0, tiled=True
    ).reshape(1, 128)
    next_codes = (next_rows / jnp.repeat(scale_here, RB)[None, :]).astype(BF16)
    return (next_codes, next_scales)


def solution(mesh):
    fine = Mesh(mesh.devices.reshape(2, 2, 4, 4, 2), ("section", "dp", "y", "x", "core"))
    rows = ("section", "dp")
    placed = (
        P(rows, TENSOR),
        P("section", None),
        P("section", None, TENSOR),
        P("section", None, None, None, TENSOR),
        P("section", TENSOR, None),
        P(rows, None, None, None, None),
        P(rows),
        P(rows, None),
    )
    return jax.shard_map(
        on_device,
        mesh=fine,
        in_specs=placed,
        out_specs=(P(rows, TENSOR), P("section", None)),
        check_vma=False,
    )
```

```python
import functools
import math

import jax
import jax.numpy as jnp
import numpy as np
from jax import lax
from jax.experimental import pallas as pl
from jax.experimental.pallas import tpu as pltpu
from jax.sharding import PartitionSpec as P

HD = 128
RB = 128
CHIPS = 16
ROPE_BASE = 500000.0
TINY = 1e-06
TENSOR = "tensor"


def device(y, x, core):
    return (y * 4 + x) * 2 + core


ACROSS = range(4)
X_ROWS = [[[device(y, x, c) for x in ACROSS] for y in ACROSS] for c in range(2)]
Y_ROWS = [[[device(y, x, c) for y in ACROSS] for x in ACROSS] for c in range(2)]
FIRST = X_ROWS[0] + Y_ROWS[1]
SECOND = Y_ROWS[0] + X_ROWS[1]
VMEM_LIMIT = 48 * 1024 * 1024
F32 = jnp.float32
BF16 = jnp.bfloat16
NT = (((1,), (1,)), ((), ()))


def hadamard():
    index = np.arange(RB)
    common = index[:, None] & index[None, :]
    parity = np.zeros((RB, RB), np.int32)
    for place in range(7):
        parity = parity + (common >> place & 1)
    return np.where(parity % 2 == 0, 1.0, -1.0).astype(np.float32)


def ancestor_table(draft_parent):
    count, size = draft_parent.shape
    target = lax.broadcasted_iota(jnp.int32, (count, size, size), 2)
    source = lax.broadcasted_iota(jnp.int32, (count, size, size), 1)
    table = ((target == draft_parent[:, :, None]) | (target == source)).astype(F32)
    for _ in range(4):
        table = jnp.minimum(jnp.einsum("rij,rjk->rik", table, table), 1.0)
    return table


def swapped(block, axis):
    return lax.ppermute(block, axis, [(0, 1), (1, 0)])


def traded(block):
    return lax.ppermute(block, TENSOR, [(i, i ^ 1) for i in range(32)])


def exchanged(pieces, groups=None):
    return lax.all_to_all(pieces, TENSOR, 0, 0, tiled=True, axis_index_groups=groups)


def gathered_chip(core, i, k):
    return jnp.where(core == 0, i * 4 + k, k * 4 + i)


def params(**more):
    return pltpu.CompilerParams(vmem_limit_bytes=VMEM_LIMIT, **more)


def decode_kernel(chip_of, place, scale_ref, codes_ref, rotation_ref, *refs):
    kv_refs, (kv_in, rows_ref, kv_out) = refs[:4], refs[4:]
    step = pl.program_id(0)
    for k in range(4):
        first = (chip_of(place, step, k) * 2 + place[0]) * 4
        for half in range(2):
            product = jnp.dot(
                codes_ref[0, k, :, half * 256 : half * 256 + 256],
                rotation_ref[...],
                preferred_element_type=F32,
            )
            for b in range(2):
                factor = scale_ref[first + half * 2 + b] * F32(1.0 / math.sqrt(RB))
                at = k * 512 + half * 256 + b * 128
                rows_ref[:, at : at + 128] = (product[:, b * 128 : b * 128 + 128] * factor).astype(
                    BF16
                )
    weight = jnp.concatenate([ref[...] for ref in kv_refs], 1)
    total = lax.dot_general(weight, rows_ref[...], NT, preferred_element_type=F32)

    def put(value):
        for h in range(4):
            for i in range(kv_out.shape[1]):
                kv_out[h, i] = value[h * 16 : h * 16 + 16]

    @pl.when(step == 0)
    def _():
        put(total + jnp.concatenate([kv_in[h, 0] for h in range(4)], 0))

    @pl.when(step > 0)
    def _():
        put(total + jnp.concatenate([kv_out[h, 0] for h in range(4)], 0))


def decode(steps, source, chip_of, copies, place, scales, codes, rotation, kv_weight, kv_in):
    def kv_at(k):
        return pl.BlockSpec((64, 512), lambda i, p, s: (0, chip_of(p, i, k)))

    return pl.pallas_call(
        functools.partial(decode_kernel, chip_of),
        grid_spec=pltpu.PrefetchScalarGridSpec(
            num_scalar_prefetch=2,
            grid=(steps,),
            in_specs=[
                pl.BlockSpec((1, 4, 128, 512), lambda i, p, s: (source(p, i), 0, 0, 0)),
                pl.BlockSpec((256, 256), lambda i, p, s: (0, 0)),
                *(kv_at(k) for k in range(4)),
                pl.BlockSpec((4, 1, 16, 128), lambda i, p, s: (0, 0, 0, 0)),
            ],
            out_specs=[
                pl.BlockSpec((128, 2048), lambda i, p, s: (0, i)),
                pl.BlockSpec((4, copies, 16, 128), lambda i, p, s: (0, 0, 0, 0)),
            ],
        ),
        out_shape=[
            jax.ShapeDtypeStruct((128, steps * 2048), BF16),
            jax.ShapeDtypeStruct((4, copies, 16, 128), F32),
        ],
        compiler_params=params(),
        cost_estimate=pl.CostEstimate(
            flops=2 * 128 * 2048 * 320 * steps, bytes_accessed=steps << 20, transcendentals=0
        ),
        name="decode",
    )(place, scales, codes, rotation, *[kv_weight] * 4, kv_in)


def query_kernel(place, rows_ref, *refs):
    own_refs, other_refs, (own_in, other_in, own_out, other_out) = refs[:4], refs[4:8], refs[8:]
    sums = []
    for weights in (own_refs, other_refs):
        total = jnp.zeros(own_out.shape, F32)
        for k in range(4):
            total += jnp.dot(
                rows_ref[:, k * 512 : k * 512 + 512], weights[k][...], preferred_element_type=F32
            )
        sums.append(total)

    @pl.when(pl.program_id(0) == 0)
    def _():
        own_out[...] = own_in[...] + sums[0]
        other_out[...] = other_in[...] + sums[1]

    @pl.when(pl.program_id(0) > 0)
    def _():
        own_out[...] += sums[0]
        other_out[...] += sums[1]


def project(steps, chip_of, place, rows, own_weight, other_weight, own_in, other_in):
    def weight_at(k):
        return pl.BlockSpec((512, 256), lambda i, p: (chip_of(p, i, k) * 2 + p[0], 0))

    still = pl.BlockSpec((128, 256), lambda i, p: (0, 0))
    return pl.pallas_call(
        query_kernel,
        grid_spec=pltpu.PrefetchScalarGridSpec(
            num_scalar_prefetch=1,
            grid=(steps,),
            in_specs=[pl.BlockSpec((128, 2048), lambda i, p: (0, i))]
            + [weight_at(k) for k in range(4)] * 2
            + [still, still],
            out_specs=[still, still],
        ),
        out_shape=[jax.ShapeDtypeStruct((128, 256), F32)] * 2,
        compiler_params=params(),
        cost_estimate=pl.CostEstimate(
            flops=2 * 128 * 2048 * 512 * steps, bytes_accessed=steps * 5 << 19, transcendentals=0
        ),
        name="query",
    )(place, rows, *[own_weight] * 4, *[other_weight] * 4, own_in, other_in)


def attend_kernel(
    head_ref, length_ref, own_ref, recv_ref, kv_ref, cos_t, sin_t, cos_q, sin_q, mask_ref, cache_ref, out_ref
):
    score_scale = F32(1.0 / math.sqrt(HD))
    parts = [kv_ref[2 * j] + kv_ref[2 * j + 1] for j in range(CHIPS)]
    keys = jnp.concatenate([p[:8] for p in parts], 0).astype(BF16).astype(F32)
    values = jnp.concatenate([p[8:] for p in parts], 0).astype(BF16)
    low, high = keys[:64], keys[64:]
    keys = jnp.concatenate(
        [low * cos_t[...] - high * sin_t[...], high * cos_t[...] + low * sin_t[...]], 0
    ).astype(BF16)
    heads = []
    for h in range(2):
        q = own_ref[:, h * 128 : h * 128 + 128] + recv_ref[:, h * 128 : h * 128 + 128]
        q = q * cos_q[...] + pltpu.roll(q, 64, 1) * sin_q[...]
        heads.append(q.astype(BF16))
    fresh = [
        jnp.dot(q, keys, preferred_element_type=F32) * score_scale for q in heads
    ]
    lane = lax.broadcasted_iota(jnp.int32, (32, 128), 1)
    for r in range(8):
        rows = slice(r * 16, r * 16 + 16)
        q = jnp.concatenate([heads[0][rows], heads[1][rows]], 0)
        old = (
            lax.dot_general(q, cache_ref[r, 0, 0], NT, preferred_element_type=F32) * score_scale
        )
        new = jnp.concatenate([fresh[0][rows], fresh[1][rows]], 0)
        mask = jnp.concatenate([mask_ref[rows, :]] * 2, 0)
        old = jnp.where(lane < length_ref[r], old, -jnp.inf)
        new = jnp.where(mask > 0.5, new, -jnp.inf)
        peak = jnp.maximum(
            jnp.max(old, -1, keepdims=True), jnp.max(new, -1, keepdims=True)
        )
        old = jnp.exp(old - peak)
        new = jnp.exp(new - peak)
        total = jnp.sum(old, -1, keepdims=True) + jnp.sum(new, -1, keepdims=True)
        old = (old / total).astype(BF16)
        new = (new / total).astype(BF16)
        mixed = jnp.dot(old, cache_ref[r, 0, 1], preferred_element_type=F32)
        mixed = mixed + lax.dot_general(new, values, NT, preferred_element_type=F32)
        mixed = mixed.astype(BF16)
        out_ref[rows, 0:128] = mixed[:16]
        out_ref[rows, 128:256] = mixed[16:]


def attend(head, lengths, own, recv, kv, cos_t, sin_t, cos_q, sin_q, mask, cache):
    def whole(array):
        return pl.BlockSpec(array.shape, lambda i, h, n: (0,) * array.ndim)

    arrays = (own, recv, kv, cos_t, sin_t, cos_q, sin_q, mask)
    return pl.pallas_call(
        attend_kernel,
        grid_spec=pltpu.PrefetchScalarGridSpec(
            num_scalar_prefetch=2,
            grid=(1,),
            in_specs=[whole(a) for a in arrays]
            + [pl.BlockSpec((8, 1, 2, 128, 128), lambda i, h, n: (0, h[0], 0, 0, 0))],
            out_specs=pl.BlockSpec((128, 256), lambda i, h, n: (0, 0)),
        ),
        out_shape=jax.ShapeDtypeStruct((128, 256), BF16),
        compiler_params=params(),
        cost_estimate=pl.CostEstimate(
            flops=2 * 256 * 128 * 512, bytes_accessed=2 << 20, transcendentals=65536
        ),
        name="attend",
    )(head, lengths, *arrays, cache)


def partial_kernel(core_ref, mine_ref, theirs_ref, own_a, own_b, other_a, other_b, rotation_ref, out_ref):
    unit = F32(1.0 / math.sqrt(RB))
    for k, (own, other) in enumerate(((own_a, other_a), (own_b, other_b))):
        for half in range(2):
            at = half * 256
            groups = (
                jnp.dot(mine_ref[...], own[:, at : at + 256], preferred_element_type=F32),
                jnp.dot(theirs_ref[...], other[:, at : at + 256], preferred_element_type=F32),
            )
            for b in range(2):
                terms = []
                for group in groups:
                    block = group[:, b * 128 : b * 128 + 128]
                    coarse = block.astype(BF16)
                    fine = (block - coarse.astype(F32)).astype(BF16)
                    turned = lax.dot_general(
                        rotation_ref[...],
                        jnp.concatenate([coarse, fine], 1),
                        NT,
                        preferred_element_type=F32,
                    )
                    scale = jnp.max(jnp.abs(turned), 0, keepdims=True) * unit + TINY
                    codes = (turned * (unit / scale)).astype(BF16)
                    terms.append(codes.astype(F32) * scale)
                row = at + b * 128
                out_ref[k, row : row + 128, :] = (terms[0] + terms[1]).astype(BF16)


def partials(place, mine, theirs, own_weight, other_weight, rotation):
    def weight_at(k):
        def at(i, p):
            chip = jnp.where(p[0] == 0, lax.rem(2 * i + k, 4) * 4 + i // 2, 2 * i + k)
            return (0, chip * 2 + p[0])

        return pl.BlockSpec((256, 512), at)

    return pl.pallas_call(
        partial_kernel,
        grid_spec=pltpu.PrefetchScalarGridSpec(
            num_scalar_prefetch=1,
            grid=(8,),
            in_specs=[
                pl.BlockSpec((128, 256), lambda i, p: (0, 0)),
                pl.BlockSpec((128, 256), lambda i, p: (0, 0)),
                weight_at(0),
                weight_at(1),
                weight_at(0),
                weight_at(1),
                pl.BlockSpec((128, 256), lambda i, p: (0, 0)),
            ],
            out_specs=pl.BlockSpec((2, 512, 128), lambda i, p: (i, 0, 0)),
        ),
        out_shape=jax.ShapeDtypeStruct((CHIPS, 512, 128), BF16),
        compiler_params=params(),
        cost_estimate=pl.CostEstimate(
            flops=2 * 128 * 8192 * 1024, bytes_accessed=12 << 20, transcendentals=0
        ),
        name="partials",
    )(place, mine, theirs, own_weight, own_weight, other_weight, other_weight, rotation)


def on_device(
    in_codes, in_scales, query_weight, kv_weight, out_weight, kv_cache, prefix_len, draft_parent
):
    rank = lax.axis_index(TENSOR)
    core = rank % 2
    head = rank // 8
    along_x = rank // 2 % 4
    second = jnp.where(core == 0, head, along_x)
    place = jnp.stack([core, second])
    signs = hadamard()
    scales = in_scales[0]

    near = exchanged(jnp.broadcast_to(in_codes[None], (4, 128, 512)), FIRST)
    far = exchanged(jnp.broadcast_to(near[None], (4, 4, 128, 512)), SECOND)

    wq = query_weight[0]
    wq_other = traded(query_weight)[0]
    wkv = kv_weight[0].transpose(2, 1, 3, 0).reshape(4, 2, 4, CHIPS, 2, 512)
    wkv_own = lax.dynamic_index_in_dim(wkv, core, 4, keepdims=False)
    wkv_other = traded(lax.dynamic_index_in_dim(wkv, 1 - core, 4, keepdims=False))
    low = jnp.where(core == 0, wkv_own, wkv_other)
    high = jnp.where(core == 0, wkv_other, wkv_own)
    wkv_both = jnp.stack([low, high], 2).reshape(64, 8192)
    wo = out_weight[0]
    wo_other = traded(out_weight)[0]

    ancestry = ancestor_table(draft_parent)
    position = prefix_len.astype(F32)[:, None] + (jnp.sum(ancestry, -1) - 1.0)
    frequency = jnp.power(ROPE_BASE, -(jnp.arange(64, dtype=F32) / 64))
    angles = position.reshape(128, 1) * frequency
    cosine, sine = jnp.cos(angles), jnp.sin(angles)
    cos_q = jnp.concatenate([cosine, cosine], 1)
    sin_q = jnp.concatenate([-sine, sine], 1)
    same = jnp.eye(8, dtype=F32)
    mask = (ancestry[:, :, None, :] * same[:, None, :, None]).reshape(128, 128)

    blocks = np.kron(np.eye(2, dtype=np.float32), signs)
    rotation = jnp.asarray(blocks, BF16)

    def near_chip(p, i, k):
        return gathered_chip(p[0], p[1], k)

    def far_source(p, i):
        return lax.rem(p[1] + 1 + i, 4)

    def far_chip(p, i, k):
        return gathered_chip(p[0], far_source(p, i), k)

    rows, kv_part = decode(
        1, lambda p, i: 0, near_chip, 1, place, scales, near[None], rotation, wkv_both,
        jnp.zeros((4, 1, 16, 128), F32),
    )
    none = jnp.zeros((128, 256), F32)
    own, other = project(1, near_chip, place, rows, wq, wq_other, none, none)
    rows, kv_part = decode(
        3, far_source, far_chip, 8, place, scales, far, rotation, wkv_both, kv_part
    )
    kv = exchanged(kv_part.reshape(32, 16, 128))
    own, other = project(3, far_chip, place, rows, wq, wq_other, own, other)
    recv = traded(other)
    attended = attend(
        head.reshape(1), prefix_len, own, recv, kv, cosine.T, sine.T, cos_q, sin_q, mask, kv_cache
    )
    theirs = traded(attended)
    twice = jnp.asarray(np.concatenate([signs, signs], 1), BF16)
    pieces = partials(place, attended, theirs, wo, wo_other, twice)
    pieces = exchanged(pieces.reshape(4, 4, 512, 128), FIRST)
    pieces = exchanged(jnp.sum(pieces.astype(F32), 0).astype(BF16), SECOND)

    here = lax.dynamic_slice_in_dim(scales, rank * 4, 4)
    turned_in = in_codes.T.astype(F32) * jnp.repeat(here, RB)[:, None]
    turned = jnp.sum(pieces.astype(F32), 0) + turned_in
    peak = jnp.max(jnp.abs(turned.reshape(4, RB, 128)), (1, 2))
    next_rows = swapped(turned, "section")
    next_peak = swapped(peak, "section")
    everyone = lax.all_to_all(
        jnp.broadcast_to(next_peak[None], (64, 4)), ("dp", TENSOR), 0, 0, tiled=True
    )
    next_scales = jnp.max(everyone.reshape(2, 128), 0) + TINY
    scale_here = lax.dynamic_slice_in_dim(next_scales, rank * 4, 4)
    next_codes = (next_rows.T / jnp.repeat(scale_here, RB)[None, :]).astype(BF16)
    return (next_codes, next_scales[None])


def solution(mesh):
    rows = ("section", "dp")
    placed = (
        P(rows, TENSOR),
        P("section", None),
        P("section", None, TENSOR),
        P("section", None, None, None, TENSOR),
        P("section", TENSOR, None),
        P(rows, None, None, None, None),
        P(rows),
        P(rows, None),
    )
    return jax.shard_map(
        on_device,
        mesh=mesh,
        in_specs=placed,
        out_specs=(P(rows, TENSOR), P("section", None)),
        check_vma=False,
    )
```

```python
import functools
import math

import jax
import jax.numpy as jnp
import numpy as np
from jax import lax
from jax.experimental import pallas as pl
from jax.experimental.pallas import tpu as pltpu
from jax.sharding import PartitionSpec as P

HD = 128
RB = 128
CHIPS = 16
ROPE_BASE = 500000.0
TINY = 1e-06
TENSOR = "tensor"


def device(y, x, core):
    return (y * 4 + x) * 2 + core


VMEM_LIMIT = 48 * 1024 * 1024
F32 = jnp.float32
BF16 = jnp.bfloat16
NT = (((1,), (1,)), ((), ()))


def hadamard():
    index = np.arange(RB)
    common = index[:, None] & index[None, :]
    parity = np.zeros((RB, RB), np.int32)
    for place in range(7):
        parity = parity + (common >> place & 1)
    return np.where(parity % 2 == 0, 1.0, -1.0).astype(np.float32)


def ancestor_table(draft_parent):
    count, size = draft_parent.shape
    target = lax.broadcasted_iota(jnp.int32, (count, size, size), 2)
    source = lax.broadcasted_iota(jnp.int32, (count, size, size), 1)
    table = ((target == draft_parent[:, :, None]) | (target == source)).astype(F32)
    for _ in range(4):
        table = jnp.minimum(jnp.einsum("rij,rjk->rik", table, table), 1.0)
    return table


def swapped(block, axis):
    return lax.ppermute(block, axis, [(0, 1), (1, 0)])


def traded(block):
    return lax.ppermute(block, TENSOR, [(i, i ^ 1) for i in range(32)])


def exchanged(pieces):
    return lax.all_to_all(pieces, TENSOR, 0, 0, tiled=True)


def shifted(block, by, second):
    pairs = []
    for y in range(4):
        for x in range(4):
            for core in range(2):
                along_y = (core == 1) != second
                to_y, to_x = ((y + by) % 4, x) if along_y else (y, (x + by) % 4)
                pairs.append((device(y, x, core), device(to_y, to_x, core)))
    return lax.ppermute(block, TENSOR, pairs)


def first_shift(block, by):
    return shifted(block, by, False)


def second_shift(block, by):
    return shifted(block, by, True)


def chip_at(place, first, second):
    first = lax.rem(place[1] + 4 + first, 4)
    second = lax.rem(place[2] + 4 + second, 4)
    return jnp.where(place[0] == 0, second * 4 + first, first * 4 + second)


def hadamard():
    index = np.arange(RB)
    common = index[:, None] & index[None, :]
    parity = np.zeros((RB, RB), np.int32)
    for place in range(7):
        parity = parity + (common >> place & 1)
    return np.where(parity % 2 == 0, 1.0, -1.0).astype(np.float32)


def ancestor_table(draft_parent):
    count, size = draft_parent.shape
    target = lax.broadcasted_iota(jnp.int32, (count, size, size), 2)
    source = lax.broadcasted_iota(jnp.int32, (count, size, size), 1)
    table = ((target == draft_parent[:, :, None]) | (target == source)).astype(F32)
    for _ in range(4):
        table = jnp.minimum(jnp.einsum("rij,rjk->rik", table, table), 1.0)
    return table


def swapped(block, axis):
    return lax.ppermute(block, axis, [(0, 1), (1, 0)])


def traded(block):
    return lax.ppermute(block, TENSOR, [(i, i ^ 1) for i in range(32)])


def exchanged(pieces, groups=None):
    return lax.all_to_all(pieces, TENSOR, 0, 0, tiled=True, axis_index_groups=groups)


def params(**more):
    return pltpu.CompilerParams(vmem_limit_bytes=VMEM_LIMIT, **more)


def decode_kernel(hop, place, scale_ref, codes_ref, rotation_ref, *refs):
    kv_refs, (kv_in, rows_ref, kv_out) = refs[:4], refs[4:]
    for k in range(4):
        first = (chip_at(place, -k, -hop) * 2 + place[0]) * 4
        for half in range(2):
            product = jnp.dot(
                codes_ref[k, :, half * 256 : half * 256 + 256],
                rotation_ref[...],
                preferred_element_type=F32,
            )
            for b in range(2):
                factor = scale_ref[first + half * 2 + b] * F32(1.0 / math.sqrt(RB))
                at = k * 512 + half * 256 + b * 128
                rows_ref[:, at : at + 128] = (product[:, b * 128 : b * 128 + 128] * factor).astype(
                    BF16
                )
    weight = jnp.concatenate([ref[...] for ref in kv_refs], 1)
    total = lax.dot_general(weight, rows_ref[...], NT, preferred_element_type=F32)
    for h in range(4):
        value = total[h * 16 : h * 16 + 16] + kv_in[h, 0]
        for i in range(kv_out.shape[1]):
            kv_out[h, i] = value


def decode(hop, copies, place, scales, codes, rotation, kv_weight, kv_in):
    def kv_at(k):
        return pl.BlockSpec((64, 512), lambda i, p, s: (0, chip_at(p, -k, -hop)))

    return pl.pallas_call(
        functools.partial(decode_kernel, hop),
        grid_spec=pltpu.PrefetchScalarGridSpec(
            num_scalar_prefetch=2,
            grid=(1,),
            in_specs=[
                pl.BlockSpec((4, 128, 512), lambda i, p, s: (0, 0, 0)),
                pl.BlockSpec((256, 256), lambda i, p, s: (0, 0)),
                *(kv_at(k) for k in range(4)),
                pl.BlockSpec((4, 1, 16, 128), lambda i, p, s: (0, 0, 0, 0)),
            ],
            out_specs=[
                pl.BlockSpec((128, 2048), lambda i, p, s: (0, 0)),
                pl.BlockSpec((4, copies, 16, 128), lambda i, p, s: (0, 0, 0, 0)),
            ],
        ),
        out_shape=[
            jax.ShapeDtypeStruct((128, 2048), BF16),
            jax.ShapeDtypeStruct((4, copies, 16, 128), F32),
        ],
        compiler_params=params(),
        cost_estimate=pl.CostEstimate(
            flops=2 * 128 * 2048 * 320, bytes_accessed=1 << 20, transcendentals=0
        ),
        name="decode",
    )(place, scales, codes, rotation, *[kv_weight] * 4, kv_in)


def query_kernel(steps, place, *refs):
    rows_refs, refs = refs[:steps], refs[steps:]
    own_refs, other_refs, (own_in, other_in, own_out, other_out) = refs[:4], refs[4:8], refs[8:]

    def at_step(step):
        @pl.when(pl.program_id(0) == step)
        def _():
            for weights, start, out in (
                (own_refs, own_in, own_out),
                (other_refs, other_in, other_out),
            ):
                total = start[...] if step == 0 else out[...]
                for k in range(4):
                    total += jnp.dot(
                        rows_refs[step][:, k * 512 : k * 512 + 512],
                        weights[k][...],
                        preferred_element_type=F32,
                    )
                out[...] = total

    for step in range(steps):
        at_step(step)


def project(hops, place, rows, own_weight, other_weight, own_in, other_in):
    steps = len(hops)

    def weight_at(k):
        def at(i, p):
            hop = hops[0]
            for step in range(1, steps):
                hop = jnp.where(i == step, hops[step], hop)
            return (chip_at(p, -k, -hop) * 2 + p[0], 0)

        return pl.BlockSpec((512, 256), at)

    still = pl.BlockSpec((128, 256), lambda i, p: (0, 0))
    return pl.pallas_call(
        functools.partial(query_kernel, steps),
        grid_spec=pltpu.PrefetchScalarGridSpec(
            num_scalar_prefetch=1,
            grid=(steps,),
            in_specs=[pl.BlockSpec((128, 2048), lambda i, p: (0, 0))] * steps
            + [weight_at(k) for k in range(4)] * 2
            + [still, still],
            out_specs=[still, still],
        ),
        out_shape=[jax.ShapeDtypeStruct((128, 256), F32)] * 2,
        compiler_params=params(),
        cost_estimate=pl.CostEstimate(
            flops=2 * 128 * 2048 * 512 * steps, bytes_accessed=steps * 5 << 19, transcendentals=0
        ),
        name="query",
    )(place, *rows, *[own_weight] * 4, *[other_weight] * 4, own_in, other_in)


def attend_kernel(
    head_ref, length_ref, own_ref, recv_ref, kv_ref, cos_t, sin_t, cos_q, sin_q, mask_ref, cache_ref, out_ref
):
    score_scale = F32(1.0 / math.sqrt(HD))
    parts = [kv_ref[2 * j] + kv_ref[2 * j + 1] for j in range(CHIPS)]
    keys = jnp.concatenate([p[:8] for p in parts], 0).astype(BF16).astype(F32)
    values = jnp.concatenate([p[8:] for p in parts], 0).astype(BF16)
    low, high = keys[:64], keys[64:]
    keys = jnp.concatenate(
        [low * cos_t[...] - high * sin_t[...], high * cos_t[...] + low * sin_t[...]], 0
    ).astype(BF16)
    heads = []
    for h in range(2):
        q = own_ref[:, h * 128 : h * 128 + 128] + recv_ref[:, h * 128 : h * 128 + 128]
        q = q * cos_q[...] + pltpu.roll(q, 64, 1) * sin_q[...]
        heads.append(q.astype(BF16))
    fresh = [
        jnp.dot(q, keys, preferred_element_type=F32) * score_scale for q in heads
    ]
    lane = lax.broadcasted_iota(jnp.int32, (32, 128), 1)
    for r in range(8):
        rows = slice(r * 16, r * 16 + 16)
        q = jnp.concatenate([heads[0][rows], heads[1][rows]], 0)
        old = (
            lax.dot_general(q, cache_ref[r, 0, 0], NT, preferred_element_type=F32) * score_scale
        )
        new = jnp.concatenate([fresh[0][rows], fresh[1][rows]], 0)
        mask = jnp.concatenate([mask_ref[rows, :]] * 2, 0)
        old = jnp.where(lane < length_ref[r], old, -jnp.inf)
        new = jnp.where(mask > 0.5, new, -jnp.inf)
        peak = jnp.maximum(
            jnp.max(old, -1, keepdims=True), jnp.max(new, -1, keepdims=True)
        )
        old = jnp.exp(old - peak)
        new = jnp.exp(new - peak)
        total = jnp.sum(old, -1, keepdims=True) + jnp.sum(new, -1, keepdims=True)
        old = (old / total).astype(BF16)
        new = (new / total).astype(BF16)
        mixed = jnp.dot(old, cache_ref[r, 0, 1], preferred_element_type=F32)
        mixed = mixed + lax.dot_general(new, values, NT, preferred_element_type=F32)
        mixed = mixed.astype(BF16)
        out_ref[rows, 0:128] = mixed[:16]
        out_ref[rows, 128:256] = mixed[16:]


def attend(head, lengths, own, recv, kv, cos_t, sin_t, cos_q, sin_q, mask, cache):
    def whole(array):
        return pl.BlockSpec(array.shape, lambda i, h, n: (0,) * array.ndim)

    arrays = (own, recv, kv, cos_t, sin_t, cos_q, sin_q, mask)
    return pl.pallas_call(
        attend_kernel,
        grid_spec=pltpu.PrefetchScalarGridSpec(
            num_scalar_prefetch=2,
            grid=(1,),
            in_specs=[whole(a) for a in arrays]
            + [pl.BlockSpec((8, 1, 2, 128, 128), lambda i, h, n: (0, h[0], 0, 0, 0))],
            out_specs=pl.BlockSpec((128, 256), lambda i, h, n: (0, 0)),
        ),
        out_shape=jax.ShapeDtypeStruct((128, 256), BF16),
        compiler_params=params(),
        cost_estimate=pl.CostEstimate(
            flops=2 * 256 * 128 * 512, bytes_accessed=2 << 20, transcendentals=65536
        ),
        name="attend",
    )(head, lengths, *arrays, cache)


def partial_kernel(place, mine, theirs, own_a, own_b, other_a, other_b, rotation_ref, out_a, out_b):
    unit = F32(1.0 / math.sqrt(RB))
    for own, other, out_ref in ((own_a, other_a, out_a), (own_b, other_b, out_b)):
        groups = (
            jnp.dot(mine[...], own[...], preferred_element_type=F32),
            jnp.dot(theirs[...], other[...], preferred_element_type=F32),
        )
        for b in range(4):
            halves = []
            for group in groups:
                block = group[:, b * 128 : b * 128 + 128]
                coarse = block.astype(BF16)
                fine = (block - coarse.astype(F32)).astype(BF16)
                halves.append(jnp.concatenate([coarse, fine], 1))
            both = lax.dot_general(
                rotation_ref[...],
                jnp.concatenate(halves, 0),
                NT,
                preferred_element_type=F32,
            )
            total = None
            for turned in (both[:, :128], both[:, 128:]):
                scale = jnp.max(jnp.abs(turned), 0, keepdims=True) * unit + TINY
                codes = (turned * (unit / scale)).astype(BF16)
                term = codes.astype(F32) * scale
                total = term if total is None else total + term
            out_ref[0, b * 128 : b * 128 + 128, :] = total.astype(out_ref.dtype)


def partials(hops, place, mine, theirs, own_weight, other_weight, rotation):
    def weight_at(hop):
        return pl.BlockSpec((256, 512), lambda i, p: (0, chip_at(p, hop, i) * 2 + p[0]))

    return pl.pallas_call(
        partial_kernel,
        grid_spec=pltpu.PrefetchScalarGridSpec(
            num_scalar_prefetch=1,
            grid=(4,),
            in_specs=[
                pl.BlockSpec((128, 256), lambda i, p: (0, 0)),
                pl.BlockSpec((128, 256), lambda i, p: (0, 0)),
                weight_at(hops[0]),
                weight_at(hops[1]),
                weight_at(hops[0]),
                weight_at(hops[1]),
                pl.BlockSpec((128, 256), lambda i, p: (0, 0)),
            ],
            out_specs=[pl.BlockSpec((1, 512, 128), lambda i, p: (i, 0, 0))] * 2,
        ),
        out_shape=[
            jax.ShapeDtypeStruct((4, 512, 128), BF16 if hop else F32) for hop in hops
        ],
        compiler_params=params(),
        cost_estimate=pl.CostEstimate(
            flops=2 * 128 * 4096 * 1024, bytes_accessed=6 << 20, transcendentals=0
        ),
        name="partials",
    )(place, mine, theirs, own_weight, own_weight, other_weight, other_weight, rotation)


def on_device(
    in_codes, in_scales, query_weight, kv_weight, out_weight, kv_cache, prefix_len, draft_parent
):
    rank = lax.axis_index(TENSOR)
    core = rank % 2
    head = rank // 8
    along_x = rank // 2 % 4
    place = jnp.stack(
        [core, jnp.where(core == 0, along_x, head), jnp.where(core == 0, head, along_x)]
    )
    signs = hadamard()
    scales = in_scales[0]

    near = jnp.stack([in_codes] + [first_shift(in_codes, k) for k in (1, 2, 3)])
    far = {k: second_shift(near, k) for k in (1, 3, 2)}

    wq = query_weight[0]
    wq_other = traded(query_weight)[0]
    wkv = kv_weight[0].transpose(2, 1, 3, 0).reshape(4, 2, 4, CHIPS, 2, 512)
    wkv_own = lax.dynamic_index_in_dim(wkv, core, 4, keepdims=False)
    wkv_other = traded(lax.dynamic_index_in_dim(wkv, 1 - core, 4, keepdims=False))
    low = jnp.where(core == 0, wkv_own, wkv_other)
    high = jnp.where(core == 0, wkv_other, wkv_own)
    wkv_both = jnp.stack([low, high], 2).reshape(64, 8192)
    wo = out_weight[0]
    wo_other = traded(out_weight)[0]

    ancestry = ancestor_table(draft_parent)
    position = prefix_len.astype(F32)[:, None] + (jnp.sum(ancestry, -1) - 1.0)
    frequency = jnp.power(ROPE_BASE, -(jnp.arange(64, dtype=F32) / 64))
    angles = position.reshape(128, 1) * frequency
    cosine, sine = jnp.cos(angles), jnp.sin(angles)
    cos_q = jnp.concatenate([cosine, cosine], 1)
    sin_q = jnp.concatenate([-sine, sine], 1)
    same = jnp.eye(8, dtype=F32)
    mask = (ancestry[:, :, None, :] * same[:, None, :, None]).reshape(128, 128)

    blocks = np.kron(np.eye(2, dtype=np.float32), signs)
    rotation = jnp.asarray(blocks, BF16)

    kv_part = jnp.zeros((4, 1, 16, 128), F32)
    own = other = jnp.zeros((128, 256), F32)
    rows, kv_part = decode(0, 1, place, scales, near, rotation, wkv_both, kv_part)
    own, other = project((0,), place, [rows], wq, wq_other, own, other)
    kv_part, own, other, mask, cos_q, sin_q, cos_t, sin_t = lax.optimization_barrier(
        (kv_part, own, other, mask, cos_q, sin_q, cosine.T, sine.T)
    )
    far_rows = []
    for k in (1, 3, 2):
        rows, kv_part = decode(
            k, 8 if k == 2 else 1, place, scales, far[k], rotation, wkv_both, kv_part
        )
        far_rows.append(rows)
    kv = exchanged(kv_part.reshape(32, 16, 128))
    own, other = project((1, 3, 2), place, far_rows, wq, wq_other, own, other)
    recv = traded(other)
    attended = attend(
        head.reshape(1), prefix_len, own, recv, kv, cos_t, sin_t, cos_q, sin_q, mask, kv_cache
    )
    theirs = traded(attended)
    twice = jnp.asarray(np.concatenate([signs, signs], 1), BF16)
    sent = {}
    for hops in ((2, 1), (3, 0)):
        for hop, piece in zip(hops, partials(hops, place, attended, theirs, wo, wo_other, twice)):
            sent[hop] = piece
    sums = sent[0]
    for k in (2, 1, 3):
        sums = sums + first_shift(sent[k], k).astype(F32)
    summed = sums[0]
    for k in (2, 1, 3):
        summed = summed + second_shift(sums[k].astype(BF16), k).astype(F32)

    here = lax.dynamic_slice_in_dim(scales, rank * 4, 4)
    turned_in = in_codes.T.astype(F32) * jnp.repeat(here, RB)[:, None]
    turned = summed + turned_in
    peak = jnp.max(jnp.abs(turned.reshape(4, RB, 128)), (1, 2))
    everyone = lax.all_to_all(
        jnp.broadcast_to(peak[None], (64, 4)), ("dp", TENSOR), 0, 0, tiled=True
    )
    next_rows = swapped(turned, "section")
    out_scale = jnp.max(everyone.reshape(2, 128), 0) + TINY
    next_scales = swapped(out_scale, "section")
    scale_here = lax.dynamic_slice_in_dim(next_scales, rank * 4, 4)
    next_codes = (next_rows.T / jnp.repeat(scale_here, RB)[None, :]).astype(BF16)
    return (next_codes, next_scales[None])


def solution(mesh):
    rows = ("section", "dp")
    placed = (
        P(rows, TENSOR),
        P("section", None),
        P("section", None, TENSOR),
        P("section", None, None, None, TENSOR),
        P("section", TENSOR, None),
        P(rows, None, None, None, None),
        P(rows),
        P(rows, None),
    )
    return jax.shard_map(
        on_device,
        mesh=mesh,
        in_specs=placed,
        out_specs=(P(rows, TENSOR), P("section", None)),
        check_vma=False,
    )
```

```python
import functools
import math

import jax
import jax.numpy as jnp
import numpy as np
from jax import lax
from jax.experimental import pallas as pl
from jax.experimental.pallas import tpu as pltpu
from jax.sharding import PartitionSpec as P

HD = 128
RB = 128
CHIPS = 16
ROPE_BASE = 500000.0
TINY = 1e-06
TENSOR = "tensor"


def device(y, x, core):
    return (y * 4 + x) * 2 + core


VMEM_LIMIT = 48 * 1024 * 1024
F32 = jnp.float32
BF16 = jnp.bfloat16
NT = (((1,), (1,)), ((), ()))


def hadamard():
    index = np.arange(RB)
    common = index[:, None] & index[None, :]
    parity = np.zeros((RB, RB), np.int32)
    for place in range(7):
        parity = parity + (common >> place & 1)
    return np.where(parity % 2 == 0, 1.0, -1.0).astype(np.float32)


def ancestor_table(draft_parent):
    count, size = draft_parent.shape
    target = lax.broadcasted_iota(jnp.int32, (count, size, size), 2)
    source = lax.broadcasted_iota(jnp.int32, (count, size, size), 1)
    table = ((target == draft_parent[:, :, None]) | (target == source)).astype(F32)
    for _ in range(4):
        table = jnp.minimum(jnp.einsum("rij,rjk->rik", table, table), 1.0)
    return table


def swapped(block, axis):
    return lax.ppermute(block, axis, [(0, 1), (1, 0)])


def traded(block):
    return lax.ppermute(block, TENSOR, [(i, i ^ 1) for i in range(32)])


def exchanged(pieces):
    groups = [[chip * 2 + core for chip in range(CHIPS)] for core in range(2)]
    return lax.all_to_all(pieces, TENSOR, 0, 0, tiled=True, axis_index_groups=groups)


def shifted(block, by, second):
    pairs = []
    for y in range(4):
        for x in range(4):
            for core in range(2):
                along_y = (core == 1) != second
                to_y, to_x = ((y + by) % 4, x) if along_y else (y, (x + by) % 4)
                pairs.append((device(y, x, core), device(to_y, to_x, core)))
    return lax.ppermute(block, TENSOR, pairs)


def first_shift(block, by):
    return shifted(block, by, False)


def second_shift(block, by):
    return shifted(block, by, True)


def chip_at(place, first, second):
    first = lax.rem(place[1] + 4 + first, 4)
    second = lax.rem(place[2] + 4 + second, 4)
    return jnp.where(place[0] == 0, second * 4 + first, first * 4 + second)


def params(**more):
    return pltpu.CompilerParams(vmem_limit_bytes=VMEM_LIMIT, **more)


def decode_kernel(hop, waits, place, scale_ref, codes_ref, rotation_ref, *refs):
    own_refs, other_refs, kv_in, (rows_ref, kv_out) = refs[:4], refs[4:8], refs[8], refs[9 + waits :]
    for k in range(4):
        first = (chip_at(place, -k, -hop) * 2 + place[0]) * 4
        for half in range(2):
            product = jnp.dot(
                codes_ref[k, :, half * 256 : half * 256 + 256],
                rotation_ref[...],
                preferred_element_type=F32,
            )
            for b in range(2):
                factor = scale_ref[first + half * 2 + b] * F32(1.0 / math.sqrt(RB))
                at = k * 512 + half * 256 + b * 128
                rows_ref[:, at : at + 128] = (product[:, b * 128 : b * 128 + 128] * factor).astype(
                    BF16
                )
    weight = jnp.concatenate(
        [
            jnp.concatenate([ref[...] for ref in own_refs], 1),
            jnp.concatenate([ref[...] for ref in other_refs], 1),
        ],
        0,
    )
    total = lax.dot_general(weight, rows_ref[...], NT, preferred_element_type=F32)
    for h in range(4):
        own = total[h * 8 : h * 8 + 8]
        other = total[32 + h * 8 : 40 + h * 8]
        value = kv_in[h, 0] + jnp.concatenate(
            [jnp.where(place[0] == 0, own, other), jnp.where(place[0] == 0, other, own)], 0
        )
        for i in range(kv_out.shape[1]):
            kv_out[h, i] = value


def decode(hop, copies, place, scales, codes, rotation, own_weight, other_weight, kv_in, after=()):
    def kv_at(k):
        return pl.BlockSpec((32, 512), lambda i, p, s: (0, chip_at(p, -k, -hop) * 2 + p[0]))

    return pl.pallas_call(
        functools.partial(decode_kernel, hop, len(after)),
        grid_spec=pltpu.PrefetchScalarGridSpec(
            num_scalar_prefetch=2,
            grid=(1,),
            in_specs=[
                pl.BlockSpec((4, 128, 512), lambda i, p, s: (0, 0, 0)),
                pl.BlockSpec((256, 256), lambda i, p, s: (0, 0)),
                *(kv_at(k) for k in range(4)),
                *(kv_at(k) for k in range(4)),
                pl.BlockSpec((4, 1, 16, 128), lambda i, p, s: (0, 0, 0, 0)),
                *(pl.BlockSpec(memory_space=pl.ANY) for _ in after),
            ],
            out_specs=[
                pl.BlockSpec((128, 2048), lambda i, p, s: (0, 0)),
                pl.BlockSpec((4, copies, 16, 128), lambda i, p, s: (0, 0, 0, 0)),
            ],
        ),
        out_shape=[
            jax.ShapeDtypeStruct((128, 2048), BF16),
            jax.ShapeDtypeStruct((4, copies, 16, 128), F32),
        ],
        compiler_params=params(),
        cost_estimate=pl.CostEstimate(
            flops=2 * 128 * 2048 * 320, bytes_accessed=1 << 20, transcendentals=0
        ),
        name="decode",
    )(place, scales, codes, rotation, *[own_weight] * 4, *[other_weight] * 4, kv_in, *after)


def query_kernel(count, place, *refs):
    rows_refs, refs = refs[:count], refs[count:]
    own_in, other_in, own_out, other_out = refs[8 * count :]
    for weights, start, out in (
        (refs[: 4 * count], own_in, own_out),
        (refs[4 * count : 8 * count], other_in, other_out),
    ):
        total = start[...]
        for i in range(4 * count):
            total += jnp.dot(
                rows_refs[i // 4][:, i % 4 * 512 : i % 4 * 512 + 512],
                weights[i][...],
                preferred_element_type=F32,
            )
        out[...] = total


def project(hops, place, rows, own_weight, other_weight, own_in, other_in):
    count = len(hops)

    def weight_at(hop, k):
        return pl.BlockSpec((512, 256), lambda i, p: (chip_at(p, -k, -hop) * 2 + p[0], 0))

    weights = [weight_at(hop, k) for hop in hops for k in range(4)]
    still = pl.BlockSpec((128, 256), lambda i, p: (0, 0))
    return pl.pallas_call(
        functools.partial(query_kernel, count),
        grid_spec=pltpu.PrefetchScalarGridSpec(
            num_scalar_prefetch=1,
            grid=(1,),
            in_specs=[pl.BlockSpec((128, 2048), lambda i, p: (0, 0))] * count
            + weights * 2
            + [still, still],
            out_specs=[still, still],
        ),
        out_shape=[jax.ShapeDtypeStruct((128, 256), F32)] * 2,
        compiler_params=params(),
        cost_estimate=pl.CostEstimate(
            flops=2 * 128 * 2048 * 512 * count, bytes_accessed=count * 5 << 19, transcendentals=0
        ),
        name="query",
    )(
        place,
        *rows,
        *[own_weight] * (4 * count),
        *[other_weight] * (4 * count),
        own_in,
        other_in,
    )


def attend_kernel(
    head_ref, length_ref, own_ref, recv_ref, kv_ref, kv_recv, cos_t, sin_t, cos_q, sin_q, mask_ref, cache_ref, out_ref
):
    score_scale = F32(1.0 / math.sqrt(HD))
    keys, values = [], []
    upper = lax.broadcasted_iota(jnp.int32, (8, 128), 0) < 4
    for chip in range(CHIPS):
        first = kv_ref[chip, 0:8] + kv_recv[chip, 0:8]
        second = kv_ref[chip, 8:16] + kv_recv[chip, 8:16]
        keys.append(jnp.where(upper, first, pltpu.roll(second, 4, 0)))
        values.append(jnp.where(upper, pltpu.roll(first, 4, 0), second))
    keys = jnp.concatenate(keys, 0).astype(BF16).astype(F32)
    values = jnp.concatenate(values, 0).astype(BF16)
    low, high = keys[:64], keys[64:]
    keys = jnp.concatenate(
        [low * cos_t[...] - high * sin_t[...], high * cos_t[...] + low * sin_t[...]], 0
    ).astype(BF16)
    heads = []
    for h in range(2):
        q = own_ref[:, h * 128 : h * 128 + 128] + recv_ref[:, h * 128 : h * 128 + 128]
        q = q * cos_q[...] + pltpu.roll(q, 64, 1) * sin_q[...]
        heads.append(q.astype(BF16))
    fresh = [
        jnp.dot(q, keys, preferred_element_type=F32) * score_scale for q in heads
    ]
    lane = lax.broadcasted_iota(jnp.int32, (32, 128), 1)
    for r in range(8):
        rows = slice(r * 16, r * 16 + 16)
        q = jnp.concatenate([heads[0][rows], heads[1][rows]], 0)
        old = (
            lax.dot_general(q, cache_ref[r, 0, 0], NT, preferred_element_type=F32) * score_scale
        )
        new = jnp.concatenate([fresh[0][rows], fresh[1][rows]], 0)
        mask = jnp.concatenate([mask_ref[rows, :]] * 2, 0)
        old = jnp.where(lane < length_ref[r], old, -jnp.inf)
        new = jnp.where(mask > 0.5, new, -jnp.inf)
        peak = jnp.maximum(
            jnp.max(old, -1, keepdims=True), jnp.max(new, -1, keepdims=True)
        )
        old = jnp.exp(old - peak)
        new = jnp.exp(new - peak)
        total = jnp.sum(old, -1, keepdims=True) + jnp.sum(new, -1, keepdims=True)
        old = (old / total).astype(BF16)
        new = (new / total).astype(BF16)
        mixed = jnp.dot(old, cache_ref[r, 0, 1], preferred_element_type=F32)
        mixed = mixed + lax.dot_general(new, values, NT, preferred_element_type=F32)
        mixed = mixed.astype(BF16)
        out_ref[rows, 0:128] = mixed[:16]
        out_ref[rows, 128:256] = mixed[16:]


def attend(head, lengths, own, recv, kv, kv_recv, cos_t, sin_t, cos_q, sin_q, mask, cache):
    def whole(array):
        return pl.BlockSpec(array.shape, lambda i, h, n: (0,) * array.ndim)

    arrays = (own, recv, kv, kv_recv, cos_t, sin_t, cos_q, sin_q, mask)
    return pl.pallas_call(
        attend_kernel,
        grid_spec=pltpu.PrefetchScalarGridSpec(
            num_scalar_prefetch=2,
            grid=(1,),
            in_specs=[whole(a) for a in arrays]
            + [pl.BlockSpec((8, 1, 2, 128, 128), lambda i, h, n: (0, h[0], 0, 0, 0))],
            out_specs=pl.BlockSpec((128, 256), lambda i, h, n: (0, 0)),
        ),
        out_shape=jax.ShapeDtypeStruct((128, 256), BF16),
        compiler_params=params(),
        cost_estimate=pl.CostEstimate(
            flops=2 * 256 * 128 * 512, bytes_accessed=2 << 20, transcendentals=65536
        ),
        name="attend",
    )(head, lengths, *arrays, cache)


def partial_kernel(slots, place, mine, theirs, own_a, own_b, other_a, other_b, rotation_ref, *outs):
    unit = F32(1.0 / math.sqrt(RB))
    for own, other, (out, at) in ((own_a, other_a, slots[0]), (own_b, other_b, slots[1])):
        out_ref = outs[out]
        groups = (
            jnp.dot(mine[...], own[...], preferred_element_type=F32),
            jnp.dot(theirs[...], other[...], preferred_element_type=F32),
        )
        for b in range(4):
            halves = []
            for group in groups:
                block = group[:, b * 128 : b * 128 + 128]
                coarse = block.astype(BF16)
                fine = (block - coarse.astype(F32)).astype(BF16)
                halves.append(jnp.concatenate([coarse, fine], 1))
            both = lax.dot_general(
                rotation_ref[...],
                jnp.concatenate(halves, 0),
                NT,
                preferred_element_type=F32,
            )
            total = None
            for turned in (both[:, :128], both[:, 128:]):
                scale = jnp.max(jnp.abs(turned), 0, keepdims=True) * unit + TINY
                codes = (turned * (unit / scale)).astype(BF16)
                term = codes.astype(F32) * scale
                total = term if total is None else total + term
            out_ref[at, b * 128 : b * 128 + 128, :] = total.astype(out_ref.dtype)


def partials(hops, place, mine, theirs, own_weight, other_weight, rotation):
    each = 2 // len(hops)
    slots = [(0, 0), (0, 1)] if each == 2 else [(0, 0), (1, 0)]

    def weight_at(slot):
        out, at = slots[slot]
        return pl.BlockSpec(
            (256, 512), lambda i, p: (0, chip_at(p, hops[out], i * each + at) * 2 + p[0])
        )

    return pl.pallas_call(
        functools.partial(partial_kernel, slots),
        grid_spec=pltpu.PrefetchScalarGridSpec(
            num_scalar_prefetch=1,
            grid=(4 // each,),
            in_specs=[
                pl.BlockSpec((128, 256), lambda i, p: (0, 0)),
                pl.BlockSpec((128, 256), lambda i, p: (0, 0)),
                weight_at(0),
                weight_at(1),
                weight_at(0),
                weight_at(1),
                pl.BlockSpec((128, 256), lambda i, p: (0, 0)),
            ],
            out_specs=[pl.BlockSpec((each, 512, 128), lambda i, p: (i, 0, 0)) for _ in hops],
        ),
        out_shape=[
            jax.ShapeDtypeStruct((4, 512, 128), BF16 if hop else F32) for hop in hops
        ],
        compiler_params=params(),
        cost_estimate=pl.CostEstimate(
            flops=2 * 128 * 2048 * 1024 * len(hops),
            bytes_accessed=len(hops) * 3 << 20,
            transcendentals=0,
        ),
        name="partials",
    )(place, mine, theirs, own_weight, own_weight, other_weight, other_weight, rotation)


def on_device(
    in_codes, in_scales, query_weight, kv_weight, out_weight, kv_cache, prefix_len, draft_parent
):
    rank = lax.axis_index(TENSOR)
    core = rank % 2
    head = rank // 8
    along_x = rank // 2 % 4
    place = jnp.stack(
        [core, jnp.where(core == 0, along_x, head), jnp.where(core == 0, head, along_x)]
    )
    signs = hadamard()
    scales = in_scales[0]

    near = jnp.stack([in_codes] + [first_shift(in_codes, k) for k in (1, 2, 3)])
    far = {k: second_shift(near, k) for k in (1, 3, 2)}

    wq = query_weight[0]
    wq_other = traded(query_weight)[0]
    wkv = kv_weight[0].transpose(2, 1, 3, 0).reshape(32, -1)
    wkv_other = traded(wkv)
    wo = out_weight[0]
    wo_other = traded(out_weight)[0]

    done = (near[1, 0, 0] + near[2, 0, 0] + near[3, 0, 0]).astype(F32) * 0.0
    ancestry = ancestor_table(draft_parent + done.astype(jnp.int32))
    position = prefix_len.astype(F32)[:, None] + (jnp.sum(ancestry, -1) - 1.0)
    frequency = jnp.power(ROPE_BASE, -(jnp.arange(64, dtype=F32) / 64))
    angles = position.reshape(128, 1) * frequency
    cosine, sine = jnp.cos(angles), jnp.sin(angles)
    cos_q = jnp.concatenate([cosine, cosine], 1)
    sin_q = jnp.concatenate([-sine, sine], 1)
    block = jnp.eye(8, dtype=F32)
    mask = (ancestry[:, :, None, :] * block[:, None, :, None]).reshape(128, 128)

    blocks = np.kron(np.eye(2, dtype=np.float32), signs)
    rotation = jnp.asarray(blocks, BF16)

    cos_t, sin_t = cosine.T, sine.T
    kv_part = jnp.zeros((4, 1, 16, 128), F32)
    own = other = jnp.zeros((128, 256), F32)
    rows, kv_part = decode(0, 1, place, scales, near, rotation, wkv, wkv_other, kv_part)
    own, other = project((0,), place, [rows], wq, wq_other, own, other)
    far_rows = []
    for k in (1, 3, 2):
        after = {1: (own,), 3: (), 2: (mask, cos_q, sin_q, cos_t, sin_t)}[k]
        rows, kv_part = decode(
            k, 4 if k == 2 else 1, place, scales, far[k], rotation, wkv, wkv_other, kv_part, after
        )
        far_rows.append(rows)
    kv = exchanged(kv_part.reshape(CHIPS, 16, 128))
    own, other = project((1, 3, 2), place, far_rows, wq, wq_other, own, other)
    recv = traded(other)
    kv_recv = traded(kv)
    attended = attend(
        head.reshape(1), prefix_len, own, recv, kv, kv_recv, cos_t, sin_t, cos_q, sin_q, mask, kv_cache
    )
    theirs = traded(attended)
    twice = jnp.asarray(np.concatenate([signs, signs], 1), BF16)
    sent = {}
    for hops in ((2,), (1, 3), (0,)):
        for hop, piece in zip(hops, partials(hops, place, attended, theirs, wo, wo_other, twice)):
            sent[hop] = piece
    sums = sent[0]
    for k in (2, 1, 3):
        sums = sums + first_shift(sent[k], k).astype(F32)
    summed = sums[0]
    for k in (2, 1, 3):
        summed = summed + second_shift(sums[k].astype(BF16), k).astype(F32)

    here = lax.dynamic_slice_in_dim(scales, rank * 4, 4)
    turned_in = in_codes.T.astype(F32) * jnp.repeat(here, RB)[:, None]
    turned = summed + turned_in
    peak = jnp.max(jnp.abs(turned.reshape(4, RB, 128)), (1, 2))
    peak = jnp.maximum(peak, swapped(peak, "dp"))
    out_scale = exchanged(jnp.broadcast_to(peak[None], (CHIPS, 4))) + TINY
    next_rows = swapped(turned, "section")
    same = swapped(out_scale, "section")
    cross = lax.ppermute(
        out_scale,
        ("section", TENSOR),
        [(s * 32 + t, (1 - s) * 32 + (t ^ 1)) for s in range(2) for t in range(32)],
    )
    by_core = jnp.where(core == 0, jnp.stack([same, cross], 1), jnp.stack([cross, same], 1))
    next_scales = by_core.reshape(1, 128)
    scale_here = lax.dynamic_index_in_dim(same, rank // 2, 0, keepdims=False)
    next_codes = (next_rows.T / jnp.repeat(scale_here, RB)[None, :]).astype(BF16)
    return (next_codes, next_scales)


def solution(mesh):
    rows = ("section", "dp")
    placed = (
        P(rows, TENSOR),
        P("section", None),
        P("section", None, TENSOR),
        P("section", None, None, None, TENSOR),
        P("section", TENSOR, None),
        P(rows, None, None, None, None),
        P(rows),
        P(rows, None),
    )
    return jax.shard_map(
        on_device,
        mesh=mesh,
        in_specs=placed,
        out_specs=(P(rows, TENSOR), P("section", None)),
        check_vma=False,
    )
```

```python
import functools
import math

import jax
import jax.numpy as jnp
import numpy as np
from jax import lax
from jax.experimental import pallas as pl
from jax.experimental.pallas import tpu as pltpu
from jax.sharding import PartitionSpec as P

HD = 128
RB = 128
CHIPS = 16
ROPE_BASE = 500000.0
TINY = 1e-06
TENSOR = "tensor"


def device(y, x, core):
    return (y * 4 + x) * 2 + core


F32 = jnp.float32
BF16 = jnp.bfloat16
NT = (((1,), (1,)), ((), ()))
LIGHT = pl.CostEstimate(flops=1024, bytes_accessed=1024, transcendentals=0)


def hadamard():
    index = np.arange(RB)
    common = index[:, None] & index[None, :]
    parity = np.zeros((RB, RB), np.int32)
    for place in range(7):
        parity = parity + (common >> place & 1)
    return np.where(parity % 2 == 0, 1.0, -1.0).astype(np.float32)


def ancestor_table(draft_parent):
    count, size = draft_parent.shape
    target = lax.broadcasted_iota(jnp.int32, (count, size, size), 2)
    source = lax.broadcasted_iota(jnp.int32, (count, size, size), 1)
    table = ((target == draft_parent[:, :, None]) | (target == source)).astype(F32)
    for _ in range(4):
        table = jnp.minimum(jnp.einsum("rij,rjk->rik", table, table), 1.0)
    return table


def swapped(block, axis):
    return lax.ppermute(block, axis, [(0, 1), (1, 0)])


def traded(block):
    return lax.ppermute(block, TENSOR, [(i, i ^ 1) for i in range(32)])


def exchanged(pieces):
    groups = [[chip * 2 + core for chip in range(CHIPS)] for core in range(2)]
    return lax.all_to_all(pieces, TENSOR, 0, 0, tiled=True, axis_index_groups=groups)


def shifted(block, by, second):
    pairs = []
    for y in range(4):
        for x in range(4):
            for core in range(2):
                along_y = (core == 1) != second
                to_y, to_x = ((y + by) % 4, x) if along_y else (y, (x + by) % 4)
                pairs.append((device(y, x, core), device(to_y, to_x, core)))
    return lax.ppermute(block, TENSOR, pairs)


def first_shift(block, by):
    return shifted(block, by, False)


def second_shift(block, by):
    return shifted(block, by, True)


def chip_at(place, first, second):
    first = lax.rem(place[1] + 4 + first, 4)
    second = lax.rem(place[2] + 4 + second, 4)
    return jnp.where(place[0] == 0, second * 4 + first, first * 4 + second)


def params(mebibytes):
    return pltpu.CompilerParams(vmem_limit_bytes=mebibytes << 20)


def decode_kernel(hop, waits, place, scale_ref, codes_ref, rotation_ref, *refs):
    own_refs, other_refs, kv_in, (rows_ref, kv_out) = refs[:4], refs[4:8], refs[8], refs[9 + waits :]
    for k in range(4):
        first = (chip_at(place, -k, -hop) * 2 + place[0]) * 4
        for half in range(2):
            product = jnp.dot(
                codes_ref[k, :, half * 256 : half * 256 + 256],
                rotation_ref[...],
                preferred_element_type=F32,
            )
            for b in range(2):
                factor = scale_ref[first + half * 2 + b] * F32(1.0 / math.sqrt(RB))
                at = k * 512 + half * 256 + b * 128
                rows_ref[:, at : at + 128] = (product[:, b * 128 : b * 128 + 128] * factor).astype(
                    BF16
                )
    weight = jnp.concatenate(
        [
            jnp.concatenate([ref[...] for ref in own_refs], 1),
            jnp.concatenate([ref[...] for ref in other_refs], 1),
        ],
        0,
    )
    total = lax.dot_general(weight, rows_ref[...], NT, preferred_element_type=F32)
    for h in range(4):
        own = total[h * 8 : h * 8 + 8]
        other = total[32 + h * 8 : 40 + h * 8]
        value = kv_in[h, 0] + jnp.concatenate(
            [jnp.where(place[0] == 0, own, other), jnp.where(place[0] == 0, other, own)], 0
        )
        for i in range(kv_out.shape[1]):
            kv_out[h, i] = value


def decode(hop, copies, place, scales, codes, rotation, own_weight, other_weight, kv_in, after=()):
    def kv_at(k):
        return pl.BlockSpec((32, 512), lambda i, p, s: (0, chip_at(p, -k, -hop) * 2 + p[0]))

    return pl.pallas_call(
        functools.partial(decode_kernel, hop, len(after)),
        grid_spec=pltpu.PrefetchScalarGridSpec(
            num_scalar_prefetch=2,
            grid=(1,),
            in_specs=[
                pl.BlockSpec((4, 128, 512), lambda i, p, s: (0, 0, 0)),
                pl.BlockSpec((256, 256), lambda i, p, s: (0, 0)),
                *(kv_at(k) for k in range(4)),
                *(kv_at(k) for k in range(4)),
                pl.BlockSpec((4, 1, 16, 128), lambda i, p, s: (0, 0, 0, 0)),
                *(pl.BlockSpec(memory_space=pl.ANY) for _ in after),
            ],
            out_specs=[
                pl.BlockSpec((128, 2048), lambda i, p, s: (0, 0)),
                pl.BlockSpec((4, copies, 16, 128), lambda i, p, s: (0, 0, 0, 0)),
            ],
        ),
        out_shape=[
            jax.ShapeDtypeStruct((128, 2048), BF16),
            jax.ShapeDtypeStruct((4, copies, 16, 128), F32),
        ],
        compiler_params=params(6),
        cost_estimate=LIGHT,
        name="decode",
    )(place, scales, codes, rotation, *[own_weight] * 4, *[other_weight] * 4, kv_in, *after)


def query_kernel(count, place, *refs):
    rows_refs, refs = refs[:count], refs[count:]
    own_in, other_in, own_out, other_out = refs[8 * count :]
    for weights, start, out in (
        (refs[: 4 * count], own_in, own_out),
        (refs[4 * count : 8 * count], other_in, other_out),
    ):
        total = start[...]
        for i in range(4 * count):
            total += jnp.dot(
                rows_refs[i // 4][:, i % 4 * 512 : i % 4 * 512 + 512],
                weights[i][...],
                preferred_element_type=F32,
            )
        out[...] = total


def project(hops, place, rows, own_weight, other_weight, own_in, other_in):
    count = len(hops)

    def weight_at(hop, k):
        return pl.BlockSpec((512, 256), lambda i, p: (chip_at(p, -k, -hop) * 2 + p[0], 0))

    weights = [weight_at(hop, k) for hop in hops for k in range(4)]
    still = pl.BlockSpec((128, 256), lambda i, p: (0, 0))
    return pl.pallas_call(
        functools.partial(query_kernel, count),
        grid_spec=pltpu.PrefetchScalarGridSpec(
            num_scalar_prefetch=1,
            grid=(1,),
            in_specs=[pl.BlockSpec((128, 2048), lambda i, p: (0, 0))] * count
            + weights * 2
            + [still, still],
            out_specs=[still, still],
        ),
        out_shape=[jax.ShapeDtypeStruct((128, 256), F32)] * 2,
        compiler_params=params(6 + 4 * count),
        cost_estimate=LIGHT,
        name="query",
    )(
        place,
        *rows,
        *[own_weight] * (4 * count),
        *[other_weight] * (4 * count),
        own_in,
        other_in,
    )


def attend_kernel(
    head_ref, length_ref, own_ref, recv_ref, kv_ref, kv_recv, cos_t, sin_t, cos_q, sin_q, mask_ref, cache_ref, out_ref
):
    score_scale = F32(1.0 / math.sqrt(HD))
    keys, values = [], []
    upper = lax.broadcasted_iota(jnp.int32, (8, 128), 0) < 4
    for chip in range(CHIPS):
        first = kv_ref[chip, 0:8] + kv_recv[chip, 0:8]
        second = kv_ref[chip, 8:16] + kv_recv[chip, 8:16]
        keys.append(jnp.where(upper, first, pltpu.roll(second, 4, 0)))
        values.append(jnp.where(upper, pltpu.roll(first, 4, 0), second))
    keys = jnp.concatenate(keys, 0).astype(BF16).astype(F32)
    values = jnp.concatenate(values, 0).astype(BF16)
    low, high = keys[:64], keys[64:]
    keys = jnp.concatenate(
        [low * cos_t[...] - high * sin_t[...], high * cos_t[...] + low * sin_t[...]], 0
    ).astype(BF16)
    heads = []
    for h in range(2):
        q = own_ref[:, h * 128 : h * 128 + 128] + recv_ref[:, h * 128 : h * 128 + 128]
        q = q * cos_q[...] + pltpu.roll(q, 64, 1) * sin_q[...]
        heads.append(q.astype(BF16))
    fresh = [
        jnp.dot(q, keys, preferred_element_type=F32) * score_scale for q in heads
    ]
    lane = lax.broadcasted_iota(jnp.int32, (32, 128), 1)
    for r in range(8):
        rows = slice(r * 16, r * 16 + 16)
        q = jnp.concatenate([heads[0][rows], heads[1][rows]], 0)
        old = (
            lax.dot_general(q, cache_ref[r, 0, 0], NT, preferred_element_type=F32) * score_scale
        )
        new = jnp.concatenate([fresh[0][rows], fresh[1][rows]], 0)
        mask = jnp.concatenate([mask_ref[rows, :]] * 2, 0)
        old = jnp.where(lane < length_ref[r], old, -jnp.inf)
        new = jnp.where(mask > 0.5, new, -jnp.inf)
        peak = jnp.maximum(
            jnp.max(old, -1, keepdims=True), jnp.max(new, -1, keepdims=True)
        )
        old = jnp.exp(old - peak)
        new = jnp.exp(new - peak)
        total = jnp.sum(old, -1, keepdims=True) + jnp.sum(new, -1, keepdims=True)
        old = (old / total).astype(BF16)
        new = (new / total).astype(BF16)
        mixed = jnp.dot(old, cache_ref[r, 0, 1], preferred_element_type=F32)
        mixed = mixed + lax.dot_general(new, values, NT, preferred_element_type=F32)
        mixed = mixed.astype(BF16)
        out_ref[rows, 0:128] = mixed[:16]
        out_ref[rows, 128:256] = mixed[16:]


def attend(head, lengths, own, recv, kv, kv_recv, cos_t, sin_t, cos_q, sin_q, mask, cache):
    def whole(array):
        return pl.BlockSpec(array.shape, lambda i, h, n: (0,) * array.ndim)

    arrays = (own, recv, kv, kv_recv, cos_t, sin_t, cos_q, sin_q, mask)
    return pl.pallas_call(
        attend_kernel,
        grid_spec=pltpu.PrefetchScalarGridSpec(
            num_scalar_prefetch=2,
            grid=(1,),
            in_specs=[whole(a) for a in arrays]
            + [pl.BlockSpec((8, 1, 2, 128, 128), lambda i, h, n: (0, h[0], 0, 0, 0))],
            out_specs=pl.BlockSpec((128, 256), lambda i, h, n: (0, 0)),
        ),
        out_shape=jax.ShapeDtypeStruct((128, 256), BF16),
        compiler_params=params(6),
        cost_estimate=pl.CostEstimate(
            flops=2 * 256 * 128 * 512, bytes_accessed=2 << 20, transcendentals=65536
        ),
        name="attend",
    )(head, lengths, *arrays, cache)


def partial_kernel(slots, place, mine, theirs, own_a, own_b, other_a, other_b, rotation_ref, *outs):
    unit = F32(1.0 / math.sqrt(RB))
    for own, other, (out, at) in ((own_a, other_a, slots[0]), (own_b, other_b, slots[1])):
        out_ref = outs[out]
        groups = (
            jnp.dot(mine[...], own[...], preferred_element_type=F32),
            jnp.dot(theirs[...], other[...], preferred_element_type=F32),
        )
        for b in range(4):
            halves = []
            for group in groups:
                block = group[:, b * 128 : b * 128 + 128]
                coarse = block.astype(BF16)
                fine = (block - coarse.astype(F32)).astype(BF16)
                halves.append(jnp.concatenate([coarse, fine], 1))
            both = lax.dot_general(
                rotation_ref[...],
                jnp.concatenate(halves, 0),
                NT,
                preferred_element_type=F32,
            )
            total = None
            for turned in (both[:, :128], both[:, 128:]):
                scale = jnp.max(jnp.abs(turned), 0, keepdims=True) * unit + TINY
                codes = (turned * (unit / scale)).astype(BF16)
                term = codes.astype(F32) * scale
                total = term if total is None else total + term
            out_ref[at, b * 128 : b * 128 + 128, :] = total.astype(out_ref.dtype)


def partials(hops, place, mine, theirs, own_weight, other_weight, rotation):
    each = 2 // len(hops)
    slots = [(0, 0), (0, 1)] if each == 2 else [(0, 0), (1, 0)]

    def weight_at(slot):
        out, at = slots[slot]
        return pl.BlockSpec(
            (256, 512), lambda i, p: (0, chip_at(p, hops[out], i * each + at) * 2 + p[0])
        )

    return pl.pallas_call(
        functools.partial(partial_kernel, slots),
        grid_spec=pltpu.PrefetchScalarGridSpec(
            num_scalar_prefetch=1,
            grid=(4 // each,),
            in_specs=[
                pl.BlockSpec((128, 256), lambda i, p: (0, 0)),
                pl.BlockSpec((128, 256), lambda i, p: (0, 0)),
                weight_at(0),
                weight_at(1),
                weight_at(0),
                weight_at(1),
                pl.BlockSpec((128, 256), lambda i, p: (0, 0)),
            ],
            out_specs=[pl.BlockSpec((each, 512, 128), lambda i, p: (i, 0, 0)) for _ in hops],
        ),
        out_shape=[
            jax.ShapeDtypeStruct((4, 512, 128), BF16 if hop else F32) for hop in hops
        ],
        compiler_params=params(8),
        cost_estimate=pl.CostEstimate(
            flops=2 * 128 * 2048 * 1024 * len(hops),
            bytes_accessed=len(hops) * 3 << 20,
            transcendentals=0,
        ),
        name="partials",
    )(place, mine, theirs, own_weight, own_weight, other_weight, other_weight, rotation)


def on_device(
    in_codes, in_scales, query_weight, kv_weight, out_weight, kv_cache, prefix_len, draft_parent
):
    rank = lax.axis_index(TENSOR)
    core = rank % 2
    head = rank // 8
    along_x = rank // 2 % 4
    place = jnp.stack(
        [core, jnp.where(core == 0, along_x, head), jnp.where(core == 0, head, along_x)]
    )
    signs = hadamard()
    scales = in_scales[0]

    near = jnp.stack([in_codes] + [first_shift(in_codes, k) for k in (1, 2, 3)])
    wq = query_weight[0]
    wq_other = traded(query_weight)[0]
    kv_other = traded(kv_weight)

    near, draft_parent, kv_weight, kv_other, out_weight = lax.optimization_barrier(
        (near, draft_parent, kv_weight, kv_other, out_weight)
    )

    far = {k: second_shift(near, k) for k in (1, 3, 2)}

    def as_rows(weight):
        return weight[0].transpose(2, 1, 3, 0).reshape(32, -1)

    wkv, wkv_other = as_rows(kv_weight), as_rows(kv_other)
    wo = out_weight[0]
    wo_other = traded(out_weight)[0]

    ancestry = ancestor_table(draft_parent)
    position = prefix_len.astype(F32)[:, None] + (jnp.sum(ancestry, -1) - 1.0)
    frequency = jnp.power(ROPE_BASE, -(jnp.arange(64, dtype=F32) / 64))
    angles = position.reshape(128, 1) * frequency
    cosine, sine = jnp.cos(angles), jnp.sin(angles)
    cos_q = jnp.concatenate([cosine, cosine], 1)
    sin_q = jnp.concatenate([-sine, sine], 1)
    block = jnp.eye(8, dtype=F32)
    mask = (ancestry[:, :, None, :] * block[:, None, :, None]).reshape(128, 128)

    blocks = np.kron(np.eye(2, dtype=np.float32), signs)
    rotation = jnp.asarray(blocks, BF16)

    cos_t, sin_t = cosine.T, sine.T
    kv_part = jnp.zeros((4, 1, 16, 128), F32)
    own = other = jnp.zeros((128, 256), F32)
    rows, kv_part = decode(0, 1, place, scales, near, rotation, wkv, wkv_other, kv_part)
    own, other = project((0,), place, [rows], wq, wq_other, own, other)
    far_rows = []
    for k in (1, 3, 2):
        after = {1: (own,), 3: (), 2: (mask, cos_q, sin_q, cos_t, sin_t)}[k]
        rows, kv_part = decode(
            k, 4 if k == 2 else 1, place, scales, far[k], rotation, wkv, wkv_other, kv_part, after
        )
        far_rows.append(rows)
    kv = exchanged(kv_part.reshape(CHIPS, 16, 128))
    own, other = project((1, 3, 2), place, far_rows, wq, wq_other, own, other)
    recv = traded(other)
    kv_recv = traded(kv)
    attended = attend(
        head.reshape(1), prefix_len, own, recv, kv, kv_recv, cos_t, sin_t, cos_q, sin_q, mask, kv_cache
    )
    theirs = traded(attended)
    twice = jnp.asarray(np.concatenate([signs, signs], 1), BF16)
    sent = {}
    for hops in ((2,), (1, 3), (0,)):
        for hop, piece in zip(hops, partials(hops, place, attended, theirs, wo, wo_other, twice)):
            sent[hop] = piece
    sums = sent[0]
    for k in (2, 1, 3):
        sums = sums + first_shift(sent[k], k).astype(F32)
    summed = sums[0]
    for k in (2, 1, 3):
        summed = summed + second_shift(sums[k].astype(BF16), k).astype(F32)

    here = lax.dynamic_slice_in_dim(scales, rank * 4, 4)
    turned_in = in_codes.T.astype(F32) * jnp.repeat(here, RB)[:, None]
    turned = summed + turned_in
    peak = jnp.max(jnp.abs(turned.reshape(4, RB, 128)), (1, 2))
    next_rows = swapped(turned, "section")
    next_peak = swapped(peak, "section")
    everyone = lax.all_to_all(
        jnp.broadcast_to(next_peak[None], (64, 4)), ("dp", TENSOR), 0, 0, tiled=True
    )
    next_scales = jnp.max(everyone.reshape(2, 128), 0) + TINY
    scale_here = lax.dynamic_slice_in_dim(next_scales, rank * 4, 4)
    next_codes = (next_rows.T / jnp.repeat(scale_here, RB)[None, :]).astype(BF16)
    return (next_codes, next_scales[None])


def solution(mesh):
    rows = ("section", "dp")
    placed = (
        P(rows, TENSOR),
        P("section", None),
        P("section", None, TENSOR),
        P("section", None, None, None, TENSOR),
        P("section", TENSOR, None),
        P(rows, None, None, None, None),
        P(rows),
        P(rows, None),
    )
    return jax.shard_map(
        on_device,
        mesh=mesh,
        in_specs=placed,
        out_specs=(P(rows, TENSOR), P("section", None)),
        check_vma=False,
    )
```

```python
import functools
import math

import jax
import jax.numpy as jnp
import numpy as np
from jax import lax
from jax.experimental import pallas as pl
from jax.experimental.pallas import tpu as pltpu
from jax.sharding import PartitionSpec as P

HD = 128
RB = 128
CHIPS = 16
ROPE_BASE = 500000.0
TINY = 1e-06
TENSOR = "tensor"


def device(y, x, core):
    return (y * 4 + x) * 2 + core


F32 = jnp.float32
BF16 = jnp.bfloat16
NT = (((1,), (1,)), ((), ()))
LIGHT = pl.CostEstimate(flops=1024, bytes_accessed=1024, transcendentals=0)


def hadamard():
    index = np.arange(RB)
    common = index[:, None] & index[None, :]
    parity = np.zeros((RB, RB), np.int32)
    for place in range(7):
        parity = parity + (common >> place & 1)
    return np.where(parity % 2 == 0, 1.0, -1.0).astype(np.float32)


def ancestor_table(draft_parent):
    count, size = draft_parent.shape
    target = lax.broadcasted_iota(jnp.int32, (count, size, size), 2)
    source = lax.broadcasted_iota(jnp.int32, (count, size, size), 1)
    table = ((target == draft_parent[:, :, None]) | (target == source)).astype(F32)
    for _ in range(4):
        table = jnp.minimum(jnp.einsum("rij,rjk->rik", table, table), 1.0)
    return table


def swapped(block, axis):
    return lax.ppermute(block, axis, [(0, 1), (1, 0)])


def traded(block):
    return lax.ppermute(block, TENSOR, [(i, i ^ 1) for i in range(32)])


def exchanged(pieces):
    groups = [[chip * 2 + core for chip in range(CHIPS)] for core in range(2)]
    return lax.all_to_all(pieces, TENSOR, 0, 0, tiled=True, axis_index_groups=groups)


def shifted(block, by, second):
    pairs = []
    for y in range(4):
        for x in range(4):
            for core in range(2):
                along_y = (core == 1) != second
                to_y, to_x = ((y + by) % 4, x) if along_y else (y, (x + by) % 4)
                pairs.append((device(y, x, core), device(to_y, to_x, core)))
    return lax.ppermute(block, TENSOR, pairs)


def first_shift(block, by):
    return shifted(block, by, False)


def second_shift(block, by):
    return shifted(block, by, True)


def chip_at(place, first, second):
    first = lax.rem(place[1] + 4 + first, 4)
    second = lax.rem(place[2] + 4 + second, 4)
    return jnp.where(place[0] == 0, second * 4 + first, first * 4 + second)


def params(mebibytes):
    return pltpu.CompilerParams(vmem_limit_bytes=mebibytes << 20)


def decode_kernel(hop, waits, place, scale_ref, codes_ref, rotation_ref, *refs):
    own_refs, other_refs, kv_in, (rows_ref, kv_out) = refs[:4], refs[4:8], refs[8], refs[9 + waits :]
    for k in range(4):
        first = (chip_at(place, -k, -hop) * 2 + place[0]) * 4
        for half in range(2):
            product = jnp.dot(
                codes_ref[k, :, half * 256 : half * 256 + 256],
                rotation_ref[...],
                preferred_element_type=F32,
            )
            for b in range(2):
                factor = scale_ref[first + half * 2 + b] * F32(1.0 / math.sqrt(RB))
                at = k * 512 + half * 256 + b * 128
                rows_ref[:, at : at + 128] = (product[:, b * 128 : b * 128 + 128] * factor).astype(
                    BF16
                )
    weight = jnp.concatenate(
        [
            jnp.concatenate([ref[...] for ref in own_refs], 1),
            jnp.concatenate([ref[...] for ref in other_refs], 1),
        ],
        0,
    )
    total = lax.dot_general(weight, rows_ref[...], NT, preferred_element_type=F32)
    for h in range(4):
        own = total[h * 8 : h * 8 + 8]
        other = total[32 + h * 8 : 40 + h * 8]
        value = kv_in[h, 0] + jnp.concatenate(
            [jnp.where(place[0] == 0, own, other), jnp.where(place[0] == 0, other, own)], 0
        )
        for i in range(kv_out.shape[1]):
            kv_out[h, i] = value


def decode(hop, copies, place, scales, codes, rotation, own_weight, other_weight, kv_in, after=()):
    def kv_at(k):
        return pl.BlockSpec((32, 512), lambda i, p, s: (0, chip_at(p, -k, -hop) * 2 + p[0]))

    return pl.pallas_call(
        functools.partial(decode_kernel, hop, len(after)),
        grid_spec=pltpu.PrefetchScalarGridSpec(
            num_scalar_prefetch=2,
            grid=(1,),
            in_specs=[
                pl.BlockSpec((4, 128, 512), lambda i, p, s: (0, 0, 0)),
                pl.BlockSpec((256, 256), lambda i, p, s: (0, 0)),
                *(kv_at(k) for k in range(4)),
                *(kv_at(k) for k in range(4)),
                pl.BlockSpec((4, 1, 16, 128), lambda i, p, s: (0, 0, 0, 0)),
                *(pl.BlockSpec(memory_space=pl.ANY) for _ in after),
            ],
            out_specs=[
                pl.BlockSpec((128, 2048), lambda i, p, s: (0, 0)),
                pl.BlockSpec((4, copies, 16, 128), lambda i, p, s: (0, 0, 0, 0)),
            ],
        ),
        out_shape=[
            jax.ShapeDtypeStruct((128, 2048), BF16),
            jax.ShapeDtypeStruct((4, copies, 16, 128), F32),
        ],
        compiler_params=params(6),
        cost_estimate=LIGHT,
        name="decode",
    )(place, scales, codes, rotation, *[own_weight] * 4, *[other_weight] * 4, kv_in, *after)


def query_kernel(hops, place, *refs):
    count = len(hops)
    rows_refs, refs = refs[:count], refs[count:]
    own_weight, other_weight, own_in, other_in, own_out, other_out, tiles, sems = refs
    copies = []
    for i in range(4 * count):
        row = pl.multiple_of((chip_at(place, -(i % 4), -hops[i // 4]) * 2 + place[0]) * 512, 512)
        for side, weight in enumerate((own_weight, other_weight)):
            copies.append(
                pltpu.make_async_copy(
                    weight.at[pl.ds(row, 512), :], tiles.at[i, side], sems.at[i, side]
                )
            )
    for copy in copies:
        copy.start()
    totals = [own_in[...], other_in[...]]
    for i in range(4 * count):
        for side in range(2):
            copies[2 * i + side].wait()
            totals[side] += jnp.dot(
                rows_refs[i // 4][:, i % 4 * 512 : i % 4 * 512 + 512],
                tiles[i, side],
                preferred_element_type=F32,
            )
    own_out[...] = totals[0]
    other_out[...] = totals[1]


def project(hops, place, rows, own_weight, other_weight, own_in, other_in):
    count = len(hops)
    still = pl.BlockSpec((128, 256), lambda i, p: (0, 0))
    return pl.pallas_call(
        functools.partial(query_kernel, hops),
        grid_spec=pltpu.PrefetchScalarGridSpec(
            num_scalar_prefetch=1,
            grid=(1,),
            in_specs=[pl.BlockSpec((128, 2048), lambda i, p: (0, 0))] * count
            + [pl.BlockSpec(memory_space=pltpu.HBM)] * 2
            + [still, still],
            out_specs=[still, still],
            scratch_shapes=[
                pltpu.VMEM((4 * count, 2, 512, 256), BF16),
                pltpu.SemaphoreType.DMA((4 * count, 2)),
            ],
        ),
        out_shape=[jax.ShapeDtypeStruct((128, 256), F32)] * 2,
        compiler_params=params(4 + 4 * count),
        cost_estimate=LIGHT,
        name="query",
    )(place, *rows, own_weight, other_weight, own_in, other_in)


def attend_kernel(
    head_ref, length_ref, own_ref, recv_ref, kv_ref, kv_recv, cos_t, sin_t, cos_q, sin_q, mask_ref, cache_ref, out_ref
):
    score_scale = F32(1.0 / math.sqrt(HD))
    keys, values = [], []
    upper = lax.broadcasted_iota(jnp.int32, (8, 128), 0) < 4
    for chip in range(CHIPS):
        first = kv_ref[chip, 0:8] + kv_recv[chip, 0:8]
        second = kv_ref[chip, 8:16] + kv_recv[chip, 8:16]
        keys.append(jnp.where(upper, first, pltpu.roll(second, 4, 0)))
        values.append(jnp.where(upper, pltpu.roll(first, 4, 0), second))
    keys = jnp.concatenate(keys, 0).astype(BF16).astype(F32)
    values = jnp.concatenate(values, 0).astype(BF16)
    low, high = keys[:64], keys[64:]
    keys = jnp.concatenate(
        [low * cos_t[...] - high * sin_t[...], high * cos_t[...] + low * sin_t[...]], 0
    ).astype(BF16)
    heads = []
    for h in range(2):
        q = own_ref[:, h * 128 : h * 128 + 128] + recv_ref[:, h * 128 : h * 128 + 128]
        q = q * cos_q[...] + pltpu.roll(q, 64, 1) * sin_q[...]
        heads.append(q.astype(BF16))
    fresh = [
        jnp.dot(q, keys, preferred_element_type=F32) * score_scale for q in heads
    ]
    lane = lax.broadcasted_iota(jnp.int32, (32, 128), 1)
    for r in range(8):
        rows = slice(r * 16, r * 16 + 16)
        q = jnp.concatenate([heads[0][rows], heads[1][rows]], 0)
        old = (
            lax.dot_general(q, cache_ref[r, 0, 0], NT, preferred_element_type=F32) * score_scale
        )
        new = jnp.concatenate([fresh[0][rows], fresh[1][rows]], 0)
        mask = jnp.concatenate([mask_ref[rows, :]] * 2, 0)
        old = jnp.where(lane < length_ref[r], old, -jnp.inf)
        new = jnp.where(mask > 0.5, new, -jnp.inf)
        peak = jnp.maximum(
            jnp.max(old, -1, keepdims=True), jnp.max(new, -1, keepdims=True)
        )
        old = jnp.exp(old - peak)
        new = jnp.exp(new - peak)
        total = jnp.sum(old, -1, keepdims=True) + jnp.sum(new, -1, keepdims=True)
        old = (old / total).astype(BF16)
        new = (new / total).astype(BF16)
        mixed = jnp.dot(old, cache_ref[r, 0, 1], preferred_element_type=F32)
        mixed = mixed + lax.dot_general(new, values, NT, preferred_element_type=F32)
        mixed = mixed.astype(BF16)
        out_ref[rows, 0:128] = mixed[:16]
        out_ref[rows, 128:256] = mixed[16:]


def attend(head, lengths, own, recv, kv, kv_recv, cos_t, sin_t, cos_q, sin_q, mask, cache):
    def whole(array):
        return pl.BlockSpec(array.shape, lambda i, h, n: (0,) * array.ndim)

    arrays = (own, recv, kv, kv_recv, cos_t, sin_t, cos_q, sin_q, mask)
    return pl.pallas_call(
        attend_kernel,
        grid_spec=pltpu.PrefetchScalarGridSpec(
            num_scalar_prefetch=2,
            grid=(1,),
            in_specs=[whole(a) for a in arrays]
            + [pl.BlockSpec((8, 1, 2, 128, 128), lambda i, h, n: (0, h[0], 0, 0, 0))],
            out_specs=pl.BlockSpec((128, 256), lambda i, h, n: (0, 0)),
        ),
        out_shape=jax.ShapeDtypeStruct((128, 256), BF16),
        compiler_params=params(6),
        cost_estimate=pl.CostEstimate(
            flops=2 * 256 * 128 * 512, bytes_accessed=2 << 20, transcendentals=65536
        ),
        name="attend",
    )(head, lengths, *arrays, cache)


def partial_kernel(hops, place, mine, theirs, own_weight, other_weight, rotation_ref, *refs):
    outs, (tiles, sems) = refs[: len(hops)], refs[len(hops) :]
    unit = F32(1.0 / math.sqrt(RB))
    parts = [(out, at) for at in range(4) for out in range(len(hops))]
    copies = []
    for i, (out, at) in enumerate(parts):
        column = pl.multiple_of((chip_at(place, hops[out], at) * 2 + place[0]) * 512, 512)
        for side, weight in enumerate((own_weight, other_weight)):
            copies.append(
                pltpu.make_async_copy(
                    weight.at[:, pl.ds(column, 512)], tiles.at[i, side], sems.at[i, side]
                )
            )
    for copy in copies:
        copy.start()
    for i, (out, at) in enumerate(parts):
        copies[2 * i].wait()
        copies[2 * i + 1].wait()
        groups = (
            jnp.dot(mine[...], tiles[i, 0], preferred_element_type=F32),
            jnp.dot(theirs[...], tiles[i, 1], preferred_element_type=F32),
        )
        for b in range(4):
            halves = []
            for group in groups:
                block = group[:, b * 128 : b * 128 + 128]
                coarse = block.astype(BF16)
                fine = (block - coarse.astype(F32)).astype(BF16)
                halves.append(jnp.concatenate([coarse, fine], 1))
            both = lax.dot_general(
                rotation_ref[...],
                jnp.concatenate(halves, 0),
                NT,
                preferred_element_type=F32,
            )
            total = None
            for turned in (both[:, :128], both[:, 128:]):
                scale = jnp.max(jnp.abs(turned), 0, keepdims=True) * unit + TINY
                codes = (turned * (unit / scale)).astype(BF16)
                term = codes.astype(F32) * scale
                total = term if total is None else total + term
            outs[out][at, b * 128 : b * 128 + 128, :] = total.astype(outs[out].dtype)


def partials(hops, place, mine, theirs, own_weight, other_weight, rotation):
    count = 4 * len(hops)
    still = pl.BlockSpec((128, 256), lambda i, p: (0, 0))
    return pl.pallas_call(
        functools.partial(partial_kernel, hops),
        grid_spec=pltpu.PrefetchScalarGridSpec(
            num_scalar_prefetch=1,
            grid=(1,),
            in_specs=[still, still]
            + [pl.BlockSpec(memory_space=pltpu.HBM)] * 2
            + [still],
            out_specs=[pl.BlockSpec((4, 512, 128), lambda i, p: (0, 0, 0)) for _ in hops],
            scratch_shapes=[
                pltpu.VMEM((count, 2, 256, 512), BF16),
                pltpu.SemaphoreType.DMA((count, 2)),
            ],
        ),
        out_shape=[
            jax.ShapeDtypeStruct((4, 512, 128), BF16 if hop else F32) for hop in hops
        ],
        compiler_params=params(6 + 4 * len(hops)),
        cost_estimate=pl.CostEstimate(
            flops=2 * 128 * 2048 * 1024 * len(hops),
            bytes_accessed=len(hops) * 3 << 20,
            transcendentals=0,
        ),
        name="partials",
    )(place, mine, theirs, own_weight, other_weight, rotation)


def on_device(
    in_codes, in_scales, query_weight, kv_weight, out_weight, kv_cache, prefix_len, draft_parent
):
    rank = lax.axis_index(TENSOR)
    core = rank % 2
    head = rank // 8
    along_x = rank // 2 % 4
    place = jnp.stack(
        [core, jnp.where(core == 0, along_x, head), jnp.where(core == 0, head, along_x)]
    )
    signs = hadamard()
    scales = in_scales[0]

    near = jnp.stack([in_codes] + [first_shift(in_codes, k) for k in (1, 2, 3)])
    wq = query_weight[0]
    wq_other = traded(query_weight)[0]
    kv_other = traded(kv_weight)

    near, draft_parent, kv_weight, kv_other, out_weight = lax.optimization_barrier(
        (near, draft_parent, kv_weight, kv_other, out_weight)
    )

    far = {k: second_shift(near, k) for k in (1, 3, 2)}

    def as_rows(weight):
        return weight[0].transpose(2, 1, 3, 0).reshape(32, -1)

    wkv, wkv_other = as_rows(kv_weight), as_rows(kv_other)
    wo = out_weight[0]
    wo_other = traded(out_weight)[0]

    ancestry = ancestor_table(draft_parent)
    position = prefix_len.astype(F32)[:, None] + (jnp.sum(ancestry, -1) - 1.0)
    frequency = jnp.power(ROPE_BASE, -(jnp.arange(64, dtype=F32) / 64))
    angles = position.reshape(128, 1) * frequency
    cosine, sine = jnp.cos(angles), jnp.sin(angles)
    cos_q = jnp.concatenate([cosine, cosine], 1)
    sin_q = jnp.concatenate([-sine, sine], 1)
    block = jnp.eye(8, dtype=F32)
    mask = (ancestry[:, :, None, :] * block[:, None, :, None]).reshape(128, 128)

    blocks = np.kron(np.eye(2, dtype=np.float32), signs)
    rotation = jnp.asarray(blocks, BF16)

    cos_t, sin_t = cosine.T, sine.T
    kv_part = jnp.zeros((4, 1, 16, 128), F32)
    own = other = jnp.zeros((128, 256), F32)
    rows, kv_part = decode(0, 1, place, scales, near, rotation, wkv, wkv_other, kv_part)
    own, other = project((0,), place, [rows], wq, wq_other, own, other)
    far_rows = []
    for k in (1, 3, 2):
        after = {1: (own,), 3: (), 2: (mask, cos_q, sin_q, cos_t, sin_t)}[k]
        rows, kv_part = decode(
            k, 4 if k == 2 else 1, place, scales, far[k], rotation, wkv, wkv_other, kv_part, after
        )
        far_rows.append(rows)
    kv = exchanged(kv_part.reshape(CHIPS, 16, 128))
    own, other = project((1, 3, 2), place, far_rows, wq, wq_other, own, other)
    recv = traded(other)
    kv_recv = traded(kv)
    attended = attend(
        head.reshape(1), prefix_len, own, recv, kv, kv_recv, cos_t, sin_t, cos_q, sin_q, mask, kv_cache
    )
    theirs = traded(attended)
    twice = jnp.asarray(np.concatenate([signs, signs], 1), BF16)
    sent = {}
    for hops in ((2,), (1, 3), (0,)):
        for hop, piece in zip(hops, partials(hops, place, attended, theirs, wo, wo_other, twice)):
            sent[hop] = piece
    sums = sent[0]
    for k in (2, 1, 3):
        sums = sums + first_shift(sent[k], k).astype(F32)
    summed = sums[0]
    for k in (2, 1, 3):
        summed = summed + second_shift(sums[k].astype(BF16), k).astype(F32)

    here = lax.dynamic_slice_in_dim(scales, rank * 4, 4)
    turned_in = in_codes.T.astype(F32) * jnp.repeat(here, RB)[:, None]
    turned = summed + turned_in
    peak = jnp.max(jnp.abs(turned.reshape(4, RB, 128)), (1, 2))
    next_peak = jnp.maximum(
        swapped(peak, "section"),
        lax.ppermute(peak, ("section", "dp"), [(0, 3), (1, 2), (2, 1), (3, 0)]),
    )
    next_rows = swapped(turned, "section")
    scale_here = next_peak + TINY
    mine = exchanged(jnp.broadcast_to(scale_here[None], (CHIPS, 4)))
    theirs = traded(mine)
    by_core = jnp.where(core == 0, jnp.stack([mine, theirs], 1), jnp.stack([theirs, mine], 1))
    next_scales = by_core.reshape(1, 128)
    next_codes = (next_rows.T / jnp.repeat(scale_here, RB)[None, :]).astype(BF16)
    return (next_codes, next_scales)


def solution(mesh):
    rows = ("section", "dp")
    placed = (
        P(rows, TENSOR),
        P("section", None),
        P("section", None, TENSOR),
        P("section", None, None, None, TENSOR),
        P("section", TENSOR, None),
        P(rows, None, None, None, None),
        P(rows),
        P(rows, None),
    )
    return jax.shard_map(
        on_device,
        mesh=mesh,
        in_specs=placed,
        out_specs=(P(rows, TENSOR), P("section", None)),
        check_vma=False,
    )
```

```python
import functools
import math

import jax
import jax.numpy as jnp
import numpy as np
from jax import lax
from jax.experimental import pallas as pl
from jax.experimental.pallas import tpu as pltpu
from jax.sharding import PartitionSpec as P

HD = 128
RB = 128
CHIPS = 16
ROPE_BASE = 500000.0
TINY = 1e-06
TENSOR = "tensor"


def device(y, x, core):
    return (y * 4 + x) * 2 + core


F32 = jnp.float32
BF16 = jnp.bfloat16
NT = (((1,), (1,)), ((), ()))
LIGHT = pl.CostEstimate(flops=1024, bytes_accessed=1024, transcendentals=0)


def hadamard():
    index = np.arange(RB)
    common = index[:, None] & index[None, :]
    parity = np.zeros((RB, RB), np.int32)
    for place in range(7):
        parity = parity + (common >> place & 1)
    return np.where(parity % 2 == 0, 1.0, -1.0).astype(np.float32)


def ancestor_table(draft_parent):
    count, size = draft_parent.shape
    target = lax.broadcasted_iota(jnp.int32, (count, size, size), 2)
    source = lax.broadcasted_iota(jnp.int32, (count, size, size), 1)
    table = ((target == draft_parent[:, :, None]) | (target == source)).astype(F32)
    for _ in range(4):
        table = jnp.minimum(jnp.einsum("rij,rjk->rik", table, table), 1.0)
    return table


def swapped(block, axis):
    return lax.ppermute(block, axis, [(0, 1), (1, 0)])


def traded(block):
    return lax.ppermute(block, TENSOR, [(i, i ^ 1) for i in range(32)])


def exchanged(pieces):
    groups = [[chip * 2 + core for chip in range(CHIPS)] for core in range(2)]
    return lax.all_to_all(pieces, TENSOR, 0, 0, tiled=True, axis_index_groups=groups)


def shifted(block, by, second):
    pairs = []
    for y in range(4):
        for x in range(4):
            for core in range(2):
                along_y = (core == 1) != second
                to_y, to_x = ((y + by) % 4, x) if along_y else (y, (x + by) % 4)
                pairs.append((device(y, x, core), device(to_y, to_x, core)))
    return lax.ppermute(block, TENSOR, pairs)


def first_shift(block, by):
    return shifted(block, by, False)


def second_shift(block, by):
    return shifted(block, by, True)


def chip_at(place, first, second):
    first = lax.rem(place[1] + 4 + first, 4)
    second = lax.rem(place[2] + 4 + second, 4)
    return jnp.where(place[0] == 0, second * 4 + first, first * 4 + second)


def in_hbm(array):
    return pltpu.with_memory_space_constraint(array, pltpu.HBM)


def params(mebibytes):
    return pltpu.CompilerParams(vmem_limit_bytes=mebibytes << 20)


def decode_kernel(hop, waits, place, scale_ref, codes_ref, rotation_ref, *refs):
    own_refs, other_refs, kv_in, (rows_ref, kv_out) = refs[:4], refs[4:8], refs[8], refs[9 + waits :]
    for k in range(4):
        first = (chip_at(place, -k, -hop) * 2 + place[0]) * 4
        for half in range(2):
            product = jnp.dot(
                codes_ref[k, :, half * 256 : half * 256 + 256],
                rotation_ref[...],
                preferred_element_type=F32,
            )
            for b in range(2):
                factor = scale_ref[first + half * 2 + b] * F32(1.0 / math.sqrt(RB))
                at = k * 512 + half * 256 + b * 128
                rows_ref[:, at : at + 128] = (product[:, b * 128 : b * 128 + 128] * factor).astype(
                    BF16
                )
    weight = jnp.concatenate(
        [
            jnp.concatenate([ref[...] for ref in own_refs], 1),
            jnp.concatenate([ref[...] for ref in other_refs], 1),
        ],
        0,
    )
    total = lax.dot_general(weight, rows_ref[...], NT, preferred_element_type=F32)
    for h in range(4):
        own = total[h * 8 : h * 8 + 8]
        other = total[32 + h * 8 : 40 + h * 8]
        value = kv_in[h, 0] + jnp.concatenate(
            [jnp.where(place[0] == 0, own, other), jnp.where(place[0] == 0, other, own)], 0
        )
        for i in range(kv_out.shape[1]):
            kv_out[h, i] = value


def decode(hop, copies, place, scales, codes, rotation, own_weight, other_weight, kv_in, after=()):
    def kv_at(k):
        return pl.BlockSpec((32, 512), lambda i, p, s: (0, chip_at(p, -k, -hop) * 2 + p[0]))

    return pl.pallas_call(
        functools.partial(decode_kernel, hop, len(after)),
        grid_spec=pltpu.PrefetchScalarGridSpec(
            num_scalar_prefetch=2,
            grid=(1,),
            in_specs=[
                pl.BlockSpec((4, 128, 512), lambda i, p, s: (0, 0, 0)),
                pl.BlockSpec((256, 256), lambda i, p, s: (0, 0)),
                *(kv_at(k) for k in range(4)),
                *(kv_at(k) for k in range(4)),
                pl.BlockSpec((4, 1, 16, 128), lambda i, p, s: (0, 0, 0, 0)),
                *(pl.BlockSpec(memory_space=pl.ANY) for _ in after),
            ],
            out_specs=[
                pl.BlockSpec((128, 2048), lambda i, p, s: (0, 0)),
                pl.BlockSpec((4, copies, 16, 128), lambda i, p, s: (0, 0, 0, 0)),
            ],
        ),
        out_shape=[
            (pltpu.HBM if hop else jax.ShapeDtypeStruct)((128, 2048), BF16),
            (pltpu.HBM if copies > 1 else jax.ShapeDtypeStruct)((4, copies, 16, 128), F32),
        ],
        compiler_params=params(6),
        cost_estimate=LIGHT,
        name="decode",
    )(place, scales, codes, rotation, *[own_weight] * 4, *[other_weight] * 4, kv_in, *after)


def query_kernel(hops, place, *refs):
    count = len(hops)
    rows_refs, refs = refs[:count], refs[count:]
    own_weight, other_weight, own_in, other_in, own_out, other_out, tiles, sems = refs
    copies = []
    for i in range(4 * count):
        row = pl.multiple_of((chip_at(place, -(i % 4), -hops[i // 4]) * 2 + place[0]) * 512, 512)
        for side, weight in enumerate((own_weight, other_weight)):
            copies.append(
                pltpu.make_async_copy(
                    weight.at[pl.ds(row, 512), :], tiles.at[i, side], sems.at[i, side]
                )
            )
    for copy in copies:
        copy.start()
    totals = [own_in[...], other_in[...]]
    for i in range(4 * count):
        for side in range(2):
            copies[2 * i + side].wait()
            totals[side] += jnp.dot(
                rows_refs[i // 4][:, i % 4 * 512 : i % 4 * 512 + 512],
                tiles[i, side],
                preferred_element_type=F32,
            )
    own_out[...] = totals[0]
    other_out[...] = totals[1]


def project(hops, place, rows, own_weight, other_weight, own_in, other_in):
    count = len(hops)
    still = pl.BlockSpec((128, 256), lambda i, p: (0, 0))
    return pl.pallas_call(
        functools.partial(query_kernel, hops),
        grid_spec=pltpu.PrefetchScalarGridSpec(
            num_scalar_prefetch=1,
            grid=(1,),
            in_specs=[pl.BlockSpec((128, 2048), lambda i, p: (0, 0))] * count
            + [pl.BlockSpec(memory_space=pltpu.HBM)] * 2
            + [still, still],
            out_specs=[still, still],
            scratch_shapes=[
                pltpu.VMEM((4 * count, 2, 512, 256), BF16),
                pltpu.SemaphoreType.DMA((4 * count, 2)),
            ],
        ),
        out_shape=[(pltpu.HBM if count == 1 else jax.ShapeDtypeStruct)((128, 256), F32)] * 2,
        compiler_params=params(4 + 4 * count),
        cost_estimate=LIGHT,
        name="query",
    )(place, *rows, own_weight, other_weight, own_in, other_in)


def attend_kernel(
    head_ref, length_ref, own_ref, recv_ref, kv_ref, kv_recv, cos_t, sin_t, cos_q, sin_q, mask_ref, cache_ref, out_ref
):
    score_scale = F32(1.0 / math.sqrt(HD))
    keys, values = [], []
    upper = lax.broadcasted_iota(jnp.int32, (8, 128), 0) < 4
    for chip in range(CHIPS):
        first = kv_ref[chip, 0:8] + kv_recv[chip, 0:8]
        second = kv_ref[chip, 8:16] + kv_recv[chip, 8:16]
        keys.append(jnp.where(upper, first, pltpu.roll(second, 4, 0)))
        values.append(jnp.where(upper, pltpu.roll(first, 4, 0), second))
    keys = jnp.concatenate(keys, 0).astype(BF16).astype(F32)
    values = jnp.concatenate(values, 0).astype(BF16)
    low, high = keys[:64], keys[64:]
    keys = jnp.concatenate(
        [low * cos_t[...] - high * sin_t[...], high * cos_t[...] + low * sin_t[...]], 0
    ).astype(BF16)
    heads = []
    for h in range(2):
        q = own_ref[:, h * 128 : h * 128 + 128] + recv_ref[:, h * 128 : h * 128 + 128]
        q = q * cos_q[...] + pltpu.roll(q, 64, 1) * sin_q[...]
        heads.append(q.astype(BF16))
    fresh = [
        jnp.dot(q, keys, preferred_element_type=F32) * score_scale for q in heads
    ]
    lane = lax.broadcasted_iota(jnp.int32, (32, 128), 1)
    for r in range(8):
        rows = slice(r * 16, r * 16 + 16)
        q = jnp.concatenate([heads[0][rows], heads[1][rows]], 0)
        old = (
            lax.dot_general(q, cache_ref[r, 0, 0], NT, preferred_element_type=F32) * score_scale
        )
        new = jnp.concatenate([fresh[0][rows], fresh[1][rows]], 0)
        mask = jnp.concatenate([mask_ref[rows, :]] * 2, 0)
        old = jnp.where(lane < length_ref[r], old, -jnp.inf)
        new = jnp.where(mask > 0.5, new, -jnp.inf)
        peak = jnp.maximum(
            jnp.max(old, -1, keepdims=True), jnp.max(new, -1, keepdims=True)
        )
        old = jnp.exp(old - peak)
        new = jnp.exp(new - peak)
        total = jnp.sum(old, -1, keepdims=True) + jnp.sum(new, -1, keepdims=True)
        old = (old / total).astype(BF16)
        new = (new / total).astype(BF16)
        mixed = jnp.dot(old, cache_ref[r, 0, 1], preferred_element_type=F32)
        mixed = mixed + lax.dot_general(new, values, NT, preferred_element_type=F32)
        mixed = mixed.astype(BF16)
        out_ref[rows, 0:128] = mixed[:16]
        out_ref[rows, 128:256] = mixed[16:]


def attend(head, lengths, own, recv, kv, kv_recv, cos_t, sin_t, cos_q, sin_q, mask, cache):
    def whole(array):
        return pl.BlockSpec(array.shape, lambda i, h, n: (0,) * array.ndim)

    arrays = (own, recv, kv, kv_recv, cos_t, sin_t, cos_q, sin_q, mask)
    return pl.pallas_call(
        attend_kernel,
        grid_spec=pltpu.PrefetchScalarGridSpec(
            num_scalar_prefetch=2,
            grid=(1,),
            in_specs=[whole(a) for a in arrays]
            + [pl.BlockSpec((8, 1, 2, 128, 128), lambda i, h, n: (0, h[0], 0, 0, 0))],
            out_specs=pl.BlockSpec((128, 256), lambda i, h, n: (0, 0)),
        ),
        out_shape=jax.ShapeDtypeStruct((128, 256), BF16),
        compiler_params=params(6),
        cost_estimate=pl.CostEstimate(
            flops=2 * 256 * 128 * 512, bytes_accessed=2 << 20, transcendentals=65536
        ),
        name="attend",
    )(head, lengths, *arrays, cache)


def partial_kernel(hops, place, mine, theirs, own_weight, other_weight, rotation_ref, *refs):
    outs, (tiles, sems) = refs[: len(hops)], refs[len(hops) :]
    unit = F32(1.0 / math.sqrt(RB))
    parts = [(out, at) for at in range(4) for out in range(len(hops))]
    copies = []
    for i, (out, at) in enumerate(parts):
        column = pl.multiple_of((chip_at(place, hops[out], at) * 2 + place[0]) * 512, 512)
        for side, weight in enumerate((own_weight, other_weight)):
            copies.append(
                pltpu.make_async_copy(
                    weight.at[:, pl.ds(column, 512)], tiles.at[i, side], sems.at[i, side]
                )
            )
    for copy in copies:
        copy.start()
    for i, (out, at) in enumerate(parts):
        copies[2 * i].wait()
        copies[2 * i + 1].wait()
        groups = (
            jnp.dot(mine[...], tiles[i, 0], preferred_element_type=F32),
            jnp.dot(theirs[...], tiles[i, 1], preferred_element_type=F32),
        )
        for b in range(4):
            halves = []
            for group in groups:
                block = group[:, b * 128 : b * 128 + 128]
                coarse = block.astype(BF16)
                fine = (block - coarse.astype(F32)).astype(BF16)
                halves.append(jnp.concatenate([coarse, fine], 1))
            both = lax.dot_general(
                rotation_ref[...],
                jnp.concatenate(halves, 0),
                NT,
                preferred_element_type=F32,
            )
            total = None
            for turned in (both[:, :128], both[:, 128:]):
                scale = jnp.max(jnp.abs(turned), 0, keepdims=True) * unit + TINY
                codes = (turned * (unit / scale)).astype(BF16)
                term = codes.astype(F32) * scale
                total = term if total is None else total + term
            outs[out][at, b * 128 : b * 128 + 128, :] = total.astype(outs[out].dtype)


def partials(hops, place, mine, theirs, own_weight, other_weight, rotation):
    count = 4 * len(hops)
    still = pl.BlockSpec((128, 256), lambda i, p: (0, 0))
    return pl.pallas_call(
        functools.partial(partial_kernel, hops),
        grid_spec=pltpu.PrefetchScalarGridSpec(
            num_scalar_prefetch=1,
            grid=(1,),
            in_specs=[still, still]
            + [pl.BlockSpec(memory_space=pltpu.HBM)] * 2
            + [still],
            out_specs=[pl.BlockSpec((4, 512, 128), lambda i, p: (0, 0, 0)) for _ in hops],
            scratch_shapes=[
                pltpu.VMEM((count, 2, 256, 512), BF16),
                pltpu.SemaphoreType.DMA((count, 2)),
            ],
        ),
        out_shape=[
            jax.ShapeDtypeStruct((4, 512, 128), BF16 if hop else F32) for hop in hops
        ],
        compiler_params=params(6 + 4 * len(hops)),
        cost_estimate=pl.CostEstimate(
            flops=2 * 128 * 2048 * 1024 * len(hops),
            bytes_accessed=len(hops) * 3 << 20,
            transcendentals=0,
        ),
        name="partials",
    )(place, mine, theirs, own_weight, other_weight, rotation)


def on_device(
    in_codes, in_scales, query_weight, kv_weight, out_weight, kv_cache, prefix_len, draft_parent
):
    rank = lax.axis_index(TENSOR)
    core = rank % 2
    head = rank // 8
    along_x = rank // 2 % 4
    place = jnp.stack(
        [core, jnp.where(core == 0, along_x, head), jnp.where(core == 0, head, along_x)]
    )
    signs = hadamard()
    scales = in_scales[0]

    near = jnp.stack([in_codes] + [first_shift(in_codes, k) for k in (1, 2, 3)])
    wq = in_hbm(query_weight[0])
    wq_other = in_hbm(traded(query_weight)[0])
    kv_other = traded(kv_weight)

    near, draft_parent, kv_weight, kv_other, out_weight = lax.optimization_barrier(
        (near, draft_parent, kv_weight, kv_other, out_weight)
    )

    far = {k: second_shift(near, k) for k in (1, 3, 2)}

    def as_rows(weight):
        return weight[0].transpose(2, 1, 3, 0).reshape(32, -1)

    wkv, wkv_other = as_rows(kv_weight), as_rows(kv_other)
    wo = in_hbm(out_weight[0])
    wo_other = in_hbm(traded(out_weight)[0])

    ancestry = ancestor_table(draft_parent)
    position = prefix_len.astype(F32)[:, None] + (jnp.sum(ancestry, -1) - 1.0)
    frequency = jnp.power(ROPE_BASE, -(jnp.arange(64, dtype=F32) / 64))
    angles = position.reshape(128, 1) * frequency
    cosine, sine = jnp.cos(angles), jnp.sin(angles)
    cos_q = jnp.concatenate([cosine, cosine], 1)
    sin_q = jnp.concatenate([-sine, sine], 1)
    block = jnp.eye(8, dtype=F32)
    mask = (ancestry[:, :, None, :] * block[:, None, :, None]).reshape(128, 128)

    blocks = np.kron(np.eye(2, dtype=np.float32), signs)
    rotation = jnp.asarray(blocks, BF16)

    cos_t, sin_t = cosine.T, sine.T
    kv_part = jnp.zeros((4, 1, 16, 128), F32)
    own = other = jnp.zeros((128, 256), F32)
    rows, kv_part = decode(0, 1, place, scales, near, rotation, wkv, wkv_other, kv_part)
    own, other = project((0,), place, [rows], wq, wq_other, own, other)
    far_rows = []
    for k in (1, 3, 2):
        after = {1: (in_hbm(own),), 3: (), 2: (mask, cos_q, sin_q, cos_t, sin_t)}[k]
        rows, kv_part = decode(
            k, 4 if k == 2 else 1, place, scales, far[k], rotation, wkv, wkv_other, kv_part, after
        )
        far_rows.append(in_hbm(rows))
    kv = exchanged(kv_part.reshape(CHIPS, 16, 128))
    own, other = project(
        (1, 3, 2), place, far_rows, wq, wq_other, in_hbm(own), in_hbm(other)
    )
    recv = traded(other)
    kv_recv = traded(kv)
    attended = attend(
        head.reshape(1), prefix_len, own, recv, kv, kv_recv, cos_t, sin_t, cos_q, sin_q, mask, kv_cache
    )
    theirs = traded(attended)
    twice = jnp.asarray(np.concatenate([signs, signs], 1), BF16)
    sent = {}
    for hops in ((2,), (1, 3), (0,)):
        for hop, piece in zip(hops, partials(hops, place, attended, theirs, wo, wo_other, twice)):
            sent[hop] = piece
    sums = sent[0]
    for k in (2, 1, 3):
        sums = sums + first_shift(sent[k], k).astype(F32)
    summed = sums[0]
    for k in (2, 1, 3):
        summed = summed + second_shift(sums[k].astype(BF16), k).astype(F32)

    here = lax.dynamic_slice_in_dim(scales, rank * 4, 4)
    turned_in = in_codes.T.astype(F32) * jnp.repeat(here, RB)[:, None]
    turned = summed + turned_in
    peak = jnp.max(jnp.abs(turned.reshape(4, RB, 128)), (1, 2))
    next_peak = jnp.maximum(
        swapped(peak, "section"),
        lax.ppermute(peak, ("section", "dp"), [(0, 3), (1, 2), (2, 1), (3, 0)]),
    )
    next_rows = swapped(turned, "section")
    scale_here = next_peak + TINY
    mine = exchanged(jnp.broadcast_to(scale_here[None], (CHIPS, 4)))
    theirs = traded(mine)
    by_core = jnp.where(core == 0, jnp.stack([mine, theirs], 1), jnp.stack([theirs, mine], 1))
    next_scales = by_core.reshape(1, 128)
    next_codes = (next_rows.T / jnp.repeat(scale_here, RB)[None, :]).astype(BF16)
    return (next_codes, next_scales)


def solution(mesh):
    rows = ("section", "dp")
    placed = (
        P(rows, TENSOR),
        P("section", None),
        P("section", None, TENSOR),
        P("section", None, None, None, TENSOR),
        P("section", TENSOR, None),
        P(rows, None, None, None, None),
        P(rows),
        P(rows, None),
    )
    return jax.shard_map(
        on_device,
        mesh=mesh,
        in_specs=placed,
        out_specs=(P(rows, TENSOR), P("section", None)),
        check_vma=False,
    )
```

```python
import functools
import math

import jax
import jax.numpy as jnp
import numpy as np
from jax import lax
from jax.experimental import pallas as pl
from jax.experimental.pallas import tpu as pltpu
from jax.sharding import PartitionSpec as P

HD = 128
RB = 128
CHIPS = 16
ROPE_BASE = 500000.0
TINY = 1e-06
TENSOR = "tensor"


def device(y, x, core):
    return (y * 4 + x) * 2 + core


F32 = jnp.float32
BF16 = jnp.bfloat16
NT = (((1,), (1,)), ((), ()))
LIGHT = pl.CostEstimate(flops=1024, bytes_accessed=1024, transcendentals=0)


def hadamard():
    index = np.arange(RB)
    common = index[:, None] & index[None, :]
    parity = np.zeros((RB, RB), np.int32)
    for place in range(7):
        parity = parity + (common >> place & 1)
    return np.where(parity % 2 == 0, 1.0, -1.0).astype(np.float32)


def ancestor_table(draft_parent):
    count, size = draft_parent.shape
    target = lax.broadcasted_iota(jnp.int32, (count, size, size), 2)
    source = lax.broadcasted_iota(jnp.int32, (count, size, size), 1)
    table = ((target == draft_parent[:, :, None]) | (target == source)).astype(F32)
    for _ in range(4):
        table = jnp.minimum(jnp.einsum("rij,rjk->rik", table, table), 1.0)
    return table


def swapped(block, axis):
    return lax.ppermute(block, axis, [(0, 1), (1, 0)])


def traded(block):
    return lax.ppermute(block, TENSOR, [(i, i ^ 1) for i in range(32)])


def exchanged(pieces):
    groups = [[chip * 2 + core for chip in range(CHIPS)] for core in range(2)]
    return lax.all_to_all(pieces, TENSOR, 0, 0, tiled=True, axis_index_groups=groups)


def shifted(block, by, second):
    pairs = []
    for y in range(4):
        for x in range(4):
            for core in range(2):
                along_y = (core == 1) != second
                to_y, to_x = ((y + by) % 4, x) if along_y else (y, (x + by) % 4)
                pairs.append((device(y, x, core), device(to_y, to_x, core)))
    return lax.ppermute(block, TENSOR, pairs)


def first_shift(block, by):
    return shifted(block, by, False)


def second_shift(block, by):
    return shifted(block, by, True)


def chip_at(place, first, second):
    first = lax.rem(place[1] + 4 + first, 4)
    second = lax.rem(place[2] + 4 + second, 4)
    return jnp.where(place[0] == 0, second * 4 + first, first * 4 + second)


def in_hbm(array):
    return pltpu.with_memory_space_constraint(array, pltpu.HBM)


def params(mebibytes):
    return pltpu.CompilerParams(vmem_limit_bytes=mebibytes << 20)


def decode_kernel(hops, waits, place, scale_ref, *refs):
    codes_refs, refs = refs[: len(hops)], refs[len(hops) :]
    rotation_ref, own_weight, other_weight, kv_in = refs[:4]
    rows_ref, kv_out = refs[4 + waits :]
    own = other = None
    for i, hop in enumerate(hops):
        own_tiles, other_tiles = [], []
        for k in range(4):
            tile = chip_at(place, -k, -hop) * 2 + place[0]
            for half in range(2):
                product = jnp.dot(
                    codes_refs[i][k, :, half * 256 : half * 256 + 256],
                    rotation_ref[...],
                    preferred_element_type=F32,
                )
                for b in range(2):
                    factor = scale_ref[tile * 4 + half * 2 + b] * F32(1.0 / math.sqrt(RB))
                    at = i * 2048 + k * 512 + half * 256 + b * 128
                    rows_ref[:, at : at + 128] = (
                        product[:, b * 128 : b * 128 + 128] * factor
                    ).astype(BF16)
            column = pl.ds(pl.multiple_of(tile * 512, 512), 512)
            own_tiles.append(own_weight[:, column])
            other_tiles.append(other_weight[:, column])
        weight = jnp.concatenate(
            [jnp.concatenate(own_tiles, 1), jnp.concatenate(other_tiles, 1)], 0
        )
        total = lax.dot_general(
            weight,
            rows_ref[:, i * 2048 : i * 2048 + 2048],
            NT,
            preferred_element_type=F32,
        )
        own = total[:32] if own is None else own + total[:32]
        other = total[32:] if other is None else other + total[32:]
    for h in range(4):
        mine, theirs = own[h * 8 : h * 8 + 8], other[h * 8 : h * 8 + 8]
        value = kv_in[h, 0] + jnp.concatenate(
            [jnp.where(place[0] == 0, mine, theirs), jnp.where(place[0] == 0, theirs, mine)], 0
        )
        for i in range(kv_out.shape[1]):
            kv_out[h, i] = value


def decode(hops, copies, place, scales, codes, rotation, own_weight, other_weight, kv_in, after=()):
    def whole(array):
        return pl.BlockSpec(array.shape, lambda i, p, s: (0,) * array.ndim)

    arrays = (*codes, rotation, own_weight, other_weight, kv_in)
    outs = [(128, 2048 * len(hops)), (4, copies, 16, 128)]
    return pl.pallas_call(
        functools.partial(decode_kernel, hops, len(after)),
        grid_spec=pltpu.PrefetchScalarGridSpec(
            num_scalar_prefetch=2,
            grid=(1,),
            in_specs=[
                *(whole(array) for array in arrays),
                *(pl.BlockSpec(memory_space=pl.ANY) for _ in after),
            ],
            out_specs=[
                pl.BlockSpec(outs[0], lambda i, p, s: (0, 0)),
                pl.BlockSpec(outs[1], lambda i, p, s: (0, 0, 0, 0)),
            ],
        ),
        out_shape=[
            pltpu.HBM(outs[0], BF16),
            (pltpu.HBM if copies > 1 else jax.ShapeDtypeStruct)(outs[1], F32),
        ],
        compiler_params=params(16),
        cost_estimate=LIGHT,
        name="decode",
    )(place, scales, *arrays, *after)


def query_kernel(groups, place, *refs):
    rows_refs, refs = refs[: len(groups)], refs[len(groups) :]
    own_weight, other_weight, own_out, other_out, tiles, sems = refs
    parts = [
        (g, i * 4 + k, hop, k)
        for g, hops in enumerate(groups)
        for i, hop in enumerate(hops)
        for k in range(4)
    ]
    copies = []
    for n, (_, _, hop, k) in enumerate(parts):
        row = pl.multiple_of((chip_at(place, -k, -hop) * 2 + place[0]) * 512, 512)
        for side, weight in enumerate((own_weight, other_weight)):
            copies.append(
                pltpu.make_async_copy(
                    weight.at[pl.ds(row, 512), :], tiles.at[n, side], sems.at[n, side]
                )
            )
    for copy in copies:
        copy.start()
    totals = [jnp.zeros(own_out.shape, F32)] * 2
    for n, (g, at, _, _) in enumerate(parts):
        for side in range(2):
            copies[2 * n + side].wait()
            totals[side] += jnp.dot(
                rows_refs[g][:, at * 512 : at * 512 + 512],
                tiles[n, side],
                preferred_element_type=F32,
            )
    own_out[...] = totals[0]
    other_out[...] = totals[1]


def project(groups, place, rows, own_weight, other_weight):
    still = pl.BlockSpec((128, 256), lambda i, p: (0, 0))
    return pl.pallas_call(
        functools.partial(query_kernel, groups),
        grid_spec=pltpu.PrefetchScalarGridSpec(
            num_scalar_prefetch=1,
            grid=(1,),
            in_specs=[pl.BlockSpec(part.shape, lambda i, p: (0, 0)) for part in rows]
            + [pl.BlockSpec(memory_space=pltpu.HBM)] * 2,
            out_specs=[still, still],
            scratch_shapes=[
                pltpu.VMEM((CHIPS, 2, 512, 256), BF16),
                pltpu.SemaphoreType.DMA((CHIPS, 2)),
            ],
        ),
        out_shape=[jax.ShapeDtypeStruct((128, 256), F32)] * 2,
        compiler_params=params(20),
        cost_estimate=LIGHT,
        name="query",
    )(place, *rows, own_weight, other_weight)


def attend_kernel(
    head_ref, length_ref, own_ref, recv_ref, kv_ref, kv_recv, cos_t, sin_t, cos_q, sin_q, mask_ref, cache_ref, out_ref
):
    score_scale = F32(1.0 / math.sqrt(HD))
    keys, values = [], []
    upper = lax.broadcasted_iota(jnp.int32, (8, 128), 0) < 4
    for chip in range(CHIPS):
        first = kv_ref[chip, 0:8] + kv_recv[chip, 0:8]
        second = kv_ref[chip, 8:16] + kv_recv[chip, 8:16]
        keys.append(jnp.where(upper, first, pltpu.roll(second, 4, 0)))
        values.append(jnp.where(upper, pltpu.roll(first, 4, 0), second))
    keys = jnp.concatenate(keys, 0).astype(BF16).astype(F32)
    values = jnp.concatenate(values, 0).astype(BF16)
    low, high = keys[:64], keys[64:]
    keys = jnp.concatenate(
        [low * cos_t[...] - high * sin_t[...], high * cos_t[...] + low * sin_t[...]], 0
    ).astype(BF16)
    heads = []
    for h in range(2):
        q = own_ref[:, h * 128 : h * 128 + 128] + recv_ref[:, h * 128 : h * 128 + 128]
        q = q * cos_q[...] + pltpu.roll(q, 64, 1) * sin_q[...]
        heads.append(q.astype(BF16))
    fresh = [
        jnp.dot(q, keys, preferred_element_type=F32) * score_scale for q in heads
    ]
    lane = lax.broadcasted_iota(jnp.int32, (32, 128), 1)
    for r in range(8):
        rows = slice(r * 16, r * 16 + 16)
        q = jnp.concatenate([heads[0][rows], heads[1][rows]], 0)
        old = (
            lax.dot_general(q, cache_ref[r, 0, 0], NT, preferred_element_type=F32) * score_scale
        )
        new = jnp.concatenate([fresh[0][rows], fresh[1][rows]], 0)
        mask = jnp.concatenate([mask_ref[rows, :]] * 2, 0)
        old = jnp.where(lane < length_ref[r], old, -jnp.inf)
        new = jnp.where(mask > 0.5, new, -jnp.inf)
        peak = jnp.maximum(
            jnp.max(old, -1, keepdims=True), jnp.max(new, -1, keepdims=True)
        )
        old = jnp.exp(old - peak)
        new = jnp.exp(new - peak)
        total = jnp.sum(old, -1, keepdims=True) + jnp.sum(new, -1, keepdims=True)
        old = (old / total).astype(BF16)
        new = (new / total).astype(BF16)
        mixed = jnp.dot(old, cache_ref[r, 0, 1], preferred_element_type=F32)
        mixed = mixed + lax.dot_general(new, values, NT, preferred_element_type=F32)
        mixed = mixed.astype(BF16)
        out_ref[rows, 0:128] = mixed[:16]
        out_ref[rows, 128:256] = mixed[16:]


def attend(head, lengths, own, recv, kv, kv_recv, cos_t, sin_t, cos_q, sin_q, mask, cache):
    def whole(array):
        return pl.BlockSpec(array.shape, lambda i, h, n: (0,) * array.ndim)

    arrays = (own, recv, kv, kv_recv, cos_t, sin_t, cos_q, sin_q, mask)
    return pl.pallas_call(
        attend_kernel,
        grid_spec=pltpu.PrefetchScalarGridSpec(
            num_scalar_prefetch=2,
            grid=(1,),
            in_specs=[whole(a) for a in arrays]
            + [pl.BlockSpec((8, 1, 2, 128, 128), lambda i, h, n: (0, h[0], 0, 0, 0))],
            out_specs=pl.BlockSpec((128, 256), lambda i, h, n: (0, 0)),
        ),
        out_shape=jax.ShapeDtypeStruct((128, 256), BF16),
        compiler_params=params(6),
        cost_estimate=pl.CostEstimate(
            flops=2 * 256 * 128 * 512, bytes_accessed=2 << 20, transcendentals=65536
        ),
        name="attend",
    )(head, lengths, *arrays, cache)


def partial_kernel(hops, place, mine, theirs, own_weight, other_weight, rotation_ref, *refs):
    outs, (tiles, sems) = refs[: len(hops)], refs[len(hops) :]
    unit = F32(1.0 / math.sqrt(RB))
    parts = [(out, at) for at in range(4) for out in range(len(hops))]
    copies = []
    for i, (out, at) in enumerate(parts):
        column = pl.multiple_of((chip_at(place, hops[out], at) * 2 + place[0]) * 512, 512)
        for side, weight in enumerate((own_weight, other_weight)):
            copies.append(
                pltpu.make_async_copy(
                    weight.at[:, pl.ds(column, 512)], tiles.at[i, side], sems.at[i, side]
                )
            )
    for copy in copies:
        copy.start()
    for i, (out, at) in enumerate(parts):
        copies[2 * i].wait()
        copies[2 * i + 1].wait()
        groups = (
            jnp.dot(mine[...], tiles[i, 0], preferred_element_type=F32),
            jnp.dot(theirs[...], tiles[i, 1], preferred_element_type=F32),
        )
        for b in range(4):
            halves = []
            for group in groups:
                block = group[:, b * 128 : b * 128 + 128]
                coarse = block.astype(BF16)
                fine = (block - coarse.astype(F32)).astype(BF16)
                halves.append(jnp.concatenate([coarse, fine], 1))
            both = lax.dot_general(
                rotation_ref[...],
                jnp.concatenate(halves, 0),
                NT,
                preferred_element_type=F32,
            )
            total = None
            for turned in (both[:, :128], both[:, 128:]):
                scale = jnp.max(jnp.abs(turned), 0, keepdims=True) * unit + TINY
                codes = (turned * (unit / scale)).astype(BF16)
                term = codes.astype(F32) * scale
                total = term if total is None else total + term
            outs[out][at, b * 128 : b * 128 + 128, :] = total.astype(outs[out].dtype)


def partials(hops, place, mine, theirs, own_weight, other_weight, rotation):
    count = 4 * len(hops)
    still = pl.BlockSpec((128, 256), lambda i, p: (0, 0))
    return pl.pallas_call(
        functools.partial(partial_kernel, hops),
        grid_spec=pltpu.PrefetchScalarGridSpec(
            num_scalar_prefetch=1,
            grid=(1,),
            in_specs=[still, still]
            + [pl.BlockSpec(memory_space=pltpu.HBM)] * 2
            + [still],
            out_specs=[pl.BlockSpec((4, 512, 128), lambda i, p: (0, 0, 0)) for _ in hops],
            scratch_shapes=[
                pltpu.VMEM((count, 2, 256, 512), BF16),
                pltpu.SemaphoreType.DMA((count, 2)),
            ],
        ),
        out_shape=[
            jax.ShapeDtypeStruct((4, 512, 128), BF16 if hop else F32) for hop in hops
        ],
        compiler_params=params(6 + 4 * len(hops)),
        cost_estimate=pl.CostEstimate(
            flops=2 * 128 * 2048 * 1024 * len(hops),
            bytes_accessed=len(hops) * 3 << 20,
            transcendentals=0,
        ),
        name="partials",
    )(place, mine, theirs, own_weight, other_weight, rotation)


def on_device(
    in_codes, in_scales, query_weight, kv_weight, out_weight, kv_cache, prefix_len, draft_parent
):
    rank = lax.axis_index(TENSOR)
    core = rank % 2
    head = rank // 8
    along_x = rank // 2 % 4
    place = jnp.stack(
        [core, jnp.where(core == 0, along_x, head), jnp.where(core == 0, head, along_x)]
    )
    signs = hadamard()
    scales = in_scales[0]

    near = jnp.stack([in_codes] + [first_shift(in_codes, k) for k in (1, 2, 3)])
    wq = in_hbm(query_weight[0])
    wq_other = in_hbm(traded(query_weight)[0])
    kv_other = traded(kv_weight)

    near, draft_parent, kv_weight, kv_other, out_weight = lax.optimization_barrier(
        (near, draft_parent, kv_weight, kv_other, out_weight)
    )

    far = {k: second_shift(near, k) for k in (1, 3, 2)}

    def as_rows(weight):
        return weight[0].transpose(2, 1, 3, 0).reshape(32, -1)

    wkv, wkv_other = as_rows(kv_weight), as_rows(kv_other)
    wo = in_hbm(out_weight[0])
    wo_other = in_hbm(traded(out_weight)[0])

    ancestry = ancestor_table(draft_parent)
    position = prefix_len.astype(F32)[:, None] + (jnp.sum(ancestry, -1) - 1.0)
    frequency = jnp.power(ROPE_BASE, -(jnp.arange(64, dtype=F32) / 64))
    angles = position.reshape(128, 1) * frequency
    cosine, sine = jnp.cos(angles), jnp.sin(angles)
    cos_q = jnp.concatenate([cosine, cosine], 1)
    sin_q = jnp.concatenate([-sine, sine], 1)
    block = jnp.eye(8, dtype=F32)
    mask = (ancestry[:, :, None, :] * block[:, None, :, None]).reshape(128, 128)

    blocks = np.kron(np.eye(2, dtype=np.float32), signs)
    rotation = jnp.asarray(blocks, BF16)

    cos_t, sin_t = cosine.T, sine.T
    near_rows, kv_part = decode(
        (0,), 1, place, scales, (near,), rotation, wkv, wkv_other, jnp.zeros((4, 1, 16, 128), F32)
    )
    hops = (1, 3, 2)
    far_rows, kv_part = decode(
        hops,
        4,
        place,
        scales,
        tuple(far[k] for k in hops),
        rotation,
        wkv,
        wkv_other,
        kv_part,
        (mask, cos_q, sin_q, cos_t, sin_t),
    )
    kv = exchanged(kv_part.reshape(CHIPS, 16, 128))
    own, other = project(
        ((0,), hops), place, (in_hbm(near_rows), in_hbm(far_rows)), wq, wq_other
    )
    recv = traded(other)
    kv_recv = traded(kv)
    attended = attend(
        head.reshape(1), prefix_len, own, recv, kv, kv_recv, cos_t, sin_t, cos_q, sin_q, mask, kv_cache
    )
    theirs = traded(attended)
    twice = jnp.asarray(np.concatenate([signs, signs], 1), BF16)
    sent = {}
    for hops in ((2,), (1, 3), (0,)):
        for hop, piece in zip(hops, partials(hops, place, attended, theirs, wo, wo_other, twice)):
            sent[hop] = piece
    sums = sent[0]
    for k in (2, 1, 3):
        sums = sums + first_shift(sent[k], k).astype(F32)
    summed = sums[0]
    for k in (2, 1, 3):
        summed = summed + second_shift(sums[k].astype(BF16), k).astype(F32)

    here = lax.dynamic_slice_in_dim(scales, rank * 4, 4)
    turned_in = in_codes.T.astype(F32) * jnp.repeat(here, RB)[:, None]
    turned = summed + turned_in
    peak = jnp.max(jnp.abs(turned.reshape(4, RB, 128)), (1, 2))
    next_peak = swapped(peak, "section")
    next_rows = swapped(turned, "section")
    everyone = lax.all_to_all(
        jnp.broadcast_to(next_peak[None], (64, 4)), ("dp", TENSOR), 0, 0, tiled=True
    )
    next_scales = jnp.max(everyone.reshape(2, 128), 0) + TINY
    scale_here = lax.dynamic_slice_in_dim(next_scales, rank * 4, 4)
    next_codes = (next_rows.T / jnp.repeat(scale_here, RB)[None, :]).astype(BF16)
    return (next_codes, next_scales[None])


def solution(mesh):
    rows = ("section", "dp")
    placed = (
        P(rows, TENSOR),
        P("section", None),
        P("section", None, TENSOR),
        P("section", None, None, None, TENSOR),
        P("section", TENSOR, None),
        P(rows, None, None, None, None),
        P(rows),
        P(rows, None),
    )
    return jax.shard_map(
        on_device,
        mesh=mesh,
        in_specs=placed,
        out_specs=(P(rows, TENSOR), P("section", None)),
        check_vma=False,
    )
```

```python
import functools
import math

import jax
import jax.numpy as jnp
import numpy as np
from jax import lax
from jax.experimental import pallas as pl
from jax.experimental.pallas import tpu as pltpu
from jax.sharding import PartitionSpec as P

HD = 128
RB = 128
CHIPS = 16
ROPE_BASE = 500000.0
TINY = 1e-06
TENSOR = "tensor"


def device(y, x, core):
    return (y * 4 + x) * 2 + core


F32 = jnp.float32
BF16 = jnp.bfloat16
NT = (((1,), (1,)), ((), ()))
LIGHT = pl.CostEstimate(flops=1024, bytes_accessed=1024, transcendentals=0)


def hadamard():
    index = np.arange(RB)
    common = index[:, None] & index[None, :]
    parity = np.zeros((RB, RB), np.int32)
    for place in range(7):
        parity = parity + (common >> place & 1)
    return np.where(parity % 2 == 0, 1.0, -1.0).astype(np.float32)


def ancestor_table(draft_parent):
    count, size = draft_parent.shape
    target = lax.broadcasted_iota(jnp.int32, (count, size, size), 2)
    source = lax.broadcasted_iota(jnp.int32, (count, size, size), 1)
    table = ((target == draft_parent[:, :, None]) | (target == source)).astype(F32)
    for _ in range(4):
        table = jnp.minimum(jnp.einsum("rij,rjk->rik", table, table), 1.0)
    return table


def swapped(block, axis):
    return lax.ppermute(block, axis, [(0, 1), (1, 0)])


def traded(block):
    return lax.ppermute(block, TENSOR, [(i, i ^ 1) for i in range(32)])


def exchanged(pieces):
    groups = [[chip * 2 + core for chip in range(CHIPS)] for core in range(2)]
    return lax.all_to_all(pieces, TENSOR, 0, 0, tiled=True, axis_index_groups=groups)


def shifted(block, by, second):
    pairs = []
    for y in range(4):
        for x in range(4):
            for core in range(2):
                along_y = (core == 1) != second
                to_y, to_x = ((y + by) % 4, x) if along_y else (y, (x + by) % 4)
                pairs.append((device(y, x, core), device(to_y, to_x, core)))
    return lax.ppermute(block, TENSOR, pairs)


def first_shift(block, by):
    return shifted(block, by, False)


def second_shift(block, by):
    return shifted(block, by, True)


def chip_at(place, first, second):
    first = lax.rem(place[1] + 4 + first, 4)
    second = lax.rem(place[2] + 4 + second, 4)
    return jnp.where(place[0] == 0, second * 4 + first, first * 4 + second)


def in_hbm(array):
    return pltpu.with_memory_space_constraint(array, pltpu.HBM)


def params(mebibytes):
    return pltpu.CompilerParams(vmem_limit_bytes=mebibytes << 20)


def decode_kernel(hops, waits, place, scale_ref, *refs):
    codes_refs, refs = refs[: len(hops)], refs[len(hops) :]
    rotation_ref, own_weight, other_weight, kv_in = refs[:4]
    rows_ref, kv_out = refs[4 + waits :]
    own = other = None
    for i, hop in enumerate(hops):
        own_tiles, other_tiles = [], []
        for k in range(4):
            tile = chip_at(place, -k, -hop) * 2 + place[0]
            for half in range(2):
                product = jnp.dot(
                    codes_refs[i][k, :, half * 256 : half * 256 + 256],
                    rotation_ref[...],
                    preferred_element_type=F32,
                )
                for b in range(2):
                    factor = scale_ref[tile * 4 + half * 2 + b] * F32(1.0 / math.sqrt(RB))
                    at = i * 2048 + k * 512 + half * 256 + b * 128
                    rows_ref[:, at : at + 128] = (
                        product[:, b * 128 : b * 128 + 128] * factor
                    ).astype(BF16)
            column = pl.ds(pl.multiple_of(tile * 512, 512), 512)
            own_tiles.append(own_weight[:, column])
            other_tiles.append(other_weight[:, column])
        weight = jnp.concatenate(
            [jnp.concatenate(own_tiles, 1), jnp.concatenate(other_tiles, 1)], 0
        )
        total = lax.dot_general(
            weight,
            rows_ref[:, i * 2048 : i * 2048 + 2048],
            NT,
            preferred_element_type=F32,
        )
        own = total[:32] if own is None else own + total[:32]
        other = total[32:] if other is None else other + total[32:]
    for h in range(4):
        mine, theirs = own[h * 8 : h * 8 + 8], other[h * 8 : h * 8 + 8]
        value = kv_in[h, 0] + jnp.concatenate(
            [jnp.where(place[0] == 0, mine, theirs), jnp.where(place[0] == 0, theirs, mine)], 0
        )
        for i in range(kv_out.shape[1]):
            kv_out[h, i] = value


def decode(hops, copies, place, scales, codes, rotation, own_weight, other_weight, kv_in, after=()):
    def whole(array):
        return pl.BlockSpec(array.shape, lambda i, p, s: (0,) * array.ndim)

    arrays = (*codes, rotation, own_weight, other_weight, kv_in)
    outs = [(128, 2048 * len(hops)), (4, copies, 16, 128)]
    return pl.pallas_call(
        functools.partial(decode_kernel, hops, len(after)),
        grid_spec=pltpu.PrefetchScalarGridSpec(
            num_scalar_prefetch=2,
            grid=(1,),
            in_specs=[
                *(whole(array) for array in arrays),
                *(pl.BlockSpec(memory_space=pl.ANY) for _ in after),
            ],
            out_specs=[
                pl.BlockSpec(outs[0], lambda i, p, s: (0, 0)),
                pl.BlockSpec(outs[1], lambda i, p, s: (0, 0, 0, 0)),
            ],
        ),
        out_shape=[
            pltpu.HBM(outs[0], BF16),
            (pltpu.HBM if copies > 1 else jax.ShapeDtypeStruct)(outs[1], F32),
        ],
        compiler_params=params(16),
        cost_estimate=LIGHT,
        name="decode",
    )(place, scales, *arrays, *after)


def query_kernel(groups, place, *refs):
    rows_refs, refs = refs[: len(groups)], refs[len(groups) :]
    own_weight, other_weight, own_out, other_out, tiles, sems = refs
    parts = [
        (g, i * 4 + k, hop, k)
        for g, hops in enumerate(groups)
        for i, hop in enumerate(hops)
        for k in range(4)
    ]
    copies = []
    for n, (_, _, hop, k) in enumerate(parts):
        row = pl.multiple_of((chip_at(place, -k, -hop) * 2 + place[0]) * 512, 512)
        for side, weight in enumerate((own_weight, other_weight)):
            copies.append(
                pltpu.make_async_copy(
                    weight.at[pl.ds(row, 512), :], tiles.at[n, side], sems.at[n, side]
                )
            )
    for copy in copies:
        copy.start()
    totals = [jnp.zeros(own_out.shape, F32)] * 2
    for n, (g, at, _, _) in enumerate(parts):
        for side in range(2):
            copies[2 * n + side].wait()
            totals[side] += jnp.dot(
                rows_refs[g][:, at * 512 : at * 512 + 512],
                tiles[n, side],
                preferred_element_type=F32,
            )
    own_out[...] = totals[0]
    other_out[...] = totals[1]


def project(groups, place, rows, own_weight, other_weight):
    still = pl.BlockSpec((128, 256), lambda i, p: (0, 0))
    return pl.pallas_call(
        functools.partial(query_kernel, groups),
        grid_spec=pltpu.PrefetchScalarGridSpec(
            num_scalar_prefetch=1,
            grid=(1,),
            in_specs=[pl.BlockSpec(part.shape, lambda i, p: (0, 0)) for part in rows]
            + [pl.BlockSpec(memory_space=pltpu.HBM)] * 2,
            out_specs=[still, still],
            scratch_shapes=[
                pltpu.VMEM((CHIPS, 2, 512, 256), BF16),
                pltpu.SemaphoreType.DMA((CHIPS, 2)),
            ],
        ),
        out_shape=[jax.ShapeDtypeStruct((128, 256), F32)] * 2,
        compiler_params=params(20),
        cost_estimate=pl.CostEstimate(
            flops=2 * 128 * 8192 * 512, bytes_accessed=40 << 20, transcendentals=0
        ),
        name="query",
    )(place, *rows, own_weight, other_weight)


def attend_kernel(
    head_ref, length_ref, own_ref, recv_ref, kv_ref, kv_recv, cos_t, sin_t, cos_q, sin_q, mask_ref, cache_ref, out_ref
):
    score_scale = F32(1.0 / math.sqrt(HD))
    keys, values = [], []
    upper = lax.broadcasted_iota(jnp.int32, (8, 128), 0) < 4
    for chip in range(CHIPS):
        first = kv_ref[chip, 0:8] + kv_recv[chip, 0:8]
        second = kv_ref[chip, 8:16] + kv_recv[chip, 8:16]
        keys.append(jnp.where(upper, first, pltpu.roll(second, 4, 0)))
        values.append(jnp.where(upper, pltpu.roll(first, 4, 0), second))
    keys = jnp.concatenate(keys, 0).astype(BF16).astype(F32)
    values = jnp.concatenate(values, 0).astype(BF16)
    low, high = keys[:64], keys[64:]
    keys = jnp.concatenate(
        [low * cos_t[...] - high * sin_t[...], high * cos_t[...] + low * sin_t[...]], 0
    ).astype(BF16)
    heads = []
    for h in range(2):
        q = own_ref[:, h * 128 : h * 128 + 128] + recv_ref[:, h * 128 : h * 128 + 128]
        q = q * cos_q[...] + pltpu.roll(q, 64, 1) * sin_q[...]
        heads.append(q.astype(BF16))
    fresh = [
        jnp.dot(q, keys, preferred_element_type=F32) * score_scale for q in heads
    ]
    lane = lax.broadcasted_iota(jnp.int32, (32, 128), 1)
    for r in range(8):
        rows = slice(r * 16, r * 16 + 16)
        q = jnp.concatenate([heads[0][rows], heads[1][rows]], 0)
        old = (
            lax.dot_general(q, cache_ref[r, 0, 0], NT, preferred_element_type=F32) * score_scale
        )
        new = jnp.concatenate([fresh[0][rows], fresh[1][rows]], 0)
        mask = jnp.concatenate([mask_ref[rows, :]] * 2, 0)
        old = jnp.where(lane < length_ref[r], old, -jnp.inf)
        new = jnp.where(mask > 0.5, new, -jnp.inf)
        peak = jnp.maximum(
            jnp.max(old, -1, keepdims=True), jnp.max(new, -1, keepdims=True)
        )
        old = jnp.exp(old - peak)
        new = jnp.exp(new - peak)
        total = jnp.sum(old, -1, keepdims=True) + jnp.sum(new, -1, keepdims=True)
        old = (old / total).astype(BF16)
        new = (new / total).astype(BF16)
        mixed = jnp.dot(old, cache_ref[r, 0, 1], preferred_element_type=F32)
        mixed = mixed + lax.dot_general(new, values, NT, preferred_element_type=F32)
        mixed = mixed.astype(BF16)
        out_ref[rows, 0:128] = mixed[:16]
        out_ref[rows, 128:256] = mixed[16:]


def attend(head, lengths, own, recv, kv, kv_recv, cos_t, sin_t, cos_q, sin_q, mask, cache):
    def whole(array):
        return pl.BlockSpec(array.shape, lambda i, h, n: (0,) * array.ndim)

    arrays = (own, recv, kv, kv_recv, cos_t, sin_t, cos_q, sin_q, mask)
    return pl.pallas_call(
        attend_kernel,
        grid_spec=pltpu.PrefetchScalarGridSpec(
            num_scalar_prefetch=2,
            grid=(1,),
            in_specs=[whole(a) for a in arrays]
            + [pl.BlockSpec((8, 1, 2, 128, 128), lambda i, h, n: (0, h[0], 0, 0, 0))],
            out_specs=pl.BlockSpec((128, 256), lambda i, h, n: (0, 0)),
        ),
        out_shape=jax.ShapeDtypeStruct((128, 256), BF16),
        compiler_params=params(6),
        cost_estimate=pl.CostEstimate(
            flops=2 * 256 * 128 * 512, bytes_accessed=2 << 20, transcendentals=65536
        ),
        name="attend",
    )(head, lengths, *arrays, cache)


def partial_kernel(hops, place, mine, theirs, own_weight, other_weight, rotation_ref, *refs):
    outs, (tiles, sems) = refs[: len(hops)], refs[len(hops) :]
    unit = F32(1.0 / math.sqrt(RB))
    parts = [(out, at) for at in range(4) for out in range(len(hops))]
    copies = []
    for i, (out, at) in enumerate(parts):
        column = pl.multiple_of((chip_at(place, hops[out], at) * 2 + place[0]) * 512, 512)
        for side, weight in enumerate((own_weight, other_weight)):
            copies.append(
                pltpu.make_async_copy(
                    weight.at[:, pl.ds(column, 512)], tiles.at[i, side], sems.at[i, side]
                )
            )
    for copy in copies:
        copy.start()
    for i, (out, at) in enumerate(parts):
        copies[2 * i].wait()
        copies[2 * i + 1].wait()
        groups = (
            jnp.dot(mine[...], tiles[i, 0], preferred_element_type=F32),
            jnp.dot(theirs[...], tiles[i, 1], preferred_element_type=F32),
        )
        for b in range(4):
            halves = []
            for group in groups:
                block = group[:, b * 128 : b * 128 + 128]
                coarse = block.astype(BF16)
                fine = (block - coarse.astype(F32)).astype(BF16)
                halves.append(jnp.concatenate([coarse, fine], 1))
            both = lax.dot_general(
                rotation_ref[...],
                jnp.concatenate(halves, 0),
                NT,
                preferred_element_type=F32,
            )
            total = None
            for turned in (both[:, :128], both[:, 128:]):
                scale = jnp.max(jnp.abs(turned), 0, keepdims=True) * unit + TINY
                codes = (turned * (unit / scale)).astype(BF16)
                term = codes.astype(F32) * scale
                total = term if total is None else total + term
            outs[out][at, b * 128 : b * 128 + 128, :] = total.astype(outs[out].dtype)


def partials(hops, place, mine, theirs, own_weight, other_weight, rotation):
    count = 4 * len(hops)
    still = pl.BlockSpec((128, 256), lambda i, p: (0, 0))
    return pl.pallas_call(
        functools.partial(partial_kernel, hops),
        grid_spec=pltpu.PrefetchScalarGridSpec(
            num_scalar_prefetch=1,
            grid=(1,),
            in_specs=[still, still]
            + [pl.BlockSpec(memory_space=pltpu.HBM)] * 2
            + [still],
            out_specs=[pl.BlockSpec((4, 512, 128), lambda i, p: (0, 0, 0)) for _ in hops],
            scratch_shapes=[
                pltpu.VMEM((count, 2, 256, 512), BF16),
                pltpu.SemaphoreType.DMA((count, 2)),
            ],
        ),
        out_shape=[
            jax.ShapeDtypeStruct((4, 512, 128), BF16 if hop else F32) for hop in hops
        ],
        compiler_params=params(6 + 4 * len(hops)),
        cost_estimate=pl.CostEstimate(
            flops=2 * 128 * 2048 * 1024 * len(hops),
            bytes_accessed=len(hops) * 3 << 20,
            transcendentals=0,
        ),
        name="partials",
    )(place, mine, theirs, own_weight, other_weight, rotation)


def on_device(
    in_codes, in_scales, query_weight, kv_weight, out_weight, kv_cache, prefix_len, draft_parent
):
    rank = lax.axis_index(TENSOR)
    core = rank % 2
    head = rank // 8
    along_x = rank // 2 % 4
    place = jnp.stack(
        [core, jnp.where(core == 0, along_x, head), jnp.where(core == 0, head, along_x)]
    )
    signs = hadamard()
    scales = in_scales[0]

    near = jnp.stack([in_codes] + [first_shift(in_codes, k) for k in (1, 2, 3)])
    wq = in_hbm(query_weight[0])
    wq_other = in_hbm(traded(query_weight)[0])
    kv_other = traded(kv_weight)

    near, draft_parent, kv_weight, kv_other, out_weight = lax.optimization_barrier(
        (near, draft_parent, kv_weight, kv_other, out_weight)
    )

    far = {k: second_shift(near, k) for k in (1, 3, 2)}

    def as_rows(weight):
        return weight[0].transpose(2, 1, 3, 0).reshape(32, -1)

    wkv, wkv_other = as_rows(kv_weight), as_rows(kv_other)
    wo = in_hbm(out_weight[0])
    wo_other = in_hbm(traded(out_weight)[0])

    ancestry = ancestor_table(draft_parent)
    position = prefix_len.astype(F32)[:, None] + (jnp.sum(ancestry, -1) - 1.0)
    frequency = jnp.power(ROPE_BASE, -(jnp.arange(64, dtype=F32) / 64))
    angles = position.reshape(128, 1) * frequency
    cosine, sine = jnp.cos(angles), jnp.sin(angles)
    cos_q = jnp.concatenate([cosine, cosine], 1)
    sin_q = jnp.concatenate([-sine, sine], 1)
    block = jnp.eye(8, dtype=F32)
    mask = (ancestry[:, :, None, :] * block[:, None, :, None]).reshape(128, 128)

    blocks = np.kron(np.eye(2, dtype=np.float32), signs)
    rotation = jnp.asarray(blocks, BF16)

    cos_t, sin_t = cosine.T, sine.T
    near_rows, kv_part = decode(
        (0,), 1, place, scales, (near,), rotation, wkv, wkv_other, jnp.zeros((4, 1, 16, 128), F32)
    )
    hops = (1, 3, 2)
    far_rows, kv_part = decode(
        hops,
        4,
        place,
        scales,
        tuple(far[k] for k in hops),
        rotation,
        wkv,
        wkv_other,
        kv_part,
        (mask, cos_q, sin_q, cos_t, sin_t),
    )
    kv = exchanged(kv_part.reshape(CHIPS, 16, 128))
    own, other = project(
        ((0,), hops), place, (in_hbm(near_rows), in_hbm(far_rows)), wq, wq_other
    )
    recv = traded(other)
    kv_recv = traded(kv)
    attended = attend(
        head.reshape(1), prefix_len, own, recv, kv, kv_recv, cos_t, sin_t, cos_q, sin_q, mask, kv_cache
    )
    theirs = traded(attended)
    twice = jnp.asarray(np.concatenate([signs, signs], 1), BF16)
    sent = {}
    for hops in ((2,), (1, 3), (0,)):
        for hop, piece in zip(hops, partials(hops, place, attended, theirs, wo, wo_other, twice)):
            sent[hop] = piece
    sums = sent[0]
    for k in (2, 1, 3):
        sums = sums + first_shift(sent[k], k).astype(F32)
    summed = sums[0]
    for k in (2, 1, 3):
        summed = summed + second_shift(sums[k].astype(BF16), k).astype(F32)

    here = lax.dynamic_slice_in_dim(scales, rank * 4, 4)
    turned_in = in_codes.T.astype(F32) * jnp.repeat(here, RB)[:, None]
    turned = summed + turned_in
    peak = jnp.max(jnp.abs(turned.reshape(4, RB, 128)), (1, 2))
    everyone = lax.all_to_all(
        jnp.broadcast_to(peak[None], (64, 4)), ("dp", TENSOR), 0, 0, tiled=True
    )
    out_scale = jnp.max(everyone.reshape(2, 128), 0) + TINY
    here = lax.dynamic_slice_in_dim(out_scale, rank * 4, 4)
    out_codes = (turned.T / jnp.repeat(here, RB)[None, :]).astype(BF16)
    next_codes = swapped(out_codes, "section")
    next_scales = swapped(out_scale[None], "section")
    return (next_codes, next_scales)


def solution(mesh):
    rows = ("section", "dp")
    placed = (
        P(rows, TENSOR),
        P("section", None),
        P("section", None, TENSOR),
        P("section", None, None, None, TENSOR),
        P("section", TENSOR, None),
        P(rows, None, None, None, None),
        P(rows),
        P(rows, None),
    )
    return jax.shard_map(
        on_device,
        mesh=mesh,
        in_specs=placed,
        out_specs=(P(rows, TENSOR), P("section", None)),
        check_vma=False,
    )
```

```python
import functools
import math

import jax
import jax.numpy as jnp
import numpy as np
from jax import lax
from jax.experimental import pallas as pl
from jax.experimental.pallas import tpu as pltpu
from jax.sharding import PartitionSpec as P

HD = 128
RB = 128
CHIPS = 16
ROPE_BASE = 500000.0
TINY = 1e-06
TENSOR = "tensor"


def device(y, x, core):
    return (y * 4 + x) * 2 + core


F32 = jnp.float32
BF16 = jnp.bfloat16
NT = (((1,), (1,)), ((), ()))
LIGHT = pl.CostEstimate(flops=1024, bytes_accessed=1024, transcendentals=0)


def hadamard():
    index = np.arange(RB)
    common = index[:, None] & index[None, :]
    parity = np.zeros((RB, RB), np.int32)
    for place in range(7):
        parity = parity + (common >> place & 1)
    return np.where(parity % 2 == 0, 1.0, -1.0).astype(np.float32)


def ancestor_table(draft_parent):
    count, size = draft_parent.shape
    target = lax.broadcasted_iota(jnp.int32, (count, size, size), 2)
    source = lax.broadcasted_iota(jnp.int32, (count, size, size), 1)
    table = ((target == draft_parent[:, :, None]) | (target == source)).astype(F32)
    for _ in range(4):
        table = jnp.minimum(jnp.einsum("rij,rjk->rik", table, table), 1.0)
    return table


def swapped(block, axis):
    return lax.ppermute(block, axis, [(0, 1), (1, 0)])


def traded(block):
    return lax.ppermute(block, TENSOR, [(i, i ^ 1) for i in range(32)])


def exchanged(pieces):
    groups = [[chip * 2 + core for chip in range(CHIPS)] for core in range(2)]
    return lax.all_to_all(pieces, TENSOR, 0, 0, tiled=True, axis_index_groups=groups)


def shifted(block, by, second):
    pairs = []
    for y in range(4):
        for x in range(4):
            for core in range(2):
                along_y = (core == 1) != second
                to_y, to_x = ((y + by) % 4, x) if along_y else (y, (x + by) % 4)
                pairs.append((device(y, x, core), device(to_y, to_x, core)))
    return lax.ppermute(block, TENSOR, pairs)


def first_shift(block, by):
    return shifted(block, by, False)


def second_shift(block, by):
    return shifted(block, by, True)


def chip_at(place, first, second):
    first = lax.rem(place[1] + 4 + first, 4)
    second = lax.rem(place[2] + 4 + second, 4)
    return jnp.where(place[0] == 0, second * 4 + first, first * 4 + second)


def in_hbm(array):
    return pltpu.with_memory_space_constraint(array, pltpu.HBM)


def params(mebibytes):
    return pltpu.CompilerParams(vmem_limit_bytes=mebibytes << 20)


def decode_kernel(hops, waits, place, scale_ref, *refs):
    codes_refs, refs = refs[: len(hops)], refs[len(hops) :]
    rotation_ref, own_weight, other_weight, kv_in = refs[:4]
    rows_ref, kv_out = refs[4 + waits :]
    own = other = None
    for i, hop in enumerate(hops):
        own_tiles, other_tiles = [], []
        for k in range(4):
            tile = chip_at(place, -k, -hop) * 2 + place[0]
            for half in range(2):
                product = jnp.dot(
                    codes_refs[i][k, :, half * 256 : half * 256 + 256],
                    rotation_ref[...],
                    preferred_element_type=F32,
                )
                for b in range(2):
                    factor = scale_ref[tile * 4 + half * 2 + b] * F32(1.0 / math.sqrt(RB))
                    at = i * 2048 + k * 512 + half * 256 + b * 128
                    rows_ref[:, at : at + 128] = (
                        product[:, b * 128 : b * 128 + 128] * factor
                    ).astype(BF16)
            column = pl.ds(pl.multiple_of(tile * 512, 512), 512)
            own_tiles.append(own_weight[:, column])
            other_tiles.append(other_weight[:, column])
        weight = jnp.concatenate(
            [jnp.concatenate(own_tiles, 1), jnp.concatenate(other_tiles, 1)], 0
        )
        total = lax.dot_general(
            weight,
            rows_ref[:, i * 2048 : i * 2048 + 2048],
            NT,
            preferred_element_type=F32,
        )
        own = total[:32] if own is None else own + total[:32]
        other = total[32:] if other is None else other + total[32:]
    for h in range(4):
        mine, theirs = own[h * 8 : h * 8 + 8], other[h * 8 : h * 8 + 8]
        value = kv_in[h, 0] + jnp.concatenate(
            [jnp.where(place[0] == 0, mine, theirs), jnp.where(place[0] == 0, theirs, mine)], 0
        )
        for i in range(kv_out.shape[1]):
            kv_out[h, i] = value


def decode(hops, copies, place, scales, codes, rotation, own_weight, other_weight, kv_in, after=()):
    def whole(array):
        return pl.BlockSpec(array.shape, lambda i, p, s: (0,) * array.ndim)

    arrays = (*codes, rotation, own_weight, other_weight, kv_in)
    outs = [(128, 2048 * len(hops)), (4, copies, 16, 128)]
    return pl.pallas_call(
        functools.partial(decode_kernel, hops, len(after)),
        grid_spec=pltpu.PrefetchScalarGridSpec(
            num_scalar_prefetch=2,
            grid=(1,),
            in_specs=[
                *(whole(array) for array in arrays),
                *(pl.BlockSpec(memory_space=pl.ANY) for _ in after),
            ],
            out_specs=[
                pl.BlockSpec(outs[0], lambda i, p, s: (0, 0)),
                pl.BlockSpec(outs[1], lambda i, p, s: (0, 0, 0, 0)),
            ],
        ),
        out_shape=[
            pltpu.HBM(outs[0], BF16),
            (pltpu.HBM if copies > 1 else jax.ShapeDtypeStruct)(outs[1], F32),
        ],
        compiler_params=params(16),
        cost_estimate=LIGHT,
        name="decode",
    )(place, scales, *arrays, *after)


def query_kernel(groups, place, *refs):
    rows_refs, refs = refs[: len(groups)], refs[len(groups) :]
    own_weight, other_weight, own_out, other_out, tiles, sems = refs
    parts = [
        (g, i * 4 + k, hop, k)
        for g, hops in enumerate(groups)
        for i, hop in enumerate(hops)
        for k in range(4)
    ]
    copies = []
    for n, (_, _, hop, k) in enumerate(parts):
        row = pl.multiple_of((chip_at(place, -k, -hop) * 2 + place[0]) * 512, 512)
        for side, weight in enumerate((own_weight, other_weight)):
            copies.append(
                pltpu.make_async_copy(
                    weight.at[pl.ds(row, 512), :], tiles.at[n, side], sems.at[n, side]
                )
            )
    for copy in copies:
        copy.start()
    totals = [jnp.zeros(own_out.shape, F32)] * 2
    for n, (g, at, _, _) in enumerate(parts):
        for side in range(2):
            copies[2 * n + side].wait()
            totals[side] += jnp.dot(
                rows_refs[g][:, at * 512 : at * 512 + 512],
                tiles[n, side],
                preferred_element_type=F32,
            )
    own_out[...] = totals[0]
    other_out[...] = totals[1]


def project(groups, place, rows, own_weight, other_weight):
    still = pl.BlockSpec((128, 256), lambda i, p: (0, 0))
    return pl.pallas_call(
        functools.partial(query_kernel, groups),
        grid_spec=pltpu.PrefetchScalarGridSpec(
            num_scalar_prefetch=1,
            grid=(1,),
            in_specs=[pl.BlockSpec(part.shape, lambda i, p: (0, 0)) for part in rows]
            + [pl.BlockSpec(memory_space=pltpu.HBM)] * 2,
            out_specs=[still, still],
            scratch_shapes=[
                pltpu.VMEM((CHIPS, 2, 512, 256), BF16),
                pltpu.SemaphoreType.DMA((CHIPS, 2)),
            ],
        ),
        out_shape=[jax.ShapeDtypeStruct((128, 256), F32)] * 2,
        compiler_params=params(20),
        cost_estimate=pl.CostEstimate(
            flops=2 * 128 * 8192 * 512, bytes_accessed=40 << 20, transcendentals=0
        ),
        name="query",
    )(place, *rows, own_weight, other_weight)


def attend_kernel(
    head_ref, length_ref, own_ref, recv_ref, kv_ref, kv_recv, cos_t, sin_t, cos_q, sin_q, mask_ref, cache_ref, out_ref
):
    score_scale = F32(1.0 / math.sqrt(HD))
    keys, values = [], []
    upper = lax.broadcasted_iota(jnp.int32, (8, 128), 0) < 4
    for chip in range(CHIPS):
        first = kv_ref[chip, 0:8] + kv_recv[chip, 0:8]
        second = kv_ref[chip, 8:16] + kv_recv[chip, 8:16]
        keys.append(jnp.where(upper, first, pltpu.roll(second, 4, 0)))
        values.append(jnp.where(upper, pltpu.roll(first, 4, 0), second))
    keys = jnp.concatenate(keys, 0).astype(BF16).astype(F32)
    values = jnp.concatenate(values, 0).astype(BF16)
    low, high = keys[:64], keys[64:]
    keys = jnp.concatenate(
        [low * cos_t[...] - high * sin_t[...], high * cos_t[...] + low * sin_t[...]], 0
    ).astype(BF16)
    heads = []
    for h in range(2):
        q = own_ref[:, h * 128 : h * 128 + 128] + recv_ref[:, h * 128 : h * 128 + 128]
        q = q * cos_q[...] + pltpu.roll(q, 64, 1) * sin_q[...]
        heads.append(q.astype(BF16))
    fresh = [
        jnp.dot(q, keys, preferred_element_type=F32) * score_scale for q in heads
    ]
    lane = lax.broadcasted_iota(jnp.int32, (32, 128), 1)
    for r in range(8):
        rows = slice(r * 16, r * 16 + 16)
        q = jnp.concatenate([heads[0][rows], heads[1][rows]], 0)
        old = (
            lax.dot_general(q, cache_ref[r, 0, 0], NT, preferred_element_type=F32) * score_scale
        )
        new = jnp.concatenate([fresh[0][rows], fresh[1][rows]], 0)
        mask = jnp.concatenate([mask_ref[rows, :]] * 2, 0)
        old = jnp.where(lane < length_ref[r], old, -jnp.inf)
        new = jnp.where(mask > 0.5, new, -jnp.inf)
        peak = jnp.maximum(
            jnp.max(old, -1, keepdims=True), jnp.max(new, -1, keepdims=True)
        )
        old = jnp.exp(old - peak)
        new = jnp.exp(new - peak)
        total = jnp.sum(old, -1, keepdims=True) + jnp.sum(new, -1, keepdims=True)
        old = (old / total).astype(BF16)
        new = (new / total).astype(BF16)
        mixed = jnp.dot(old, cache_ref[r, 0, 1], preferred_element_type=F32)
        mixed = mixed + lax.dot_general(new, values, NT, preferred_element_type=F32)
        mixed = mixed.astype(BF16)
        out_ref[rows, 0:128] = mixed[:16]
        out_ref[rows, 128:256] = mixed[16:]


def attend(head, lengths, own, recv, kv, kv_recv, cos_t, sin_t, cos_q, sin_q, mask, cache):
    def whole(array):
        return pl.BlockSpec(array.shape, lambda i, h, n: (0,) * array.ndim)

    arrays = (own, recv, kv, kv_recv, cos_t, sin_t, cos_q, sin_q, mask)
    return pl.pallas_call(
        attend_kernel,
        grid_spec=pltpu.PrefetchScalarGridSpec(
            num_scalar_prefetch=2,
            grid=(1,),
            in_specs=[whole(a) for a in arrays]
            + [pl.BlockSpec((8, 1, 2, 128, 128), lambda i, h, n: (0, h[0], 0, 0, 0))],
            out_specs=pl.BlockSpec((128, 256), lambda i, h, n: (0, 0)),
        ),
        out_shape=jax.ShapeDtypeStruct((128, 256), BF16),
        compiler_params=params(6),
        cost_estimate=pl.CostEstimate(
            flops=2 * 256 * 128 * 512, bytes_accessed=2 << 20, transcendentals=65536
        ),
        name="attend",
    )(head, lengths, *arrays, cache)


def partial_kernel(hops, place, mine, theirs, own_weight, other_weight, rotation_ref, *refs):
    outs, (tiles, sems) = refs[: len(hops)], refs[len(hops) :]
    unit = F32(1.0 / math.sqrt(RB))
    parts = [(out, at) for at in range(4) for out in range(len(hops))]
    copies = []
    for i, (out, at) in enumerate(parts):
        column = pl.multiple_of((chip_at(place, hops[out], at) * 2 + place[0]) * 512, 512)
        for side, weight in enumerate((own_weight, other_weight)):
            copies.append(
                pltpu.make_async_copy(
                    weight.at[:, pl.ds(column, 512)], tiles.at[i, side], sems.at[i, side]
                )
            )
    for copy in copies:
        copy.start()
    for i, (out, at) in enumerate(parts):
        copies[2 * i].wait()
        copies[2 * i + 1].wait()
        groups = (
            jnp.dot(mine[...], tiles[i, 0], preferred_element_type=F32),
            jnp.dot(theirs[...], tiles[i, 1], preferred_element_type=F32),
        )
        for b in range(4):
            halves = []
            for group in groups:
                block = group[:, b * 128 : b * 128 + 128]
                coarse = block.astype(BF16)
                fine = (block - coarse.astype(F32)).astype(BF16)
                halves.append(jnp.concatenate([coarse, fine], 1))
            both = lax.dot_general(
                rotation_ref[...],
                jnp.concatenate(halves, 0),
                NT,
                preferred_element_type=F32,
            )
            total = None
            for turned in (both[:, :128], both[:, 128:]):
                scale = jnp.max(jnp.abs(turned), 0, keepdims=True) * unit + TINY
                codes = (turned * (unit / scale)).astype(BF16)
                term = codes.astype(F32) * scale
                total = term if total is None else total + term
            outs[out][at, b * 128 : b * 128 + 128, :] = total.astype(outs[out].dtype)


def partials(hops, place, mine, theirs, own_weight, other_weight, rotation):
    count = 4 * len(hops)
    still = pl.BlockSpec((128, 256), lambda i, p: (0, 0))
    return pl.pallas_call(
        functools.partial(partial_kernel, hops),
        grid_spec=pltpu.PrefetchScalarGridSpec(
            num_scalar_prefetch=1,
            grid=(1,),
            in_specs=[still, still]
            + [pl.BlockSpec(memory_space=pltpu.HBM)] * 2
            + [still],
            out_specs=[pl.BlockSpec((4, 512, 128), lambda i, p: (0, 0, 0)) for _ in hops],
            scratch_shapes=[
                pltpu.VMEM((count, 2, 256, 512), BF16),
                pltpu.SemaphoreType.DMA((count, 2)),
            ],
        ),
        out_shape=[
            jax.ShapeDtypeStruct((4, 512, 128), BF16 if hop else F32) for hop in hops
        ],
        compiler_params=params(6 + 4 * len(hops)),
        cost_estimate=pl.CostEstimate(
            flops=2 * 128 * 2048 * 1024 * len(hops),
            bytes_accessed=len(hops) * 3 << 20,
            transcendentals=0,
        ),
        name="partials",
    )(place, mine, theirs, own_weight, other_weight, rotation)


def on_device(
    in_codes, in_scales, query_weight, kv_weight, out_weight, kv_cache, prefix_len, draft_parent
):
    rank = lax.axis_index(TENSOR)
    core = rank % 2
    head = rank // 8
    along_x = rank // 2 % 4
    place = jnp.stack(
        [core, jnp.where(core == 0, along_x, head), jnp.where(core == 0, head, along_x)]
    )
    signs = hadamard()
    scales = in_scales[0]

    near = jnp.stack([in_codes] + [first_shift(in_codes, k) for k in (1, 2, 3)])
    wq = in_hbm(query_weight[0])
    wq_other = in_hbm(traded(query_weight)[0])
    kv_other = traded(kv_weight)

    near, draft_parent, kv_weight, kv_other, out_weight = lax.optimization_barrier(
        (near, draft_parent, kv_weight, kv_other, out_weight)
    )

    far = {k: second_shift(near, k) for k in (1, 3, 2)}

    def as_rows(weight):
        return weight[0].transpose(2, 1, 3, 0).reshape(32, -1)

    wkv, wkv_other = as_rows(kv_weight), as_rows(kv_other)
    wo = in_hbm(out_weight[0])
    wo_other = in_hbm(traded(out_weight)[0])

    ancestry = ancestor_table(draft_parent)
    position = prefix_len.astype(F32)[:, None] + (jnp.sum(ancestry, -1) - 1.0)
    frequency = jnp.power(ROPE_BASE, -(jnp.arange(64, dtype=F32) / 64))
    angles = position.reshape(128, 1) * frequency
    cosine, sine = jnp.cos(angles), jnp.sin(angles)
    cos_q = jnp.concatenate([cosine, cosine], 1)
    sin_q = jnp.concatenate([-sine, sine], 1)
    block = jnp.eye(8, dtype=F32)
    mask = (ancestry[:, :, None, :] * block[:, None, :, None]).reshape(128, 128)

    blocks = np.kron(np.eye(2, dtype=np.float32), signs)
    rotation = jnp.asarray(blocks, BF16)

    cos_t, sin_t = cosine.T, sine.T
    near_rows, kv_part = decode(
        (0,), 1, place, scales, (near,), rotation, wkv, wkv_other, jnp.zeros((4, 1, 16, 128), F32)
    )
    hops = (1, 3, 2)
    far_rows, kv_part = decode(
        hops,
        4,
        place,
        scales,
        tuple(far[k] for k in hops),
        rotation,
        wkv,
        wkv_other,
        kv_part,
        (mask, cos_q, sin_q, cos_t, sin_t, wq_other),
    )
    kv = exchanged(kv_part.reshape(CHIPS, 16, 128))
    own, other = project(
        ((0,), hops), place, (in_hbm(near_rows), in_hbm(far_rows)), wq, wq_other
    )
    other, kv = lax.optimization_barrier((other, kv))
    recv = traded(other)
    kv_recv = traded(kv)
    attended = attend(
        head.reshape(1), prefix_len, own, recv, kv, kv_recv, cos_t, sin_t, cos_q, sin_q, mask, kv_cache
    )
    theirs = traded(attended)
    twice = jnp.asarray(np.concatenate([signs, signs], 1), BF16)
    sent = {}
    for hops in ((2,), (1, 3), (0,)):
        for hop, piece in zip(hops, partials(hops, place, attended, theirs, wo, wo_other, twice)):
            sent[hop] = piece
    sums = sent[0]
    for k in (2, 1, 3):
        sums = sums + first_shift(sent[k], k).astype(F32)
    summed = sums[0]
    for k in (2, 1, 3):
        summed = summed + second_shift(sums[k].astype(BF16), k).astype(F32)

    here = lax.dynamic_slice_in_dim(scales, rank * 4, 4)
    turned_in = in_codes.T.astype(F32) * jnp.repeat(here, RB)[:, None]
    turned = summed + turned_in
    peak = jnp.max(jnp.abs(turned.reshape(4, RB, 128)), (1, 2))
    next_peak = swapped(peak, "section")
    next_rows = swapped(turned, "section")
    spread = lax.dynamic_update_slice_in_dim(jnp.zeros((128,), F32), next_peak, rank * 4, 0)
    everyone = lax.all_to_all(
        jnp.broadcast_to(spread[None, None], (64, 8, 128)), ("dp", TENSOR), 0, 0, tiled=True
    )
    next_scales = jnp.max(everyone, (0, 1)) + TINY
    scale_here = lax.dynamic_slice_in_dim(next_scales, rank * 4, 4)
    next_codes = (next_rows.T / jnp.repeat(scale_here, RB)[None, :]).astype(BF16)
    return (next_codes, next_scales[None])


def solution(mesh):
    rows = ("section", "dp")
    placed = (
        P(rows, TENSOR),
        P("section", None),
        P("section", None, TENSOR),
        P("section", None, None, None, TENSOR),
        P("section", TENSOR, None),
        P(rows, None, None, None, None),
        P(rows),
        P(rows, None),
    )
    return jax.shard_map(
        on_device,
        mesh=mesh,
        in_specs=placed,
        out_specs=(P(rows, TENSOR), P("section", None)),
        check_vma=False,
    )
```

```python
import functools
import math

import jax
import jax.numpy as jnp
import numpy as np
from jax import lax
from jax.experimental import pallas as pl
from jax.experimental.pallas import tpu as pltpu
from jax.sharding import PartitionSpec as P

HD = 128
RB = 128
CHIPS = 16
ROPE_BASE = 500000.0
TINY = 1e-06
TENSOR = "tensor"


def device(y, x, core):
    return (y * 4 + x) * 2 + core


F32 = jnp.float32
BF16 = jnp.bfloat16
NT = (((1,), (1,)), ((), ()))
LIGHT = pl.CostEstimate(flops=1024, bytes_accessed=1024, transcendentals=0)


def hadamard():
    index = np.arange(RB)
    common = index[:, None] & index[None, :]
    parity = np.zeros((RB, RB), np.int32)
    for place in range(7):
        parity = parity + (common >> place & 1)
    return np.where(parity % 2 == 0, 1.0, -1.0).astype(np.float32)


def ancestor_table(draft_parent):
    count, size = draft_parent.shape
    target = lax.broadcasted_iota(jnp.int32, (count, size, size), 2)
    source = lax.broadcasted_iota(jnp.int32, (count, size, size), 1)
    table = ((target == draft_parent[:, :, None]) | (target == source)).astype(F32)
    for _ in range(4):
        table = jnp.minimum(jnp.einsum("rij,rjk->rik", table, table), 1.0)
    return table


def swapped(block, axis):
    return lax.ppermute(block, axis, [(0, 1), (1, 0)])


def traded(block):
    return lax.ppermute(block, TENSOR, [(i, i ^ 1) for i in range(32)])


def exchanged(pieces):
    groups = [[chip * 2 + core for chip in range(CHIPS)] for core in range(2)]
    return lax.all_to_all(pieces, TENSOR, 0, 0, tiled=True, axis_index_groups=groups)


def shifted(block, by, second):
    pairs = []
    for y in range(4):
        for x in range(4):
            for core in range(2):
                along_y = (core == 1) != second
                to_y, to_x = ((y + by) % 4, x) if along_y else (y, (x + by) % 4)
                pairs.append((device(y, x, core), device(to_y, to_x, core)))
    return lax.ppermute(block, TENSOR, pairs)


def first_shift(block, by):
    return shifted(block, by, False)


def second_shift(block, by):
    return shifted(block, by, True)


def chip_at(place, first, second):
    first = lax.rem(place[1] + 4 + first, 4)
    second = lax.rem(place[2] + 4 + second, 4)
    return jnp.where(place[0] == 0, second * 4 + first, first * 4 + second)


def in_hbm(array):
    return pltpu.with_memory_space_constraint(array, pltpu.HBM)


def params(mebibytes):
    return pltpu.CompilerParams(vmem_limit_bytes=mebibytes << 20)


def decode_kernel(hops, waits, place, scale_ref, *refs):
    codes_refs, refs = refs[: len(hops)], refs[len(hops) :]
    rotation_ref, own_weight, other_weight, kv_in = refs[:4]
    rows_ref, kv_out = refs[4 + waits :]
    own = other = None
    for i, hop in enumerate(hops):
        own_tiles, other_tiles = [], []
        for k in range(4):
            tile = chip_at(place, -k, -hop) * 2 + place[0]
            for half in range(2):
                product = jnp.dot(
                    codes_refs[i][k, :, half * 256 : half * 256 + 256],
                    rotation_ref[...],
                    preferred_element_type=F32,
                )
                for b in range(2):
                    factor = scale_ref[tile * 4 + half * 2 + b] * F32(1.0 / math.sqrt(RB))
                    at = i * 2048 + k * 512 + half * 256 + b * 128
                    rows_ref[:, at : at + 128] = (
                        product[:, b * 128 : b * 128 + 128] * factor
                    ).astype(BF16)
            column = pl.ds(pl.multiple_of(tile * 512, 512), 512)
            own_tiles.append(own_weight[:, column])
            other_tiles.append(other_weight[:, column])
        weight = jnp.concatenate(
            [jnp.concatenate(own_tiles, 1), jnp.concatenate(other_tiles, 1)], 0
        )
        total = lax.dot_general(
            weight,
            rows_ref[:, i * 2048 : i * 2048 + 2048],
            NT,
            preferred_element_type=F32,
        )
        own = total[:32] if own is None else own + total[:32]
        other = total[32:] if other is None else other + total[32:]
    for h in range(4):
        mine, theirs = own[h * 8 : h * 8 + 8], other[h * 8 : h * 8 + 8]
        value = kv_in[h, 0] + jnp.concatenate(
            [jnp.where(place[0] == 0, mine, theirs), jnp.where(place[0] == 0, theirs, mine)], 0
        )
        for i in range(kv_out.shape[1]):
            kv_out[h, i] = value


def decode(hops, copies, place, scales, codes, rotation, own_weight, other_weight, kv_in, after=()):
    def whole(array):
        return pl.BlockSpec(array.shape, lambda i, p, s: (0,) * array.ndim)

    arrays = (*codes, rotation, own_weight, other_weight, kv_in)
    outs = [(128, 2048 * len(hops)), (4, copies, 16, 128)]
    return pl.pallas_call(
        functools.partial(decode_kernel, hops, len(after)),
        grid_spec=pltpu.PrefetchScalarGridSpec(
            num_scalar_prefetch=2,
            grid=(1,),
            in_specs=[
                *(whole(array) for array in arrays),
                *(pl.BlockSpec(memory_space=pl.ANY) for _ in after),
            ],
            out_specs=[
                pl.BlockSpec(outs[0], lambda i, p, s: (0, 0)),
                pl.BlockSpec(outs[1], lambda i, p, s: (0, 0, 0, 0)),
            ],
        ),
        out_shape=[
            pltpu.HBM(outs[0], BF16),
            (pltpu.HBM if copies > 1 else jax.ShapeDtypeStruct)(outs[1], F32),
        ],
        compiler_params=params(16),
        cost_estimate=LIGHT,
        name="decode",
    )(place, scales, *arrays, *after)


def query_kernel(groups, place, *refs):
    rows_refs, refs = refs[: len(groups)], refs[len(groups) :]
    own_weight, other_weight, own_out, other_out, tiles, sems = refs
    parts = [
        (g, i * 4 + k, hop, k)
        for g, hops in enumerate(groups)
        for i, hop in enumerate(hops)
        for k in range(4)
    ]
    copies = []
    for n, (_, _, hop, k) in enumerate(parts):
        row = pl.multiple_of((chip_at(place, -k, -hop) * 2 + place[0]) * 512, 512)
        for side, weight in enumerate((own_weight, other_weight)):
            copies.append(
                pltpu.make_async_copy(
                    weight.at[pl.ds(row, 512), :], tiles.at[n, side], sems.at[n, side]
                )
            )
    for copy in copies:
        copy.start()
    totals = [jnp.zeros(own_out.shape, F32)] * 2
    for n, (g, at, _, _) in enumerate(parts):
        for side in range(2):
            copies[2 * n + side].wait()
            totals[side] += jnp.dot(
                rows_refs[g][:, at * 512 : at * 512 + 512],
                tiles[n, side],
                preferred_element_type=F32,
            )
    own_out[...] = totals[0]
    other_out[...] = totals[1]


def project(groups, place, rows, own_weight, other_weight):
    still = pl.BlockSpec((128, 256), lambda i, p: (0, 0))
    return pl.pallas_call(
        functools.partial(query_kernel, groups),
        grid_spec=pltpu.PrefetchScalarGridSpec(
            num_scalar_prefetch=1,
            grid=(1,),
            in_specs=[pl.BlockSpec(part.shape, lambda i, p: (0, 0)) for part in rows]
            + [pl.BlockSpec(memory_space=pltpu.HBM)] * 2,
            out_specs=[still, still],
            scratch_shapes=[
                pltpu.VMEM((CHIPS, 2, 512, 256), BF16),
                pltpu.SemaphoreType.DMA((CHIPS, 2)),
            ],
        ),
        out_shape=[jax.ShapeDtypeStruct((128, 256), F32)] * 2,
        compiler_params=params(20),
        cost_estimate=pl.CostEstimate(
            flops=2 * 128 * 8192 * 512, bytes_accessed=40 << 20, transcendentals=0
        ),
        name="query",
    )(place, *rows, own_weight, other_weight)


def tile_copies(hops, place, own_weight, other_weight, tiles, sems):
    copies = []
    for i, (at, hop) in enumerate((at, hop) for at in range(4) for hop in hops):
        column = pl.multiple_of((chip_at(place, hop, at) * 2 + place[0]) * 512, 512)
        for side, weight in enumerate((own_weight, other_weight)):
            copies.append(
                pltpu.make_async_copy(
                    weight.at[:, pl.ds(column, 512)], tiles.at[i, side], sems.at[i, side]
                )
            )
    return copies


def tiles_of(hops):
    return pltpu.VMEM((4 * len(hops), 2, 256, 512), BF16)


def attend_kernel(
    hops,
    place,
    head_ref, length_ref, own_ref, recv_ref, kv_ref, kv_recv, cos_t, sin_t, cos_q, sin_q, mask_ref, cache_ref,
    own_weight, other_weight, out_ref, tiles, sems
):
    copies = tile_copies(hops, place, own_weight, other_weight, tiles, sems)
    for copy in copies:
        copy.start()
    score_scale = F32(1.0 / math.sqrt(HD))
    keys, values = [], []
    upper = lax.broadcasted_iota(jnp.int32, (8, 128), 0) < 4
    for chip in range(CHIPS):
        first = kv_ref[chip, 0:8] + kv_recv[chip, 0:8]
        second = kv_ref[chip, 8:16] + kv_recv[chip, 8:16]
        keys.append(jnp.where(upper, first, pltpu.roll(second, 4, 0)))
        values.append(jnp.where(upper, pltpu.roll(first, 4, 0), second))
    keys = jnp.concatenate(keys, 0).astype(BF16).astype(F32)
    values = jnp.concatenate(values, 0).astype(BF16)
    low, high = keys[:64], keys[64:]
    keys = jnp.concatenate(
        [low * cos_t[...] - high * sin_t[...], high * cos_t[...] + low * sin_t[...]], 0
    ).astype(BF16)
    heads = []
    for h in range(2):
        q = own_ref[:, h * 128 : h * 128 + 128] + recv_ref[:, h * 128 : h * 128 + 128]
        q = q * cos_q[...] + pltpu.roll(q, 64, 1) * sin_q[...]
        heads.append(q.astype(BF16))
    fresh = [
        jnp.dot(q, keys, preferred_element_type=F32) * score_scale for q in heads
    ]
    lane = lax.broadcasted_iota(jnp.int32, (32, 128), 1)
    for r in range(8):
        rows = slice(r * 16, r * 16 + 16)
        q = jnp.concatenate([heads[0][rows], heads[1][rows]], 0)
        old = (
            lax.dot_general(q, cache_ref[r, 0, 0], NT, preferred_element_type=F32) * score_scale
        )
        new = jnp.concatenate([fresh[0][rows], fresh[1][rows]], 0)
        mask = jnp.concatenate([mask_ref[rows, :]] * 2, 0)
        old = jnp.where(lane < length_ref[r], old, -jnp.inf)
        new = jnp.where(mask > 0.5, new, -jnp.inf)
        peak = jnp.maximum(
            jnp.max(old, -1, keepdims=True), jnp.max(new, -1, keepdims=True)
        )
        old = jnp.exp(old - peak)
        new = jnp.exp(new - peak)
        total = jnp.sum(old, -1, keepdims=True) + jnp.sum(new, -1, keepdims=True)
        old = (old / total).astype(BF16)
        new = (new / total).astype(BF16)
        mixed = jnp.dot(old, cache_ref[r, 0, 1], preferred_element_type=F32)
        mixed = mixed + lax.dot_general(new, values, NT, preferred_element_type=F32)
        mixed = mixed.astype(BF16)
        out_ref[rows, 0:128] = mixed[:16]
        out_ref[rows, 128:256] = mixed[16:]
    for copy in copies:
        copy.wait()


def attend(hops, place, head, lengths, arrays, cache, own_weight, other_weight):
    def whole(array):
        return pl.BlockSpec(array.shape, lambda i, p, h, n: (0,) * array.ndim)

    return pl.pallas_call(
        functools.partial(attend_kernel, hops),
        grid_spec=pltpu.PrefetchScalarGridSpec(
            num_scalar_prefetch=3,
            grid=(1,),
            in_specs=[whole(a) for a in arrays]
            + [pl.BlockSpec((8, 1, 2, 128, 128), lambda i, p, h, n: (0, h[0], 0, 0, 0))]
            + [pl.BlockSpec(memory_space=pltpu.HBM)] * 2,
            out_specs=[
                pl.BlockSpec((128, 256), lambda i, p, h, n: (0, 0)),
                pl.BlockSpec(memory_space=pl.ANY),
            ],
            scratch_shapes=[pltpu.SemaphoreType.DMA((4 * len(hops), 2))],
        ),
        out_shape=[jax.ShapeDtypeStruct((128, 256), BF16), tiles_of(hops)],
        compiler_params=params(6),
        cost_estimate=pl.CostEstimate(
            flops=2 * 256 * 128 * 512, bytes_accessed=2 << 20, transcendentals=65536
        ),
        name="attend",
    )(place, head, lengths, *arrays, cache, own_weight, other_weight)


def partial_kernel(
    hops, later, place, mine, theirs, tiles, own_weight, other_weight, rotation_ref, *refs
):
    outs, refs = refs[: len(hops)], refs[len(hops) :]
    copies = tile_copies(later, place, own_weight, other_weight, *refs) if later else []
    for copy in copies:
        copy.start()
    unit = F32(1.0 / math.sqrt(RB))
    for i, (at, out) in enumerate((at, out) for at in range(4) for out in range(len(hops))):
        groups = (
            jnp.dot(mine[...], tiles[i, 0], preferred_element_type=F32),
            jnp.dot(theirs[...], tiles[i, 1], preferred_element_type=F32),
        )
        for b in range(4):
            halves = []
            for group in groups:
                block = group[:, b * 128 : b * 128 + 128]
                coarse = block.astype(BF16)
                fine = (block - coarse.astype(F32)).astype(BF16)
                halves.append(jnp.concatenate([coarse, fine], 1))
            both = lax.dot_general(
                rotation_ref[...],
                jnp.concatenate(halves, 0),
                NT,
                preferred_element_type=F32,
            )
            total = None
            for turned in (both[:, :128], both[:, 128:]):
                scale = jnp.max(jnp.abs(turned), 0, keepdims=True) * unit + TINY
                codes = (turned * (unit / scale)).astype(BF16)
                term = codes.astype(F32) * scale
                total = term if total is None else total + term
            outs[out][at, b * 128 : b * 128 + 128, :] = total.astype(outs[out].dtype)


    for copy in copies:
        copy.wait()


def partials(hops, later, place, mine, theirs, tiles, own_weight, other_weight, rotation):
    still = pl.BlockSpec((128, 256), lambda i, p: (0, 0))
    out_specs = [pl.BlockSpec((4, 512, 128), lambda i, p: (0, 0, 0)) for _ in hops]
    out_shape = [jax.ShapeDtypeStruct((4, 512, 128), BF16 if hop else F32) for hop in hops]
    scratch = []
    if later:
        out_specs.append(pl.BlockSpec(memory_space=pl.ANY))
        out_shape.append(tiles_of(later))
        scratch.append(pltpu.SemaphoreType.DMA((4 * len(later), 2)))
    return pl.pallas_call(
        functools.partial(partial_kernel, hops, later),
        grid_spec=pltpu.PrefetchScalarGridSpec(
            num_scalar_prefetch=1,
            grid=(1,),
            in_specs=[still, still, pl.BlockSpec(tiles.shape, lambda i, p: (0, 0, 0, 0))]
            + [pl.BlockSpec(memory_space=pltpu.HBM)] * 2
            + [still],
            out_specs=out_specs,
            scratch_shapes=scratch,
        ),
        out_shape=out_shape,
        compiler_params=params(8 + 6 * len(hops)),
        cost_estimate=pl.CostEstimate(
            flops=2 * 128 * 2048 * 1024 * len(hops),
            bytes_accessed=len(hops) * 3 << 20,
            transcendentals=0,
        ),
        name="partials",
    )(place, mine, theirs, tiles, own_weight, other_weight, rotation)


def on_device(
    in_codes, in_scales, query_weight, kv_weight, out_weight, kv_cache, prefix_len, draft_parent
):
    rank = lax.axis_index(TENSOR)
    core = rank % 2
    head = rank // 8
    along_x = rank // 2 % 4
    place = jnp.stack(
        [core, jnp.where(core == 0, along_x, head), jnp.where(core == 0, head, along_x)]
    )
    signs = hadamard()
    scales = in_scales[0]

    near = jnp.stack([in_codes] + [first_shift(in_codes, k) for k in (1, 2, 3)])
    wq = in_hbm(query_weight[0])
    wq_other = in_hbm(traded(query_weight)[0])
    kv_other = traded(kv_weight)

    near, draft_parent, kv_weight, kv_other, out_weight = lax.optimization_barrier(
        (near, draft_parent, kv_weight, kv_other, out_weight)
    )

    far = {k: second_shift(near, k) for k in (1, 3, 2)}

    def as_rows(weight):
        return weight[0].transpose(2, 1, 3, 0).reshape(32, -1)

    wkv, wkv_other = as_rows(kv_weight), as_rows(kv_other)
    wo = in_hbm(out_weight[0])
    wo_other = in_hbm(traded(out_weight)[0])

    blocks = np.kron(np.eye(2, dtype=np.float32), signs)
    rotation = jnp.asarray(blocks, BF16)

    near_rows, kv_part = decode(
        (0,), 1, place, scales, (near,), rotation, wkv, wkv_other, jnp.zeros((4, 1, 16, 128), F32)
    )
    lengths, kv_part = lax.optimization_barrier((prefix_len, kv_part))

    ancestry = ancestor_table(draft_parent)
    position = lengths.astype(F32)[:, None] + (jnp.sum(ancestry, -1) - 1.0)
    frequency = jnp.power(ROPE_BASE, -(jnp.arange(64, dtype=F32) / 64))
    angles = position.reshape(128, 1) * frequency
    cosine, sine = jnp.cos(angles), jnp.sin(angles)
    cos_q = jnp.concatenate([cosine, cosine], 1)
    sin_q = jnp.concatenate([-sine, sine], 1)
    block = jnp.eye(8, dtype=F32)
    mask = (ancestry[:, :, None, :] * block[:, None, :, None]).reshape(128, 128)

    cos_t, sin_t = cosine.T, sine.T
    hops = (1, 3, 2)
    far_rows, kv_part = decode(
        hops,
        4,
        place,
        scales,
        tuple(far[k] for k in hops),
        rotation,
        wkv,
        wkv_other,
        kv_part,
        (mask, cos_q, sin_q, cos_t, sin_t, wq_other),
    )
    kv = exchanged(kv_part.reshape(CHIPS, 16, 128))
    own, other = project(
        ((0,), hops), place, (in_hbm(near_rows), in_hbm(far_rows)), wq, wq_other
    )
    other, kv = lax.optimization_barrier((other, kv))
    recv = traded(other)
    kv_recv = traded(kv)
    calls = ((2,), (1, 3), (0,))
    attended, tiles = attend(
        calls[0],
        place,
        head.reshape(1),
        prefix_len,
        (own, recv, kv, kv_recv, cos_t, sin_t, cos_q, sin_q, mask),
        kv_cache,
        wo,
        wo_other,
    )
    theirs = traded(attended)
    twice = jnp.asarray(np.concatenate([signs, signs], 1), BF16)
    sent = {}
    for hops, later in zip(calls, calls[1:] + (None,)):
        pieces = partials(hops, later, place, attended, theirs, tiles, wo, wo_other, twice)
        tiles = pieces[-1]
        for hop, piece in zip(hops, pieces):
            sent[hop] = piece
    sums = sent[0]
    for k in (2, 1, 3):
        sums = sums + first_shift(sent[k], k).astype(F32)
    summed = sums[0]
    for k in (2, 1, 3):
        summed = summed + second_shift(sums[k].astype(BF16), k).astype(F32)

    here = lax.dynamic_slice_in_dim(scales, rank * 4, 4)
    turned_in = in_codes.T.astype(F32) * jnp.repeat(here, RB)[:, None]
    turned = summed + turned_in
    peak = jnp.max(jnp.abs(turned.reshape(4, RB, 128)), (1, 2))
    next_rows = swapped(turned, "section")
    everyone = lax.all_to_all(
        jnp.broadcast_to(peak[None], (128, 4)), ("section", "dp", TENSOR), 0, 0, tiled=True
    )
    from_there = lax.dynamic_index_in_dim(
        everyone.reshape(2, 2, 128), 1 - lax.axis_index("section"), 0, keepdims=False
    )
    next_scales = jnp.max(from_there, 0) + TINY
    scale_here = lax.dynamic_slice_in_dim(next_scales, rank * 4, 4)
    next_codes = (next_rows.T / jnp.repeat(scale_here, RB)[None, :]).astype(BF16)
    return (next_codes, next_scales[None])


def solution(mesh):
    rows = ("section", "dp")
    placed = (
        P(rows, TENSOR),
        P("section", None),
        P("section", None, TENSOR),
        P("section", None, None, None, TENSOR),
        P("section", TENSOR, None),
        P(rows, None, None, None, None),
        P(rows),
        P(rows, None),
    )
    return jax.shard_map(
        on_device,
        mesh=mesh,
        in_specs=placed,
        out_specs=(P(rows, TENSOR), P("section", None)),
        check_vma=False,
    )
```

```python
import functools
import math

import jax
import jax.numpy as jnp
import numpy as np
from jax import lax
from jax.experimental import pallas as pl
from jax.experimental.pallas import tpu as pltpu
from jax.sharding import PartitionSpec as P

HD = 128
RB = 128
CHIPS = 16
ROPE_BASE = 500000.0
TINY = 1e-06
TENSOR = "tensor"


def device(y, x, core):
    return (y * 4 + x) * 2 + core


F32 = jnp.float32
BF16 = jnp.bfloat16
NT = (((1,), (1,)), ((), ()))
LIGHT = pl.CostEstimate(flops=1024, bytes_accessed=1024, transcendentals=0)


def hadamard():
    index = np.arange(RB)
    common = index[:, None] & index[None, :]
    parity = np.zeros((RB, RB), np.int32)
    for place in range(7):
        parity = parity + (common >> place & 1)
    return np.where(parity % 2 == 0, 1.0, -1.0).astype(np.float32)


def ancestor_table(draft_parent):
    count, size = draft_parent.shape
    target = lax.broadcasted_iota(jnp.int32, (count, size, size), 2)
    source = lax.broadcasted_iota(jnp.int32, (count, size, size), 1)
    table = ((target == draft_parent[:, :, None]) | (target == source)).astype(F32)
    for _ in range(4):
        table = jnp.minimum(jnp.einsum("rij,rjk->rik", table, table), 1.0)
    return table


def swapped(block, axis):
    return lax.ppermute(block, axis, [(0, 1), (1, 0)])


def traded(block):
    return lax.ppermute(block, TENSOR, [(i, i ^ 1) for i in range(32)])


def exchanged(pieces):
    groups = [[chip * 2 + core for chip in range(CHIPS)] for core in range(2)]
    return lax.all_to_all(pieces, TENSOR, 0, 0, tiled=True, axis_index_groups=groups)


def shifted(block, by, second):
    pairs = []
    for y in range(4):
        for x in range(4):
            for core in range(2):
                along_y = (core == 1) != second
                to_y, to_x = ((y + by) % 4, x) if along_y else (y, (x + by) % 4)
                pairs.append((device(y, x, core), device(to_y, to_x, core)))
    return lax.ppermute(block, TENSOR, pairs)


def first_shift(block, by):
    return shifted(block, by, False)


def second_shift(block, by):
    return shifted(block, by, True)


def chip_at(place, first, second):
    first = lax.rem(place[1] + 4 + first, 4)
    second = lax.rem(place[2] + 4 + second, 4)
    return jnp.where(place[0] == 0, second * 4 + first, first * 4 + second)


def in_hbm(array):
    return pltpu.with_memory_space_constraint(array, pltpu.HBM)


def params(mebibytes):
    return pltpu.CompilerParams(vmem_limit_bytes=mebibytes << 20)


def decode_kernel(hops, waits, place, scale_ref, *refs):
    codes_refs, refs = refs[: len(hops)], refs[len(hops) :]
    rotation_ref, own_weight, other_weight, kv_in = refs[:4]
    rows_ref, kv_out = refs[4 + waits :]
    own = other = None
    for i, hop in enumerate(hops):
        own_tiles, other_tiles = [], []
        for k in range(4):
            tile = chip_at(place, -k, -hop) * 2 + place[0]
            for half in range(2):
                product = jnp.dot(
                    codes_refs[i][k, :, half * 256 : half * 256 + 256],
                    rotation_ref[...],
                    preferred_element_type=F32,
                )
                for b in range(2):
                    factor = scale_ref[tile * 4 + half * 2 + b] * F32(1.0 / math.sqrt(RB))
                    at = i * 2048 + k * 512 + half * 256 + b * 128
                    rows_ref[:, at : at + 128] = (
                        product[:, b * 128 : b * 128 + 128] * factor
                    ).astype(BF16)
            column = pl.ds(pl.multiple_of(tile * 512, 512), 512)
            own_tiles.append(own_weight[:, column])
            other_tiles.append(other_weight[:, column])
        weight = jnp.concatenate(
            [jnp.concatenate(own_tiles, 1), jnp.concatenate(other_tiles, 1)], 0
        )
        total = lax.dot_general(
            weight,
            rows_ref[:, i * 2048 : i * 2048 + 2048],
            NT,
            preferred_element_type=F32,
        )
        own = total[:32] if own is None else own + total[:32]
        other = total[32:] if other is None else other + total[32:]
    for h in range(4):
        mine, theirs = own[h * 8 : h * 8 + 8], other[h * 8 : h * 8 + 8]
        value = kv_in[h, 0] + jnp.concatenate(
            [jnp.where(place[0] == 0, mine, theirs), jnp.where(place[0] == 0, theirs, mine)], 0
        )
        for i in range(kv_out.shape[1]):
            kv_out[h, i] = value


def decode(hops, copies, place, scales, codes, rotation, own_weight, other_weight, kv_in, after=()):
    def whole(array):
        return pl.BlockSpec(array.shape, lambda i, p, s: (0,) * array.ndim)

    arrays = (*codes, rotation, own_weight, other_weight, kv_in)
    outs = [(128, 2048 * len(hops)), (4, copies, 16, 128)]
    return pl.pallas_call(
        functools.partial(decode_kernel, hops, len(after)),
        grid_spec=pltpu.PrefetchScalarGridSpec(
            num_scalar_prefetch=2,
            grid=(1,),
            in_specs=[
                *(whole(array) for array in arrays),
                *(pl.BlockSpec(memory_space=pl.ANY) for _ in after),
            ],
            out_specs=[
                pl.BlockSpec(outs[0], lambda i, p, s: (0, 0)),
                pl.BlockSpec(outs[1], lambda i, p, s: (0, 0, 0, 0)),
            ],
        ),
        out_shape=[
            pltpu.HBM(outs[0], BF16),
            pltpu.HBM(outs[1], F32),
        ],
        compiler_params=params(16),
        cost_estimate=LIGHT,
        name="decode",
    )(place, scales, *arrays, *after)


def query_kernel(groups, place, *refs):
    rows_refs, refs = refs[: len(groups)], refs[len(groups) :]
    own_weight, other_weight, own_out, other_out, tiles, sems = refs
    parts = [
        (g, i * 4 + k, hop, k)
        for g, hops in enumerate(groups)
        for i, hop in enumerate(hops)
        for k in range(4)
    ]
    copies = []
    for n, (_, _, hop, k) in enumerate(parts):
        row = pl.multiple_of((chip_at(place, -k, -hop) * 2 + place[0]) * 512, 512)
        for side, weight in enumerate((own_weight, other_weight)):
            copies.append(
                pltpu.make_async_copy(
                    weight.at[pl.ds(row, 512), :], tiles.at[n, side], sems.at[n, side]
                )
            )
    for copy in copies:
        copy.start()
    totals = [jnp.zeros(own_out.shape, F32)] * 2
    for n, (g, at, _, _) in enumerate(parts):
        for side in range(2):
            copies[2 * n + side].wait()
            totals[side] += jnp.dot(
                rows_refs[g][:, at * 512 : at * 512 + 512],
                tiles[n, side],
                preferred_element_type=F32,
            )
    own_out[...] = totals[0]
    other_out[...] = totals[1]


def project(groups, place, rows, own_weight, other_weight):
    still = pl.BlockSpec((128, 256), lambda i, p: (0, 0))
    return pl.pallas_call(
        functools.partial(query_kernel, groups),
        grid_spec=pltpu.PrefetchScalarGridSpec(
            num_scalar_prefetch=1,
            grid=(1,),
            in_specs=[pl.BlockSpec(part.shape, lambda i, p: (0, 0)) for part in rows]
            + [pl.BlockSpec(memory_space=pltpu.HBM)] * 2,
            out_specs=[still, still],
            scratch_shapes=[
                pltpu.VMEM((CHIPS, 2, 512, 256), BF16),
                pltpu.SemaphoreType.DMA((CHIPS, 2)),
            ],
        ),
        out_shape=[jax.ShapeDtypeStruct((128, 256), F32)] * 2,
        compiler_params=params(20),
        cost_estimate=pl.CostEstimate(
            flops=2 * 128 * 8192 * 512, bytes_accessed=40 << 20, transcendentals=0
        ),
        name="query",
    )(place, *rows, own_weight, other_weight)


def attend_kernel(
    head_ref, length_ref, own_ref, recv_ref, kv_ref, kv_recv, cos_t, sin_t, cos_q, sin_q, mask_ref, cache_ref, out_ref
):
    score_scale = F32(1.0 / math.sqrt(HD))
    keys, values = [], []
    upper = lax.broadcasted_iota(jnp.int32, (8, 128), 0) < 4
    for chip in range(CHIPS):
        first = kv_ref[chip, 0:8] + kv_recv[chip, 0:8]
        second = kv_ref[chip, 8:16] + kv_recv[chip, 8:16]
        keys.append(jnp.where(upper, first, pltpu.roll(second, 4, 0)))
        values.append(jnp.where(upper, pltpu.roll(first, 4, 0), second))
    keys = jnp.concatenate(keys, 0).astype(BF16).astype(F32)
    values = jnp.concatenate(values, 0).astype(BF16)
    low, high = keys[:64], keys[64:]
    keys = jnp.concatenate(
        [low * cos_t[...] - high * sin_t[...], high * cos_t[...] + low * sin_t[...]], 0
    ).astype(BF16)
    heads = []
    for h in range(2):
        q = own_ref[:, h * 128 : h * 128 + 128] + recv_ref[:, h * 128 : h * 128 + 128]
        q = q * cos_q[...] + pltpu.roll(q, 64, 1) * sin_q[...]
        heads.append(q.astype(BF16))
    fresh = [
        jnp.dot(q, keys, preferred_element_type=F32) * score_scale for q in heads
    ]
    lane = lax.broadcasted_iota(jnp.int32, (32, 128), 1)
    for r in range(8):
        rows = slice(r * 16, r * 16 + 16)
        q = jnp.concatenate([heads[0][rows], heads[1][rows]], 0)
        old = (
            lax.dot_general(q, cache_ref[r, 0, 0], NT, preferred_element_type=F32) * score_scale
        )
        new = jnp.concatenate([fresh[0][rows], fresh[1][rows]], 0)
        mask = jnp.concatenate([mask_ref[rows, :]] * 2, 0)
        old = jnp.where(lane < length_ref[r], old, -jnp.inf)
        new = jnp.where(mask > 0.5, new, -jnp.inf)
        peak = jnp.maximum(
            jnp.max(old, -1, keepdims=True), jnp.max(new, -1, keepdims=True)
        )
        old = jnp.exp(old - peak)
        new = jnp.exp(new - peak)
        total = jnp.sum(old, -1, keepdims=True) + jnp.sum(new, -1, keepdims=True)
        old = (old / total).astype(BF16)
        new = (new / total).astype(BF16)
        mixed = jnp.dot(old, cache_ref[r, 0, 1], preferred_element_type=F32)
        mixed = mixed + lax.dot_general(new, values, NT, preferred_element_type=F32)
        mixed = mixed.astype(BF16)
        out_ref[rows, 0:128] = mixed[:16]
        out_ref[rows, 128:256] = mixed[16:]


def attend(head, lengths, own, recv, kv, kv_recv, cos_t, sin_t, cos_q, sin_q, mask, cache):
    def whole(array):
        return pl.BlockSpec(array.shape, lambda i, h, n: (0,) * array.ndim)

    arrays = (own, recv, kv, kv_recv, cos_t, sin_t, cos_q, sin_q, mask)
    return pl.pallas_call(
        attend_kernel,
        grid_spec=pltpu.PrefetchScalarGridSpec(
            num_scalar_prefetch=2,
            grid=(1,),
            in_specs=[whole(a) for a in arrays]
            + [pl.BlockSpec((8, 1, 2, 128, 128), lambda i, h, n: (0, h[0], 0, 0, 0))],
            out_specs=pl.BlockSpec((128, 256), lambda i, h, n: (0, 0)),
        ),
        out_shape=jax.ShapeDtypeStruct((128, 256), BF16),
        compiler_params=params(6),
        cost_estimate=pl.CostEstimate(
            flops=2 * 256 * 128 * 512, bytes_accessed=2 << 20, transcendentals=65536
        ),
        name="attend",
    )(head, lengths, *arrays, cache)


def partial_kernel(hops, place, mine, theirs, own_weight, other_weight, rotation_ref, *refs):
    outs, (tiles, sems) = refs[: len(hops)], refs[len(hops) :]
    unit = F32(1.0 / math.sqrt(RB))
    parts = [(out, at) for at in range(4) for out in range(len(hops))]
    copies = []
    for i, (out, at) in enumerate(parts):
        column = pl.multiple_of((chip_at(place, hops[out], at) * 2 + place[0]) * 512, 512)
        for side, weight in enumerate((own_weight, other_weight)):
            copies.append(
                pltpu.make_async_copy(
                    weight.at[:, pl.ds(column, 512)], tiles.at[i, side], sems.at[i, side]
                )
            )
    for copy in copies:
        copy.start()
    for i, (out, at) in enumerate(parts):
        copies[2 * i].wait()
        copies[2 * i + 1].wait()
        groups = (
            jnp.dot(mine[...], tiles[i, 0], preferred_element_type=F32),
            jnp.dot(theirs[...], tiles[i, 1], preferred_element_type=F32),
        )
        for b in range(4):
            halves = []
            for group in groups:
                block = group[:, b * 128 : b * 128 + 128]
                coarse = block.astype(BF16)
                fine = (block - coarse.astype(F32)).astype(BF16)
                halves.append(jnp.concatenate([coarse, fine], 1))
            both = lax.dot_general(
                rotation_ref[...],
                jnp.concatenate(halves, 0),
                NT,
                preferred_element_type=F32,
            )
            total = None
            for turned in (both[:, :128], both[:, 128:]):
                scale = jnp.max(jnp.abs(turned), 0, keepdims=True) * unit + TINY
                codes = (turned * (unit / scale)).astype(BF16)
                term = codes.astype(F32) * scale
                total = term if total is None else total + term
            outs[out][at, b * 128 : b * 128 + 128, :] = total.astype(outs[out].dtype)


def partials(hops, place, mine, theirs, own_weight, other_weight, rotation):
    count = 4 * len(hops)
    still = pl.BlockSpec((128, 256), lambda i, p: (0, 0))
    return pl.pallas_call(
        functools.partial(partial_kernel, hops),
        grid_spec=pltpu.PrefetchScalarGridSpec(
            num_scalar_prefetch=1,
            grid=(1,),
            in_specs=[still, still]
            + [pl.BlockSpec(memory_space=pltpu.HBM)] * 2
            + [still],
            out_specs=[pl.BlockSpec((4, 512, 128), lambda i, p: (0, 0, 0)) for _ in hops],
            scratch_shapes=[
                pltpu.VMEM((count, 2, 256, 512), BF16),
                pltpu.SemaphoreType.DMA((count, 2)),
            ],
        ),
        out_shape=[
            jax.ShapeDtypeStruct((4, 512, 128), BF16 if hop else F32) for hop in hops
        ],
        compiler_params=params(6 + 4 * len(hops)),
        cost_estimate=pl.CostEstimate(
            flops=2 * 128 * 2048 * 1024 * len(hops),
            bytes_accessed=len(hops) * 3 << 20,
            transcendentals=0,
        ),
        name="partials",
    )(place, mine, theirs, own_weight, other_weight, rotation)


def on_device(
    in_codes, in_scales, query_weight, kv_weight, out_weight, kv_cache, prefix_len, draft_parent
):
    rank = lax.axis_index(TENSOR)
    core = rank % 2
    head = rank // 8
    along_x = rank // 2 % 4
    place = jnp.stack(
        [core, jnp.where(core == 0, along_x, head), jnp.where(core == 0, head, along_x)]
    )
    signs = hadamard()
    scales = in_scales[0]

    near = jnp.stack([in_codes] + [first_shift(in_codes, k) for k in (1, 2, 3)])
    wq = in_hbm(query_weight[0])
    wq_other = in_hbm(traded(query_weight)[0])
    kv_other = traded(kv_weight)

    near, draft_parent, kv_weight, kv_other, out_weight = lax.optimization_barrier(
        (near, draft_parent, kv_weight, kv_other, out_weight)
    )

    far = {k: second_shift(near, k) for k in (1, 3, 2)}

    def as_rows(weight):
        return weight[0].transpose(2, 1, 3, 0).reshape(32, -1)

    wkv, wkv_other = as_rows(kv_weight), as_rows(kv_other)
    wo = in_hbm(out_weight[0])
    wo_other = in_hbm(traded(out_weight)[0])

    blocks = np.kron(np.eye(2, dtype=np.float32), signs)
    rotation = jnp.asarray(blocks, BF16)

    near_rows, kv_part = decode(
        (0,), 1, place, scales, (near,), rotation, wkv, wkv_other, jnp.zeros((4, 1, 16, 128), F32)
    )
    lengths, kv_part = lax.optimization_barrier((prefix_len, kv_part))

    ancestry = ancestor_table(draft_parent)
    position = lengths.astype(F32)[:, None] + (jnp.sum(ancestry, -1) - 1.0)
    frequency = jnp.power(ROPE_BASE, -(jnp.arange(64, dtype=F32) / 64))
    angles = position.reshape(128, 1) * frequency
    cosine, sine = jnp.cos(angles), jnp.sin(angles)
    cos_q = jnp.concatenate([cosine, cosine], 1)
    sin_q = jnp.concatenate([-sine, sine], 1)
    block = jnp.eye(8, dtype=F32)
    mask = (ancestry[:, :, None, :] * block[:, None, :, None]).reshape(128, 128)

    cos_t, sin_t = cosine.T, sine.T
    hops = (1, 3, 2)
    far_rows, kv_part = decode(
        hops,
        4,
        place,
        scales,
        tuple(far[k] for k in hops),
        rotation,
        wkv,
        wkv_other,
        in_hbm(kv_part),
        (mask, cos_q, sin_q, cos_t, sin_t, wq_other),
    )
    kv = exchanged(kv_part.reshape(CHIPS, 16, 128))
    own, other = project(
        ((0,), hops), place, (in_hbm(near_rows), in_hbm(far_rows)), wq, wq_other
    )
    other, kv = lax.optimization_barrier((other, kv))
    recv = traded(other)
    kv_recv = traded(kv)
    attended = attend(
        head.reshape(1), prefix_len, own, recv, kv, kv_recv, cos_t, sin_t, cos_q, sin_q, mask, kv_cache
    )
    theirs = traded(attended)
    twice = jnp.asarray(np.concatenate([signs, signs], 1), BF16)
    sent = {}
    for hops in ((2,), (1, 3), (0,)):
        for hop, piece in zip(hops, partials(hops, place, attended, theirs, wo, wo_other, twice)):
            sent[hop] = piece
    sums = sent[0]
    for k in (2, 1, 3):
        sums = sums + first_shift(sent[k], k).astype(F32)
    summed = sums[0]
    for k in (2, 1, 3):
        summed = summed + second_shift(sums[k].astype(BF16), k).astype(F32)

    here = lax.dynamic_slice_in_dim(scales, rank * 4, 4)
    turned_in = in_codes.T.astype(F32) * jnp.repeat(here, RB)[:, None]
    turned = summed + turned_in
    peak = jnp.max(jnp.abs(turned.reshape(4, RB, 128)), (1, 2))
    next_rows = swapped(turned, "section")
    everyone = lax.all_to_all(
        jnp.broadcast_to(peak[None, None], (128, 1, 4)),
        ("section", "dp", TENSOR),
        0,
        0,
        tiled=True,
    )
    from_there = lax.dynamic_index_in_dim(
        everyone.reshape(2, 2, 128), 1 - lax.axis_index("section"), 0, keepdims=False
    )
    next_scales = jnp.max(from_there, 0) + TINY
    scale_here = lax.dynamic_slice_in_dim(next_scales, rank * 4, 4)
    next_codes = (next_rows.T / jnp.repeat(scale_here, RB)[None, :]).astype(BF16)
    return (next_codes, next_scales[None])


def solution(mesh):
    rows = ("section", "dp")
    placed = (
        P(rows, TENSOR),
        P("section", None),
        P("section", None, TENSOR),
        P("section", None, None, None, TENSOR),
        P("section", TENSOR, None),
        P(rows, None, None, None, None),
        P(rows),
        P(rows, None),
    )
    return jax.shard_map(
        on_device,
        mesh=mesh,
        in_specs=placed,
        out_specs=(P(rows, TENSOR), P("section", None)),
        check_vma=False,
    )
```

```python
import functools
import math

import jax
import jax.numpy as jnp
import numpy as np
from jax import lax
from jax.experimental import pallas as pl
from jax.experimental.pallas import tpu as pltpu
from jax.sharding import PartitionSpec as P

HD = 128
RB = 128
CHIPS = 16
ROPE_BASE = 500000.0
TINY = 1e-06
TENSOR = "tensor"


def device(y, x, core):
    return (y * 4 + x) * 2 + core


F32 = jnp.float32
BF16 = jnp.bfloat16
NT = (((1,), (1,)), ((), ()))
LIGHT = pl.CostEstimate(flops=1024, bytes_accessed=1024, transcendentals=0)


def hadamard():
    index = np.arange(RB)
    common = index[:, None] & index[None, :]
    parity = np.zeros((RB, RB), np.int32)
    for place in range(7):
        parity = parity + (common >> place & 1)
    return np.where(parity % 2 == 0, 1.0, -1.0).astype(np.float32)


def ancestor_table(draft_parent):
    count, size = draft_parent.shape
    target = lax.broadcasted_iota(jnp.int32, (count, size, size), 2)
    source = lax.broadcasted_iota(jnp.int32, (count, size, size), 1)
    table = ((target == draft_parent[:, :, None]) | (target == source)).astype(F32)
    for _ in range(4):
        table = jnp.minimum(jnp.einsum("rij,rjk->rik", table, table), 1.0)
    return table


def swapped(block, axis):
    return lax.ppermute(block, axis, [(0, 1), (1, 0)])


def traded(block):
    return lax.ppermute(block, TENSOR, [(i, i ^ 1) for i in range(32)])


def exchanged(pieces):
    groups = [[chip * 2 + core for chip in range(CHIPS)] for core in range(2)]
    return lax.all_to_all(pieces, TENSOR, 0, 0, tiled=True, axis_index_groups=groups)


def shifted(block, by, second):
    pairs = []
    for y in range(4):
        for x in range(4):
            for core in range(2):
                along_y = (core == 1) != second
                to_y, to_x = ((y + by) % 4, x) if along_y else (y, (x + by) % 4)
                pairs.append((device(y, x, core), device(to_y, to_x, core)))
    return lax.ppermute(block, TENSOR, pairs)


def first_shift(block, by):
    return shifted(block, by, False)


def second_shift(block, by):
    return shifted(block, by, True)


def chip_at(place, first, second):
    first = lax.rem(place[1] + 4 + first, 4)
    second = lax.rem(place[2] + 4 + second, 4)
    return jnp.where(place[0] == 0, second * 4 + first, first * 4 + second)


def in_hbm(array):
    return pltpu.with_memory_space_constraint(array, pltpu.HBM)


def params(mebibytes):
    return pltpu.CompilerParams(vmem_limit_bytes=mebibytes << 20)


def decode_kernel(hops, waits, place, scale_ref, *refs):
    codes_refs, refs = refs[: len(hops)], refs[len(hops) :]
    rotation_ref, own_weight, other_weight, kv_in = refs[:4]
    rows_out, kv_out, rows_ref, before, sems = refs[4 + waits :]
    coming = pltpu.make_async_copy(kv_in, before, sems.at[len(hops)])
    coming.start()
    leaving = []
    own = other = None
    for i, hop in enumerate(hops):
        own_tiles, other_tiles = [], []
        for k in range(4):
            tile = chip_at(place, -k, -hop) * 2 + place[0]
            for half in range(2):
                product = jnp.dot(
                    codes_refs[i][k, :, half * 256 : half * 256 + 256],
                    rotation_ref[...],
                    preferred_element_type=F32,
                )
                for b in range(2):
                    factor = scale_ref[tile * 4 + half * 2 + b] * F32(1.0 / math.sqrt(RB))
                    at = i * 2048 + k * 512 + half * 256 + b * 128
                    rows_ref[:, at : at + 128] = (
                        product[:, b * 128 : b * 128 + 128] * factor
                    ).astype(BF16)
            column = pl.ds(pl.multiple_of(tile * 512, 512), 512)
            own_tiles.append(own_weight[:, column])
            other_tiles.append(other_weight[:, column])
        span = pl.ds(i * 2048, 2048)
        leaving.append(pltpu.make_async_copy(rows_ref.at[:, span], rows_out.at[:, span], sems.at[i]))
        leaving[i].start()
        weight = jnp.concatenate(
            [jnp.concatenate(own_tiles, 1), jnp.concatenate(other_tiles, 1)], 0
        )
        total = lax.dot_general(
            weight,
            rows_ref[:, i * 2048 : i * 2048 + 2048],
            NT,
            preferred_element_type=F32,
        )
        own = total[:32] if own is None else own + total[:32]
        other = total[32:] if other is None else other + total[32:]
    coming.wait()
    for h in range(4):
        mine, theirs = own[h * 8 : h * 8 + 8], other[h * 8 : h * 8 + 8]
        value = before[h, 0] + jnp.concatenate(
            [jnp.where(place[0] == 0, mine, theirs), jnp.where(place[0] == 0, theirs, mine)], 0
        )
        for i in range(kv_out.shape[1]):
            kv_out[h, i] = value
    for copy in leaving:
        copy.wait()


def decode(hops, copies, place, scales, codes, rotation, own_weight, other_weight, kv_in, after=()):
    def whole(array):
        return pl.BlockSpec(array.shape, lambda i, p, s: (0,) * array.ndim)

    arrays = (*codes, rotation, own_weight, other_weight)
    outs = [(128, 2048 * len(hops)), (4, copies, 16, 128)]
    return pl.pallas_call(
        functools.partial(decode_kernel, hops, len(after)),
        grid_spec=pltpu.PrefetchScalarGridSpec(
            num_scalar_prefetch=2,
            grid=(1,),
            in_specs=[
                *(whole(array) for array in arrays),
                pl.BlockSpec(memory_space=pl.ANY),
                *(pl.BlockSpec(memory_space=pl.ANY) for _ in after),
            ],
            out_specs=[
                pl.BlockSpec(memory_space=pl.ANY),
                pl.BlockSpec(outs[1], lambda i, p, s: (0, 0, 0, 0)),
            ],
            scratch_shapes=[
                pltpu.VMEM(outs[0], BF16),
                pltpu.VMEM(kv_in.shape, F32),
                pltpu.SemaphoreType.DMA((len(hops) + 1,)),
            ],
        ),
        out_shape=[
            pltpu.HBM(outs[0], BF16),
            pltpu.HBM(outs[1], F32),
        ],
        compiler_params=params(16),
        cost_estimate=LIGHT,
        name="decode",
    )(place, scales, *arrays, kv_in, *after)


def query_kernel(groups, place, *refs):
    rows_refs, refs = refs[: len(groups)], refs[len(groups) :]
    own_weight, other_weight, own_out, other_out, tiles, sems = refs
    parts = [
        (g, i * 4 + k, hop, k)
        for g, hops in enumerate(groups)
        for i, hop in enumerate(hops)
        for k in range(4)
    ]
    copies = []
    for n, (_, _, hop, k) in enumerate(parts):
        row = pl.multiple_of((chip_at(place, -k, -hop) * 2 + place[0]) * 512, 512)
        for side, weight in enumerate((own_weight, other_weight)):
            copies.append(
                pltpu.make_async_copy(
                    weight.at[pl.ds(row, 512), :], tiles.at[n, side], sems.at[n, side]
                )
            )
    for copy in copies:
        copy.start()
    totals = [jnp.zeros(own_out.shape, F32)] * 2
    for n, (g, at, _, _) in enumerate(parts):
        for side in range(2):
            copies[2 * n + side].wait()
            totals[side] += jnp.dot(
                rows_refs[g][:, at * 512 : at * 512 + 512],
                tiles[n, side],
                preferred_element_type=F32,
            )
    own_out[...] = totals[0]
    other_out[...] = totals[1]


def project(groups, place, rows, own_weight, other_weight):
    still = pl.BlockSpec((128, 256), lambda i, p: (0, 0))
    return pl.pallas_call(
        functools.partial(query_kernel, groups),
        grid_spec=pltpu.PrefetchScalarGridSpec(
            num_scalar_prefetch=1,
            grid=(1,),
            in_specs=[pl.BlockSpec(part.shape, lambda i, p: (0, 0)) for part in rows]
            + [pl.BlockSpec(memory_space=pltpu.HBM)] * 2,
            out_specs=[still, still],
            scratch_shapes=[
                pltpu.VMEM((CHIPS, 2, 512, 256), BF16),
                pltpu.SemaphoreType.DMA((CHIPS, 2)),
            ],
        ),
        out_shape=[jax.ShapeDtypeStruct((128, 256), F32)] * 2,
        compiler_params=params(20),
        cost_estimate=pl.CostEstimate(
            flops=2 * 128 * 8192 * 512, bytes_accessed=40 << 20, transcendentals=0
        ),
        name="query",
    )(place, *rows, own_weight, other_weight)


def attend_kernel(
    head_ref, length_ref, own_ref, recv_ref, kv_ref, kv_recv, cos_t, sin_t, cos_q, sin_q, mask_ref, cache_ref, out_ref
):
    score_scale = F32(1.0 / math.sqrt(HD))
    keys, values = [], []
    upper = lax.broadcasted_iota(jnp.int32, (8, 128), 0) < 4
    for chip in range(CHIPS):
        first = kv_ref[chip, 0:8] + kv_recv[chip, 0:8]
        second = kv_ref[chip, 8:16] + kv_recv[chip, 8:16]
        keys.append(jnp.where(upper, first, pltpu.roll(second, 4, 0)))
        values.append(jnp.where(upper, pltpu.roll(first, 4, 0), second))
    keys = jnp.concatenate(keys, 0).astype(BF16).astype(F32)
    values = jnp.concatenate(values, 0).astype(BF16)
    low, high = keys[:64], keys[64:]
    keys = jnp.concatenate(
        [low * cos_t[...] - high * sin_t[...], high * cos_t[...] + low * sin_t[...]], 0
    ).astype(BF16)
    heads = []
    for h in range(2):
        q = own_ref[:, h * 128 : h * 128 + 128] + recv_ref[:, h * 128 : h * 128 + 128]
        q = q * cos_q[...] + pltpu.roll(q, 64, 1) * sin_q[...]
        heads.append(q.astype(BF16))
    fresh = [
        jnp.dot(q, keys, preferred_element_type=F32) * score_scale for q in heads
    ]
    lane = lax.broadcasted_iota(jnp.int32, (32, 128), 1)
    for r in range(8):
        rows = slice(r * 16, r * 16 + 16)
        q = jnp.concatenate([heads[0][rows], heads[1][rows]], 0)
        old = (
            lax.dot_general(q, cache_ref[r, 0, 0], NT, preferred_element_type=F32) * score_scale
        )
        new = jnp.concatenate([fresh[0][rows], fresh[1][rows]], 0)
        mask = jnp.concatenate([mask_ref[rows, :]] * 2, 0)
        old = jnp.where(lane < length_ref[r], old, -jnp.inf)
        new = jnp.where(mask > 0.5, new, -jnp.inf)
        peak = jnp.maximum(
            jnp.max(old, -1, keepdims=True), jnp.max(new, -1, keepdims=True)
        )
        old = jnp.exp(old - peak)
        new = jnp.exp(new - peak)
        total = jnp.sum(old, -1, keepdims=True) + jnp.sum(new, -1, keepdims=True)
        old = (old / total).astype(BF16)
        new = (new / total).astype(BF16)
        mixed = jnp.dot(old, cache_ref[r, 0, 1], preferred_element_type=F32)
        mixed = mixed + lax.dot_general(new, values, NT, preferred_element_type=F32)
        mixed = mixed.astype(BF16)
        out_ref[rows, 0:128] = mixed[:16]
        out_ref[rows, 128:256] = mixed[16:]


def attend(head, lengths, own, recv, kv, kv_recv, cos_t, sin_t, cos_q, sin_q, mask, cache):
    def whole(array):
        return pl.BlockSpec(array.shape, lambda i, h, n: (0,) * array.ndim)

    arrays = (own, recv, kv, kv_recv, cos_t, sin_t, cos_q, sin_q, mask)
    return pl.pallas_call(
        attend_kernel,
        grid_spec=pltpu.PrefetchScalarGridSpec(
            num_scalar_prefetch=2,
            grid=(1,),
            in_specs=[whole(a) for a in arrays]
            + [pl.BlockSpec((8, 1, 2, 128, 128), lambda i, h, n: (0, h[0], 0, 0, 0))],
            out_specs=pl.BlockSpec((128, 256), lambda i, h, n: (0, 0)),
        ),
        out_shape=jax.ShapeDtypeStruct((128, 256), BF16),
        compiler_params=params(6),
        cost_estimate=pl.CostEstimate(
            flops=2 * 256 * 128 * 512, bytes_accessed=2 << 20, transcendentals=65536
        ),
        name="attend",
    )(head, lengths, *arrays, cache)


def partial_kernel(hops, place, mine, theirs, own_weight, other_weight, rotation_ref, *refs):
    outs, (tiles, sems) = refs[: len(hops)], refs[len(hops) :]
    unit = F32(1.0 / math.sqrt(RB))
    parts = [(out, at) for at in range(4) for out in range(len(hops))]
    copies = []
    for i, (out, at) in enumerate(parts):
        column = pl.multiple_of((chip_at(place, hops[out], at) * 2 + place[0]) * 512, 512)
        for side, weight in enumerate((own_weight, other_weight)):
            copies.append(
                pltpu.make_async_copy(
                    weight.at[:, pl.ds(column, 512)], tiles.at[i, side], sems.at[i, side]
                )
            )
    for copy in copies:
        copy.start()
    for i, (out, at) in enumerate(parts):
        copies[2 * i].wait()
        copies[2 * i + 1].wait()
        groups = (
            jnp.dot(mine[...], tiles[i, 0], preferred_element_type=F32),
            jnp.dot(theirs[...], tiles[i, 1], preferred_element_type=F32),
        )
        for b in range(4):
            halves = []
            for group in groups:
                block = group[:, b * 128 : b * 128 + 128]
                coarse = block.astype(BF16)
                fine = (block - coarse.astype(F32)).astype(BF16)
                halves.append(jnp.concatenate([coarse, fine], 1))
            both = lax.dot_general(
                rotation_ref[...],
                jnp.concatenate(halves, 0),
                NT,
                preferred_element_type=F32,
            )
            total = None
            for turned in (both[:, :128], both[:, 128:]):
                scale = jnp.max(jnp.abs(turned), 0, keepdims=True) * unit + TINY
                codes = (turned * (unit / scale)).astype(BF16)
                term = codes.astype(F32) * scale
                total = term if total is None else total + term
            outs[out][at, b * 128 : b * 128 + 128, :] = total.astype(outs[out].dtype)


def partials(hops, place, mine, theirs, own_weight, other_weight, rotation):
    count = 4 * len(hops)
    still = pl.BlockSpec((128, 256), lambda i, p: (0, 0))
    return pl.pallas_call(
        functools.partial(partial_kernel, hops),
        grid_spec=pltpu.PrefetchScalarGridSpec(
            num_scalar_prefetch=1,
            grid=(1,),
            in_specs=[still, still]
            + [pl.BlockSpec(memory_space=pltpu.HBM)] * 2
            + [still],
            out_specs=[pl.BlockSpec((4, 512, 128), lambda i, p: (0, 0, 0)) for _ in hops],
            scratch_shapes=[
                pltpu.VMEM((count, 2, 256, 512), BF16),
                pltpu.SemaphoreType.DMA((count, 2)),
            ],
        ),
        out_shape=[
            jax.ShapeDtypeStruct((4, 512, 128), BF16 if hop else F32) for hop in hops
        ],
        compiler_params=params(6 + 4 * len(hops)),
        cost_estimate=pl.CostEstimate(
            flops=2 * 128 * 2048 * 1024 * len(hops),
            bytes_accessed=len(hops) * 3 << 20,
            transcendentals=0,
        ),
        name="partials",
    )(place, mine, theirs, own_weight, other_weight, rotation)


def on_device(
    in_codes, in_scales, query_weight, kv_weight, out_weight, kv_cache, prefix_len, draft_parent
):
    rank = lax.axis_index(TENSOR)
    core = rank % 2
    head = rank // 8
    along_x = rank // 2 % 4
    place = jnp.stack(
        [core, jnp.where(core == 0, along_x, head), jnp.where(core == 0, head, along_x)]
    )
    signs = hadamard()
    scales = in_scales[0]

    near = jnp.stack([in_codes] + [first_shift(in_codes, k) for k in (1, 2, 3)])
    wq = in_hbm(query_weight[0])
    wq_other = in_hbm(traded(query_weight)[0])
    kv_other = traded(kv_weight)

    near, draft_parent, kv_weight, kv_other, out_weight = lax.optimization_barrier(
        (near, draft_parent, kv_weight, kv_other, out_weight)
    )

    far = {k: second_shift(near, k) for k in (1, 3, 2)}

    def as_rows(weight):
        return weight[0].transpose(2, 1, 3, 0).reshape(32, -1)

    wkv, wkv_other = as_rows(kv_weight), as_rows(kv_other)
    wo = in_hbm(out_weight[0])
    wo_other = in_hbm(traded(out_weight)[0])

    blocks = np.kron(np.eye(2, dtype=np.float32), signs)
    rotation = jnp.asarray(blocks, BF16)

    near_rows, kv_part = decode(
        (0,), 1, place, scales, (near,), rotation, wkv, wkv_other, jnp.zeros((4, 1, 16, 128), F32)
    )
    lengths, kv_part = lax.optimization_barrier((prefix_len, kv_part))

    ancestry = ancestor_table(draft_parent)
    position = lengths.astype(F32)[:, None] + (jnp.sum(ancestry, -1) - 1.0)
    frequency = jnp.power(ROPE_BASE, -(jnp.arange(64, dtype=F32) / 64))
    angles = position.reshape(128, 1) * frequency
    cosine, sine = jnp.cos(angles), jnp.sin(angles)
    cos_q = jnp.concatenate([cosine, cosine], 1)
    sin_q = jnp.concatenate([-sine, sine], 1)
    block = jnp.eye(8, dtype=F32)
    mask = (ancestry[:, :, None, :] * block[:, None, :, None]).reshape(128, 128)

    cos_t, sin_t = cosine.T, sine.T
    hops = (1, 3, 2)
    far_rows, kv_part = decode(
        hops,
        4,
        place,
        scales,
        tuple(far[k] for k in hops),
        rotation,
        wkv,
        wkv_other,
        in_hbm(kv_part),
        (mask, cos_q, sin_q, cos_t, sin_t, wq_other),
    )
    kv = exchanged(kv_part.reshape(CHIPS, 16, 128))
    own, other = project(
        ((0,), hops), place, (in_hbm(near_rows), in_hbm(far_rows)), wq, wq_other
    )
    other, kv = lax.optimization_barrier((other, kv))
    recv = traded(other)
    kv_recv = traded(kv)
    attended = attend(
        head.reshape(1), prefix_len, own, recv, kv, kv_recv, cos_t, sin_t, cos_q, sin_q, mask, kv_cache
    )
    theirs = traded(attended)
    twice = jnp.asarray(np.concatenate([signs, signs], 1), BF16)
    sent = {}
    for hops in ((2,), (1, 3), (0,)):
        for hop, piece in zip(hops, partials(hops, place, attended, theirs, wo, wo_other, twice)):
            sent[hop] = piece
    sums = sent[0]
    for k in (2, 1, 3):
        sums = sums + first_shift(sent[k], k).astype(F32)
    summed = sums[0]
    for k in (2, 1, 3):
        summed = summed + second_shift(sums[k].astype(BF16), k).astype(F32)

    here = lax.dynamic_slice_in_dim(scales, rank * 4, 4)
    turned_in = in_codes.T.astype(F32) * jnp.repeat(here, RB)[:, None]
    turned = summed + turned_in
    peak = jnp.max(jnp.abs(turned.reshape(4, RB, 128)), (1, 2))
    next_rows = swapped(turned, "section")
    spread = lax.dynamic_update_slice_in_dim(jnp.zeros((128,), F32), peak, rank * 4, 0)
    everyone = lax.all_to_all(
        jnp.broadcast_to(spread[None, None], (128, 1, 128)),
        ("section", "dp", TENSOR),
        0,
        0,
        tiled=True,
    )
    from_there = lax.dynamic_slice_in_dim(everyone, 64 * (1 - lax.axis_index("section")), 64)
    next_scales = jnp.max(from_there, (0, 1)) + TINY
    scale_here = lax.dynamic_slice_in_dim(next_scales, rank * 4, 4)
    next_codes = (next_rows.T / jnp.repeat(scale_here, RB)[None, :]).astype(BF16)
    return (next_codes, next_scales[None])


def solution(mesh):
    rows = ("section", "dp")
    placed = (
        P(rows, TENSOR),
        P("section", None),
        P("section", None, TENSOR),
        P("section", None, None, None, TENSOR),
        P("section", TENSOR, None),
        P(rows, None, None, None, None),
        P(rows),
        P(rows, None),
    )
    return jax.shard_map(
        on_device,
        mesh=mesh,
        in_specs=placed,
        out_specs=(P(rows, TENSOR), P("section", None)),
        check_vma=False,
    )
```

```python
import functools
import math

import jax
import jax.numpy as jnp
import numpy as np
from jax import lax
from jax.experimental import pallas as pl
from jax.experimental.pallas import tpu as pltpu
from jax.sharding import PartitionSpec as P

HD = 128
RB = 128
CHIPS = 16
ROPE_BASE = 500000.0
TINY = 1e-06
TENSOR = "tensor"


def device(y, x, core):
    return (y * 4 + x) * 2 + core


F32 = jnp.float32
BF16 = jnp.bfloat16
NT = (((1,), (1,)), ((), ()))
LIGHT = pl.CostEstimate(flops=1024, bytes_accessed=1024, transcendentals=0)


def hadamard():
    index = np.arange(RB)
    common = index[:, None] & index[None, :]
    parity = np.zeros((RB, RB), np.int32)
    for place in range(7):
        parity = parity + (common >> place & 1)
    return np.where(parity % 2 == 0, 1.0, -1.0).astype(np.float32)


def ancestor_table(draft_parent):
    count, size = draft_parent.shape
    target = lax.broadcasted_iota(jnp.int32, (count, size, size), 2)
    source = lax.broadcasted_iota(jnp.int32, (count, size, size), 1)
    table = ((target == draft_parent[:, :, None]) | (target == source)).astype(F32)
    for _ in range(4):
        table = jnp.minimum(jnp.einsum("rij,rjk->rik", table, table), 1.0)
    return table


def swapped(block, axis):
    return lax.ppermute(block, axis, [(0, 1), (1, 0)])


def traded(block):
    return lax.ppermute(block, TENSOR, [(i, i ^ 1) for i in range(32)])


def exchanged(pieces):
    groups = [[chip * 2 + core for chip in range(CHIPS)] for core in range(2)]
    return lax.all_to_all(pieces, TENSOR, 0, 0, tiled=True, axis_index_groups=groups)


def shifted(block, by, second):
    pairs = []
    for y in range(4):
        for x in range(4):
            for core in range(2):
                along_y = (core == 1) != second
                to_y, to_x = ((y + by) % 4, x) if along_y else (y, (x + by) % 4)
                pairs.append((device(y, x, core), device(to_y, to_x, core)))
    return lax.ppermute(block, TENSOR, pairs)


def first_shift(block, by):
    return shifted(block, by, False)


def second_shift(block, by):
    return shifted(block, by, True)


def chip_at(place, first, second):
    first = lax.rem(place[1] + 4 + first, 4)
    second = lax.rem(place[2] + 4 + second, 4)
    return jnp.where(place[0] == 0, second * 4 + first, first * 4 + second)


def in_hbm(array):
    return pltpu.with_memory_space_constraint(array, pltpu.HBM)


def params(mebibytes):
    return pltpu.CompilerParams(vmem_limit_bytes=mebibytes << 20)


def decode_kernel(hops, waits, place, scale_ref, *refs):
    codes_refs, refs = refs[: len(hops)], refs[len(hops) :]
    rotation_ref, own_weight, other_weight, kv_in = refs[:4]
    rows_ref, kv_out = refs[4 + waits :]
    own = other = None
    for i, hop in enumerate(hops):
        own_tiles, other_tiles = [], []
        for k in range(4):
            tile = chip_at(place, -k, -hop) * 2 + place[0]
            for half in range(2):
                product = jnp.dot(
                    codes_refs[i][k, :, half * 256 : half * 256 + 256],
                    rotation_ref[...],
                    preferred_element_type=F32,
                )
                for b in range(2):
                    factor = scale_ref[tile * 4 + half * 2 + b] * F32(1.0 / math.sqrt(RB))
                    at = i * 2048 + k * 512 + half * 256 + b * 128
                    rows_ref[:, at : at + 128] = (
                        product[:, b * 128 : b * 128 + 128] * factor
                    ).astype(BF16)
            column = pl.ds(pl.multiple_of(tile * 512, 512), 512)
            own_tiles.append(own_weight[:, column])
            other_tiles.append(other_weight[:, column])
        weight = jnp.concatenate(
            [jnp.concatenate(own_tiles, 1), jnp.concatenate(other_tiles, 1)], 0
        )
        total = lax.dot_general(
            weight,
            rows_ref[:, i * 2048 : i * 2048 + 2048],
            NT,
            preferred_element_type=F32,
        )
        own = total[:32] if own is None else own + total[:32]
        other = total[32:] if other is None else other + total[32:]
    for h in range(4):
        mine, theirs = own[h * 8 : h * 8 + 8], other[h * 8 : h * 8 + 8]
        value = kv_in[h, 0] + jnp.concatenate(
            [jnp.where(place[0] == 0, mine, theirs), jnp.where(place[0] == 0, theirs, mine)], 0
        )
        for i in range(kv_out.shape[1]):
            kv_out[h, i] = value


def decode(hops, copies, place, scales, codes, rotation, own_weight, other_weight, kv_in, after=()):
    def whole(array):
        return pl.BlockSpec(array.shape, lambda i, p, s: (0,) * array.ndim)

    arrays = (*codes, rotation, own_weight, other_weight, kv_in)
    outs = [(128, 2048 * len(hops)), (4, copies, 16, 128)]
    return pl.pallas_call(
        functools.partial(decode_kernel, hops, len(after)),
        grid_spec=pltpu.PrefetchScalarGridSpec(
            num_scalar_prefetch=2,
            grid=(1,),
            in_specs=[
                *(whole(array) for array in arrays),
                *(pl.BlockSpec(memory_space=pl.ANY) for _ in after),
            ],
            out_specs=[
                pl.BlockSpec(outs[0], lambda i, p, s: (0, 0)),
                pl.BlockSpec(outs[1], lambda i, p, s: (0, 0, 0, 0)),
            ],
        ),
        out_shape=[
            pltpu.HBM(outs[0], BF16),
            pltpu.HBM(outs[1], F32),
        ],
        compiler_params=params(16),
        cost_estimate=LIGHT,
        name="decode",
    )(place, scales, *arrays, *after)


def query_kernel(groups, place, *refs):
    rows_refs, refs = refs[: len(groups)], refs[len(groups) :]
    own_weight, other_weight, own_out, other_out, tiles, sems = refs
    parts = [
        (g, i * 4 + k, hop, k)
        for g, hops in enumerate(groups)
        for i, hop in enumerate(hops)
        for k in range(4)
    ]
    copies = []
    for n, (_, _, hop, k) in enumerate(parts):
        row = pl.multiple_of((chip_at(place, -k, -hop) * 2 + place[0]) * 512, 512)
        for side, weight in enumerate((own_weight, other_weight)):
            copies.append(
                pltpu.make_async_copy(
                    weight.at[pl.ds(row, 512), :], tiles.at[n, side], sems.at[n, side]
                )
            )
    for copy in copies:
        copy.start()
    totals = [jnp.zeros(own_out.shape, F32)] * 2
    for n, (g, at, _, _) in enumerate(parts):
        for side in range(2):
            copies[2 * n + side].wait()
            totals[side] += jnp.dot(
                rows_refs[g][:, at * 512 : at * 512 + 512],
                tiles[n, side],
                preferred_element_type=F32,
            )
    own_out[...] = totals[0]
    other_out[...] = totals[1]


def project(groups, place, rows, own_weight, other_weight):
    still = pl.BlockSpec((128, 256), lambda i, p: (0, 0))
    return pl.pallas_call(
        functools.partial(query_kernel, groups),
        grid_spec=pltpu.PrefetchScalarGridSpec(
            num_scalar_prefetch=1,
            grid=(1,),
            in_specs=[pl.BlockSpec(part.shape, lambda i, p: (0, 0)) for part in rows]
            + [pl.BlockSpec(memory_space=pltpu.HBM)] * 2,
            out_specs=[still, still],
            scratch_shapes=[
                pltpu.VMEM((CHIPS, 2, 512, 256), BF16),
                pltpu.SemaphoreType.DMA((CHIPS, 2)),
            ],
        ),
        out_shape=[jax.ShapeDtypeStruct((128, 256), F32)] * 2,
        compiler_params=params(20),
        cost_estimate=pl.CostEstimate(
            flops=2 * 128 * 8192 * 512, bytes_accessed=40 << 20, transcendentals=0
        ),
        name="query",
    )(place, *rows, own_weight, other_weight)


def attend_kernel(
    head_ref, length_ref, own_ref, recv_ref, kv_ref, kv_recv, cos_t, sin_t, cos_q, sin_q, mask_ref, cache_ref, out_ref
):
    score_scale = F32(1.0 / math.sqrt(HD))
    keys, values = [], []
    upper = lax.broadcasted_iota(jnp.int32, (8, 128), 0) < 4
    for chip in range(CHIPS):
        first = kv_ref[chip, 0:8] + kv_recv[chip, 0:8]
        second = kv_ref[chip, 8:16] + kv_recv[chip, 8:16]
        keys.append(jnp.where(upper, first, pltpu.roll(second, 4, 0)))
        values.append(jnp.where(upper, pltpu.roll(first, 4, 0), second))
    keys = jnp.concatenate(keys, 0).astype(BF16).astype(F32)
    values = jnp.concatenate(values, 0).astype(BF16)
    low, high = keys[:64], keys[64:]
    keys = jnp.concatenate(
        [low * cos_t[...] - high * sin_t[...], high * cos_t[...] + low * sin_t[...]], 0
    ).astype(BF16)
    heads = []
    for h in range(2):
        q = own_ref[:, h * 128 : h * 128 + 128] + recv_ref[:, h * 128 : h * 128 + 128]
        q = q * cos_q[...] + pltpu.roll(q, 64, 1) * sin_q[...]
        heads.append(q.astype(BF16))
    fresh = [
        jnp.dot(q, keys, preferred_element_type=F32) * score_scale for q in heads
    ]
    lane = lax.broadcasted_iota(jnp.int32, (32, 128), 1)
    for r in range(8):
        rows = slice(r * 16, r * 16 + 16)
        q = jnp.concatenate([heads[0][rows], heads[1][rows]], 0)
        old = (
            lax.dot_general(q, cache_ref[r, 0, 0], NT, preferred_element_type=F32) * score_scale
        )
        new = jnp.concatenate([fresh[0][rows], fresh[1][rows]], 0)
        mask = jnp.concatenate([mask_ref[rows, :]] * 2, 0)
        old = jnp.where(lane < length_ref[r], old, -jnp.inf)
        new = jnp.where(mask > 0.5, new, -jnp.inf)
        peak = jnp.maximum(
            jnp.max(old, -1, keepdims=True), jnp.max(new, -1, keepdims=True)
        )
        old = jnp.exp(old - peak)
        new = jnp.exp(new - peak)
        total = jnp.sum(old, -1, keepdims=True) + jnp.sum(new, -1, keepdims=True)
        old = (old / total).astype(BF16)
        new = (new / total).astype(BF16)
        mixed = jnp.dot(old, cache_ref[r, 0, 1], preferred_element_type=F32)
        mixed = mixed + lax.dot_general(new, values, NT, preferred_element_type=F32)
        mixed = mixed.astype(BF16)
        out_ref[rows, 0:128] = mixed[:16]
        out_ref[rows, 128:256] = mixed[16:]


def attend(head, lengths, own, recv, kv, kv_recv, cos_t, sin_t, cos_q, sin_q, mask, cache):
    def whole(array):
        return pl.BlockSpec(array.shape, lambda i, h, n: (0,) * array.ndim)

    arrays = (own, recv, kv, kv_recv, cos_t, sin_t, cos_q, sin_q, mask)
    return pl.pallas_call(
        attend_kernel,
        grid_spec=pltpu.PrefetchScalarGridSpec(
            num_scalar_prefetch=2,
            grid=(1,),
            in_specs=[whole(a) for a in arrays]
            + [pl.BlockSpec((8, 1, 2, 128, 128), lambda i, h, n: (0, h[0], 0, 0, 0))],
            out_specs=pl.BlockSpec((128, 256), lambda i, h, n: (0, 0)),
        ),
        out_shape=jax.ShapeDtypeStruct((128, 256), BF16),
        compiler_params=params(6),
        cost_estimate=pl.CostEstimate(
            flops=2 * 256 * 128 * 512, bytes_accessed=2 << 20, transcendentals=65536
        ),
        name="attend",
    )(head, lengths, *arrays, cache)


def partial_kernel(hops, place, mine, theirs, own_weight, other_weight, rotation_ref, *refs):
    outs, (tiles, sems) = refs[: len(hops)], refs[len(hops) :]
    unit = F32(1.0 / math.sqrt(RB))
    parts = [(out, at) for at in range(4) for out in range(len(hops))]
    copies = []
    for i, (out, at) in enumerate(parts):
        column = pl.multiple_of((chip_at(place, hops[out], at) * 2 + place[0]) * 512, 512)
        for side, weight in enumerate((own_weight, other_weight)):
            copies.append(
                pltpu.make_async_copy(
                    weight.at[:, pl.ds(column, 512)], tiles.at[i, side], sems.at[i, side]
                )
            )
    for copy in copies:
        copy.start()
    for i, (out, at) in enumerate(parts):
        copies[2 * i].wait()
        copies[2 * i + 1].wait()
        groups = (
            jnp.dot(mine[...], tiles[i, 0], preferred_element_type=F32),
            jnp.dot(theirs[...], tiles[i, 1], preferred_element_type=F32),
        )
        for b in range(4):
            halves = []
            for group in groups:
                block = group[:, b * 128 : b * 128 + 128]
                coarse = block.astype(BF16)
                fine = (block - coarse.astype(F32)).astype(BF16)
                halves.append(jnp.concatenate([coarse, fine], 1))
            both = lax.dot_general(
                rotation_ref[...],
                jnp.concatenate(halves, 0),
                NT,
                preferred_element_type=F32,
            )
            total = None
            for turned in (both[:, :128], both[:, 128:]):
                scale = jnp.max(jnp.abs(turned), 0, keepdims=True) * unit + TINY
                codes = (turned * (unit / scale)).astype(BF16)
                term = codes.astype(F32) * scale
                total = term if total is None else total + term
            outs[out][at, b * 128 : b * 128 + 128, :] = total.astype(outs[out].dtype)


def partials(hops, place, mine, theirs, own_weight, other_weight, rotation):
    count = 4 * len(hops)
    still = pl.BlockSpec((128, 256), lambda i, p: (0, 0))
    return pl.pallas_call(
        functools.partial(partial_kernel, hops),
        grid_spec=pltpu.PrefetchScalarGridSpec(
            num_scalar_prefetch=1,
            grid=(1,),
            in_specs=[still, still]
            + [pl.BlockSpec(memory_space=pltpu.HBM)] * 2
            + [still],
            out_specs=[pl.BlockSpec((4, 512, 128), lambda i, p: (0, 0, 0)) for _ in hops],
            scratch_shapes=[
                pltpu.VMEM((count, 2, 256, 512), BF16),
                pltpu.SemaphoreType.DMA((count, 2)),
            ],
        ),
        out_shape=[
            jax.ShapeDtypeStruct((4, 512, 128), BF16 if hop else F32) for hop in hops
        ],
        compiler_params=params(6 + 4 * len(hops)),
        cost_estimate=pl.CostEstimate(
            flops=2 * 128 * 2048 * 1024 * len(hops),
            bytes_accessed=len(hops) * 3 << 20,
            transcendentals=0,
        ),
        name="partials",
    )(place, mine, theirs, own_weight, other_weight, rotation)


def on_device(
    in_codes, in_scales, query_weight, kv_weight, out_weight, kv_cache, prefix_len, draft_parent
):
    rank = lax.axis_index(TENSOR)
    core = rank % 2
    head = rank // 8
    along_x = rank // 2 % 4
    place = jnp.stack(
        [core, jnp.where(core == 0, along_x, head), jnp.where(core == 0, head, along_x)]
    )
    signs = hadamard()
    scales = in_scales[0]

    near = jnp.stack([in_codes] + [first_shift(in_codes, k) for k in (1, 2, 3)])
    wq = in_hbm(query_weight[0])
    wq_other = in_hbm(traded(query_weight)[0])
    kv_other = traded(kv_weight)

    near, draft_parent, kv_weight, kv_other, out_weight = lax.optimization_barrier(
        (near, draft_parent, kv_weight, kv_other, out_weight)
    )

    far = {k: second_shift(near, k) for k in (1, 3, 2)}

    def as_rows(weight):
        return weight[0].transpose(2, 1, 3, 0).reshape(32, -1)

    wkv, wkv_other = as_rows(kv_weight), as_rows(kv_other)
    wo = in_hbm(out_weight[0])
    wo_other = in_hbm(traded(out_weight)[0])

    blocks = np.kron(np.eye(2, dtype=np.float32), signs)
    rotation = jnp.asarray(blocks, BF16)

    near_rows, kv_part = decode(
        (0,), 1, place, scales, (near,), rotation, wkv, wkv_other, jnp.zeros((4, 1, 16, 128), F32)
    )
    lengths, kv_part = lax.optimization_barrier((prefix_len, kv_part))

    ancestry = ancestor_table(draft_parent)
    position = lengths.astype(F32)[:, None] + (jnp.sum(ancestry, -1) - 1.0)
    frequency = jnp.power(ROPE_BASE, -(jnp.arange(64, dtype=F32) / 64))
    angles = position.reshape(128, 1) * frequency
    cosine, sine = jnp.cos(angles), jnp.sin(angles)
    cos_q = jnp.concatenate([cosine, cosine], 1)
    sin_q = jnp.concatenate([-sine, sine], 1)
    block = jnp.eye(8, dtype=F32)
    mask = (ancestry[:, :, None, :] * block[:, None, :, None]).reshape(128, 128)

    cos_t, sin_t = cosine.T, sine.T
    hops = (1, 3, 2)
    far_rows, kv_part = decode(
        hops,
        4,
        place,
        scales,
        tuple(far[k] for k in hops),
        rotation,
        wkv,
        wkv_other,
        in_hbm(kv_part),
        (mask, cos_q, sin_q, cos_t, sin_t, wq_other),
    )
    kv = exchanged(kv_part.reshape(CHIPS, 16, 128))
    own, other = project(
        ((0,), hops), place, (in_hbm(near_rows), in_hbm(far_rows)), wq, wq_other
    )
    other, kv = lax.optimization_barrier((other, kv))
    recv = traded(other)
    kv_recv = traded(kv)
    attended = attend(
        head.reshape(1), prefix_len, own, recv, kv, kv_recv, cos_t, sin_t, cos_q, sin_q, mask, kv_cache
    )
    theirs = traded(attended)
    twice = jnp.asarray(np.concatenate([signs, signs], 1), BF16)
    sent = {}
    for hops in ((2,), (1, 3), (0,)):
        for hop, piece in zip(hops, partials(hops, place, attended, theirs, wo, wo_other, twice)):
            sent[hop] = piece
    sums = sent[0]
    for k in (2, 1, 3):
        sums = sums + first_shift(sent[k], k).astype(F32)
    summed = sums[0]
    for k in (2, 1, 3):
        summed = summed + second_shift(sums[k].astype(BF16), k).astype(F32)

    here = lax.dynamic_slice_in_dim(scales, rank * 4, 4)
    turned_in = in_codes.T.astype(F32) * jnp.repeat(here, RB)[:, None]
    turned = summed + turned_in
    peak = jnp.max(jnp.abs(turned.reshape(4, RB, 128)), (1, 2))
    next_rows = swapped(turned, "section")
    spread = lax.dynamic_update_slice_in_dim(jnp.zeros((128,), F32), peak, rank * 4, 0)
    everyone = lax.all_to_all(
        jnp.broadcast_to(spread[None, None], (128, 1, 128)),
        ("section", "dp", TENSOR),
        0,
        0,
        tiled=True,
    )
    from_there = lax.dynamic_slice_in_dim(everyone, 64 * (1 - lax.axis_index("section")), 64)
    next_scales = jnp.max(from_there, (0, 1)) + TINY
    scale_here = lax.dynamic_slice_in_dim(next_scales, rank * 4, 4)
    next_codes = (next_rows.T / jnp.repeat(scale_here, RB)[None, :]).astype(BF16)
    return (next_codes, next_scales[None])


def solution(mesh):
    rows = ("section", "dp")
    placed = (
        P(rows, TENSOR),
        P("section", None),
        P("section", None, TENSOR),
        P("section", None, None, None, TENSOR),
        P("section", TENSOR, None),
        P(rows, None, None, None, None),
        P(rows),
        P(rows, None),
    )
    return jax.shard_map(
        on_device,
        mesh=mesh,
        in_specs=placed,
        out_specs=(P(rows, TENSOR), P("section", None)),
        check_vma=False,
    )
```

```python
import functools
import math

import jax
import jax.numpy as jnp
import numpy as np
from jax import lax
from jax.experimental import pallas as pl
from jax.experimental.pallas import tpu as pltpu
from jax.sharding import PartitionSpec as P

HD = 128
RB = 128
CHIPS = 16
ROPE_BASE = 500000.0
TINY = 1e-06
TENSOR = "tensor"


def device(y, x, core):
    return (y * 4 + x) * 2 + core


F32 = jnp.float32
BF16 = jnp.bfloat16
NT = (((1,), (1,)), ((), ()))
LIGHT = pl.CostEstimate(flops=1024, bytes_accessed=1024, transcendentals=0)


def hadamard():
    index = np.arange(RB)
    common = index[:, None] & index[None, :]
    parity = np.zeros((RB, RB), np.int32)
    for place in range(7):
        parity = parity + (common >> place & 1)
    return np.where(parity % 2 == 0, 1.0, -1.0).astype(np.float32)


def ancestor_table(draft_parent):
    count, size = draft_parent.shape
    target = lax.broadcasted_iota(jnp.int32, (count, size, size), 2)
    source = lax.broadcasted_iota(jnp.int32, (count, size, size), 1)
    table = ((target == draft_parent[:, :, None]) | (target == source)).astype(F32)
    for _ in range(4):
        table = jnp.minimum(jnp.einsum("rij,rjk->rik", table, table), 1.0)
    return table


def swapped(block, axis):
    return lax.ppermute(block, axis, [(0, 1), (1, 0)])


def traded(block):
    return lax.ppermute(block, TENSOR, [(i, i ^ 1) for i in range(32)])


def exchanged(pieces):
    groups = [[chip * 2 + core for chip in range(CHIPS)] for core in range(2)]
    return lax.all_to_all(pieces, TENSOR, 0, 0, tiled=True, axis_index_groups=groups)


def shifted(block, by, second):
    pairs = []
    for y in range(4):
        for x in range(4):
            for core in range(2):
                along_y = (core == 1) != second
                to_y, to_x = ((y + by) % 4, x) if along_y else (y, (x + by) % 4)
                pairs.append((device(y, x, core), device(to_y, to_x, core)))
    return lax.ppermute(block, TENSOR, pairs)


def first_shift(block, by):
    return shifted(block, by, False)


def second_shift(block, by):
    return shifted(block, by, True)


def chip_at(place, first, second):
    first = lax.rem(place[1] + 4 + first, 4)
    second = lax.rem(place[2] + 4 + second, 4)
    return jnp.where(place[0] == 0, second * 4 + first, first * 4 + second)


def in_hbm(array):
    return pltpu.with_memory_space_constraint(array, pltpu.HBM)


def params(mebibytes):
    return pltpu.CompilerParams(vmem_limit_bytes=mebibytes << 20)


def decode_kernel(hops, waits, place, scale_ref, *refs):
    codes_refs, refs = refs[: len(hops)], refs[len(hops) :]
    rotation_ref, own_weight, other_weight, kv_in = refs[:4]
    rows_ref, kv_out = refs[4 + waits :]
    own = other = None
    for i, hop in enumerate(hops):
        own_tiles, other_tiles = [], []
        for k in range(4):
            tile = chip_at(place, -k, -hop) * 2 + place[0]
            for half in range(2):
                product = jnp.dot(
                    codes_refs[i][k, :, half * 256 : half * 256 + 256],
                    rotation_ref[...],
                    preferred_element_type=F32,
                )
                for b in range(2):
                    factor = scale_ref[tile * 4 + half * 2 + b] * F32(1.0 / math.sqrt(RB))
                    at = i * 2048 + k * 512 + half * 256 + b * 128
                    rows_ref[:, at : at + 128] = (
                        product[:, b * 128 : b * 128 + 128] * factor
                    ).astype(BF16)
            column = pl.ds(pl.multiple_of(tile * 512, 512), 512)
            own_tiles.append(own_weight[:, column])
            other_tiles.append(other_weight[:, column])
        weight = jnp.concatenate(
            [jnp.concatenate(own_tiles, 1), jnp.concatenate(other_tiles, 1)], 0
        )
        total = lax.dot_general(
            weight,
            rows_ref[:, i * 2048 : i * 2048 + 2048],
            NT,
            preferred_element_type=F32,
        )
        own = total[:32] if own is None else own + total[:32]
        other = total[32:] if other is None else other + total[32:]
    for h in range(4):
        mine, theirs = own[h * 8 : h * 8 + 8], other[h * 8 : h * 8 + 8]
        value = kv_in[h, 0] + jnp.concatenate(
            [jnp.where(place[0] == 0, mine, theirs), jnp.where(place[0] == 0, theirs, mine)], 0
        )
        for i in range(kv_out.shape[1]):
            kv_out[h, i] = value


def decode(hops, copies, place, scales, codes, rotation, own_weight, other_weight, kv_in, after=()):
    def whole(array):
        return pl.BlockSpec(array.shape, lambda i, p, s: (0,) * array.ndim)

    arrays = (*codes, rotation, own_weight, other_weight, kv_in)
    outs = [(128, 2048 * len(hops)), (4, copies, 16, 128)]
    return pl.pallas_call(
        functools.partial(decode_kernel, hops, len(after)),
        grid_spec=pltpu.PrefetchScalarGridSpec(
            num_scalar_prefetch=2,
            grid=(1,),
            in_specs=[
                *(whole(array) for array in arrays),
                *(pl.BlockSpec(memory_space=pl.ANY) for _ in after),
            ],
            out_specs=[
                pl.BlockSpec(outs[0], lambda i, p, s: (0, 0)),
                pl.BlockSpec(outs[1], lambda i, p, s: (0, 0, 0, 0)),
            ],
        ),
        out_shape=[
            pltpu.HBM(outs[0], BF16),
            pltpu.HBM(outs[1], F32),
        ],
        compiler_params=params(16),
        cost_estimate=LIGHT,
        name="decode",
    )(place, scales, *arrays, *after)


def query_kernel(groups, place, *refs):
    rows_refs, refs = refs[: len(groups)], refs[len(groups) :]
    own_weight, other_weight, own_out, other_out, tiles, sems = refs
    parts = [
        (g, i * 4 + k, hop, k)
        for g, hops in enumerate(groups)
        for i, hop in enumerate(hops)
        for k in range(4)
    ]
    copies = []
    for n, (_, _, hop, k) in enumerate(parts):
        row = pl.multiple_of((chip_at(place, -k, -hop) * 2 + place[0]) * 512, 512)
        for side, weight in enumerate((own_weight, other_weight)):
            copies.append(
                pltpu.make_async_copy(
                    weight.at[pl.ds(row, 512), :], tiles.at[n, side], sems.at[n, side]
                )
            )
    for copy in copies:
        copy.start()
    totals = [jnp.zeros(own_out.shape, F32)] * 2
    for n, (g, at, _, _) in enumerate(parts):
        for side in range(2):
            copies[2 * n + side].wait()
            totals[side] += jnp.dot(
                rows_refs[g][:, at * 512 : at * 512 + 512],
                tiles[n, side],
                preferred_element_type=F32,
            )
    own_out[...] = totals[0]
    other_out[...] = totals[1]


def project(groups, place, rows, own_weight, other_weight):
    still = pl.BlockSpec((128, 256), lambda i, p: (0, 0))
    return pl.pallas_call(
        functools.partial(query_kernel, groups),
        grid_spec=pltpu.PrefetchScalarGridSpec(
            num_scalar_prefetch=1,
            grid=(1,),
            in_specs=[pl.BlockSpec(part.shape, lambda i, p: (0, 0)) for part in rows]
            + [pl.BlockSpec(memory_space=pltpu.HBM)] * 2,
            out_specs=[still, still],
            scratch_shapes=[
                pltpu.VMEM((CHIPS, 2, 512, 256), BF16),
                pltpu.SemaphoreType.DMA((CHIPS, 2)),
            ],
        ),
        out_shape=[jax.ShapeDtypeStruct((128, 256), F32)] * 2,
        compiler_params=params(20),
        cost_estimate=pl.CostEstimate(
            flops=2 * 128 * 8192 * 512, bytes_accessed=40 << 20, transcendentals=0
        ),
        name="query",
    )(place, *rows, own_weight, other_weight)


def attend_kernel(
    head_ref, length_ref, own_ref, recv_ref, kv_ref, kv_recv, cos_t, sin_t, cos_q, sin_q, mask_ref, cache_ref, out_ref
):
    score_scale = F32(1.0 / math.sqrt(HD))
    keys, values = [], []
    upper = lax.broadcasted_iota(jnp.int32, (8, 128), 0) < 4
    for chip in range(CHIPS):
        first = kv_ref[chip, 0:8] + kv_recv[chip, 0:8]
        second = kv_ref[chip, 8:16] + kv_recv[chip, 8:16]
        keys.append(jnp.where(upper, first, pltpu.roll(second, 4, 0)))
        values.append(jnp.where(upper, pltpu.roll(first, 4, 0), second))
    keys = jnp.concatenate(keys, 0).astype(BF16).astype(F32)
    values = jnp.concatenate(values, 0).astype(BF16)
    low, high = keys[:64], keys[64:]
    keys = jnp.concatenate(
        [low * cos_t[...] - high * sin_t[...], high * cos_t[...] + low * sin_t[...]], 0
    ).astype(BF16)
    heads = []
    for h in range(2):
        q = own_ref[:, h * 128 : h * 128 + 128] + recv_ref[:, h * 128 : h * 128 + 128]
        q = q * cos_q[...] + pltpu.roll(q, 64, 1) * sin_q[...]
        heads.append(q.astype(BF16))
    fresh = [
        jnp.dot(q, keys, preferred_element_type=F32) * score_scale for q in heads
    ]
    lane = lax.broadcasted_iota(jnp.int32, (32, 128), 1)
    for r in range(8):
        rows = slice(r * 16, r * 16 + 16)
        q = jnp.concatenate([heads[0][rows], heads[1][rows]], 0)
        old = (
            lax.dot_general(q, cache_ref[r, 0, 0], NT, preferred_element_type=F32) * score_scale
        )
        new = jnp.concatenate([fresh[0][rows], fresh[1][rows]], 0)
        mask = jnp.concatenate([mask_ref[rows, :]] * 2, 0)
        old = jnp.where(lane < length_ref[r], old, -jnp.inf)
        new = jnp.where(mask > 0.5, new, -jnp.inf)
        peak = jnp.maximum(
            jnp.max(old, -1, keepdims=True), jnp.max(new, -1, keepdims=True)
        )
        old = jnp.exp(old - peak)
        new = jnp.exp(new - peak)
        total = jnp.sum(old, -1, keepdims=True) + jnp.sum(new, -1, keepdims=True)
        old = (old / total).astype(BF16)
        new = (new / total).astype(BF16)
        mixed = jnp.dot(old, cache_ref[r, 0, 1], preferred_element_type=F32)
        mixed = mixed + lax.dot_general(new, values, NT, preferred_element_type=F32)
        mixed = mixed.astype(BF16)
        out_ref[rows, 0:128] = mixed[:16]
        out_ref[rows, 128:256] = mixed[16:]


def attend(head, lengths, own, recv, kv, kv_recv, cos_t, sin_t, cos_q, sin_q, mask, cache):
    def whole(array):
        return pl.BlockSpec(array.shape, lambda i, h, n: (0,) * array.ndim)

    arrays = (own, recv, kv, kv_recv, cos_t, sin_t, cos_q, sin_q, mask)
    return pl.pallas_call(
        attend_kernel,
        grid_spec=pltpu.PrefetchScalarGridSpec(
            num_scalar_prefetch=2,
            grid=(1,),
            in_specs=[whole(a) for a in arrays]
            + [pl.BlockSpec((8, 1, 2, 128, 128), lambda i, h, n: (0, h[0], 0, 0, 0))],
            out_specs=pl.BlockSpec((128, 256), lambda i, h, n: (0, 0)),
        ),
        out_shape=jax.ShapeDtypeStruct((128, 256), BF16),
        compiler_params=params(6),
        cost_estimate=pl.CostEstimate(
            flops=2 * 256 * 128 * 512, bytes_accessed=2 << 20, transcendentals=65536
        ),
        name="attend",
    )(head, lengths, *arrays, cache)


def partial_kernel(hops, place, mine, theirs, own_weight, other_weight, rotation_ref, *refs):
    outs, (tiles, sems) = refs[: len(hops)], refs[len(hops) :]
    unit = F32(1.0 / math.sqrt(RB))
    parts = [(out, at) for at in range(4) for out in range(len(hops))]
    copies = []
    for i, (out, at) in enumerate(parts):
        column = pl.multiple_of((chip_at(place, hops[out], at) * 2 + place[0]) * 512, 512)
        for side, weight in enumerate((own_weight, other_weight)):
            copies.append(
                pltpu.make_async_copy(
                    weight.at[:, pl.ds(column, 512)], tiles.at[i, side], sems.at[i, side]
                )
            )
    for copy in copies:
        copy.start()
    for i, (out, at) in enumerate(parts):
        copies[2 * i].wait()
        copies[2 * i + 1].wait()
        groups = (
            jnp.dot(mine[...], tiles[i, 0], preferred_element_type=F32),
            jnp.dot(theirs[...], tiles[i, 1], preferred_element_type=F32),
        )
        for b in range(4):
            halves = []
            for group in groups:
                block = group[:, b * 128 : b * 128 + 128]
                coarse = block.astype(BF16)
                fine = (block - coarse.astype(F32)).astype(BF16)
                halves.append(jnp.concatenate([coarse, fine], 1))
            both = lax.dot_general(
                rotation_ref[...],
                jnp.concatenate(halves, 0),
                NT,
                preferred_element_type=F32,
            )
            total = None
            for turned in (both[:, :128], both[:, 128:]):
                scale = jnp.max(jnp.abs(turned), 0, keepdims=True) * unit + TINY
                codes = (turned * (unit / scale)).astype(BF16)
                term = codes.astype(F32) * scale
                total = term if total is None else total + term
            outs[out][at, b * 128 : b * 128 + 128, :] = total.astype(outs[out].dtype)


def partials(hops, place, mine, theirs, own_weight, other_weight, rotation):
    count = 4 * len(hops)
    still = pl.BlockSpec((128, 256), lambda i, p: (0, 0))
    return pl.pallas_call(
        functools.partial(partial_kernel, hops),
        grid_spec=pltpu.PrefetchScalarGridSpec(
            num_scalar_prefetch=1,
            grid=(1,),
            in_specs=[still, still]
            + [pl.BlockSpec(memory_space=pltpu.HBM)] * 2
            + [still],
            out_specs=[pl.BlockSpec((4, 512, 128), lambda i, p: (0, 0, 0)) for _ in hops],
            scratch_shapes=[
                pltpu.VMEM((count, 2, 256, 512), BF16),
                pltpu.SemaphoreType.DMA((count, 2)),
            ],
        ),
        out_shape=[
            jax.ShapeDtypeStruct((4, 512, 128), BF16 if hop else F32) for hop in hops
        ],
        compiler_params=params(6 + 4 * len(hops)),
        cost_estimate=pl.CostEstimate(
            flops=2 * 128 * 2048 * 1024 * len(hops),
            bytes_accessed=len(hops) * 3 << 20,
            transcendentals=0,
        ),
        name="partials",
    )(place, mine, theirs, own_weight, other_weight, rotation)


def on_device(
    in_codes, in_scales, query_weight, kv_weight, out_weight, kv_cache, prefix_len, draft_parent
):
    rank = lax.axis_index(TENSOR)
    core = rank % 2
    head = rank // 8
    along_x = rank // 2 % 4
    place = jnp.stack(
        [core, jnp.where(core == 0, along_x, head), jnp.where(core == 0, head, along_x)]
    )
    signs = hadamard()
    scales = in_scales[0]

    arrived = {k: first_shift(in_codes, k) for k in (2, 1, 3)}
    near = jnp.stack([in_codes] + [arrived[k] for k in (1, 2, 3)])
    wq = in_hbm(query_weight[0])
    wq_other = in_hbm(traded(query_weight)[0])
    kv_other = traded(kv_weight)

    near, draft_parent, kv_weight, kv_other, out_weight = lax.optimization_barrier(
        (near, draft_parent, kv_weight, kv_other, out_weight)
    )

    far = {k: second_shift(near, k) for k in (2, 1, 3)}

    def as_rows(weight):
        return weight[0].transpose(2, 1, 3, 0).reshape(32, -1)

    wkv, wkv_other = as_rows(kv_weight), as_rows(kv_other)
    wo = in_hbm(out_weight[0])
    wo_other = in_hbm(traded(out_weight)[0])

    blocks = np.kron(np.eye(2, dtype=np.float32), signs)
    rotation = jnp.asarray(blocks, BF16)

    near_rows, kv_part = decode(
        (0,), 1, place, scales, (near,), rotation, wkv, wkv_other, jnp.zeros((4, 1, 16, 128), F32)
    )
    lengths, kv_part = lax.optimization_barrier((prefix_len, kv_part))

    ancestry = ancestor_table(draft_parent)
    position = lengths.astype(F32)[:, None] + (jnp.sum(ancestry, -1) - 1.0)
    frequency = jnp.power(ROPE_BASE, -(jnp.arange(64, dtype=F32) / 64))
    angles = position.reshape(128, 1) * frequency
    cosine, sine = jnp.cos(angles), jnp.sin(angles)
    cos_q = jnp.concatenate([cosine, cosine], 1)
    sin_q = jnp.concatenate([-sine, sine], 1)
    block = jnp.eye(8, dtype=F32)
    mask = (ancestry[:, :, None, :] * block[:, None, :, None]).reshape(128, 128)

    cos_t, sin_t = cosine.T, sine.T
    hops = (2, 1, 3)
    far_rows, kv_part = decode(
        hops,
        4,
        place,
        scales,
        tuple(far[k] for k in hops),
        rotation,
        wkv,
        wkv_other,
        in_hbm(kv_part),
        (mask, cos_q, sin_q, cos_t, sin_t, wq_other),
    )
    kv = exchanged(kv_part.reshape(CHIPS, 16, 128))
    own, other = project(
        ((0,), hops), place, (in_hbm(near_rows), in_hbm(far_rows)), wq, wq_other
    )
    other, kv = lax.optimization_barrier((other, kv))
    recv = traded(other)
    kv_recv = traded(kv)
    attended = attend(
        head.reshape(1), prefix_len, own, recv, kv, kv_recv, cos_t, sin_t, cos_q, sin_q, mask, kv_cache
    )
    theirs = traded(attended)
    twice = jnp.asarray(np.concatenate([signs, signs], 1), BF16)
    sent = {}
    for hops in ((2,), (1, 3), (0,)):
        for hop, piece in zip(hops, partials(hops, place, attended, theirs, wo, wo_other, twice)):
            sent[hop] = piece
    sums = sent[0]
    for k in (2, 1, 3):
        sums = sums + first_shift(sent[k], k).astype(F32)
    summed = sums[0]
    for k in (2, 1, 3):
        summed = summed + second_shift(sums[k].astype(BF16), k).astype(F32)

    here = lax.dynamic_slice_in_dim(scales, rank * 4, 4)
    turned_in = in_codes.T.astype(F32) * jnp.repeat(here, RB)[:, None]
    turned = summed + turned_in
    peak = jnp.max(jnp.abs(turned.reshape(4, RB, 128)), (1, 2))
    next_rows = swapped(turned, "section")
    spread = lax.dynamic_update_slice_in_dim(jnp.zeros((128,), F32), peak, rank * 4, 0)
    everyone = lax.all_to_all(
        jnp.broadcast_to(spread[None, None], (128, 1, 128)),
        ("section", "dp", TENSOR),
        0,
        0,
        tiled=True,
    )
    from_there = lax.dynamic_slice_in_dim(everyone, 64 * (1 - lax.axis_index("section")), 64)
    next_scales = jnp.max(from_there, (0, 1)) + TINY
    scale_here = lax.dynamic_slice_in_dim(next_scales, rank * 4, 4)
    next_codes = (next_rows.T / jnp.repeat(scale_here, RB)[None, :]).astype(BF16)
    return (next_codes, next_scales[None])


def solution(mesh):
    rows = ("section", "dp")
    placed = (
        P(rows, TENSOR),
        P("section", None),
        P("section", None, TENSOR),
        P("section", None, None, None, TENSOR),
        P("section", TENSOR, None),
        P(rows, None, None, None, None),
        P(rows),
        P(rows, None),
    )
    return jax.shard_map(
        on_device,
        mesh=mesh,
        in_specs=placed,
        out_specs=(P(rows, TENSOR), P("section", None)),
        check_vma=False,
    )
```

```python
import functools
import math

import jax
import jax.numpy as jnp
import numpy as np
from jax import lax
from jax.experimental import pallas as pl
from jax.experimental.pallas import tpu as pltpu
from jax.sharding import PartitionSpec as P

HD = 128
RB = 128
CHIPS = 16
ROPE_BASE = 500000.0
TINY = 1e-06
TENSOR = "tensor"


def device(y, x, core):
    return (y * 4 + x) * 2 + core


F32 = jnp.float32
BF16 = jnp.bfloat16
NT = (((1,), (1,)), ((), ()))
LIGHT = pl.CostEstimate(flops=1024, bytes_accessed=1024, transcendentals=0)


def hadamard():
    index = np.arange(RB)
    common = index[:, None] & index[None, :]
    parity = np.zeros((RB, RB), np.int32)
    for place in range(7):
        parity = parity + (common >> place & 1)
    return np.where(parity % 2 == 0, 1.0, -1.0).astype(np.float32)


def ancestor_table(draft_parent):
    count, size = draft_parent.shape
    target = lax.broadcasted_iota(jnp.int32, (count, size, size), 2)
    source = lax.broadcasted_iota(jnp.int32, (count, size, size), 1)
    table = ((target == draft_parent[:, :, None]) | (target == source)).astype(F32)
    for _ in range(4):
        table = jnp.minimum(jnp.einsum("rij,rjk->rik", table, table), 1.0)
    return table


def swapped(block, axis):
    return lax.ppermute(block, axis, [(0, 1), (1, 0)])


def traded(block):
    return lax.ppermute(block, TENSOR, [(i, i ^ 1) for i in range(32)])


def exchanged(pieces):
    groups = [[chip * 2 + core for chip in range(CHIPS)] for core in range(2)]
    return lax.all_to_all(pieces, TENSOR, 0, 0, tiled=True, axis_index_groups=groups)


def shifted(block, by, second):
    pairs = []
    for y in range(4):
        for x in range(4):
            for core in range(2):
                along_y = (core == 1) != second
                to_y, to_x = ((y + by) % 4, x) if along_y else (y, (x + by) % 4)
                pairs.append((device(y, x, core), device(to_y, to_x, core)))
    return lax.ppermute(block, TENSOR, pairs)


def first_shift(block, by):
    return shifted(block, by, False)


def second_shift(block, by):
    return shifted(block, by, True)


def chip_at(place, first, second):
    first = lax.rem(place[1] + 4 + first, 4)
    second = lax.rem(place[2] + 4 + second, 4)
    return jnp.where(place[0] == 0, second * 4 + first, first * 4 + second)


def in_hbm(array):
    return pltpu.with_memory_space_constraint(array, pltpu.HBM)


def params(mebibytes):
    return pltpu.CompilerParams(vmem_limit_bytes=mebibytes << 20)


def decode_kernel(hops, waits, place, scale_ref, *refs):
    codes_refs, refs = refs[: len(hops)], refs[len(hops) :]
    rotation_ref, own_weight, other_weight, kv_in = refs[:4]
    rows_ref, kv_out = refs[4 + waits :]
    own = other = None
    for i, hop in enumerate(hops):
        own_tiles, other_tiles = [], []
        for k in range(4):
            tile = chip_at(place, -k, -hop) * 2 + place[0]
            for half in range(2):
                product = jnp.dot(
                    codes_refs[i][k, :, half * 256 : half * 256 + 256],
                    rotation_ref[...],
                    preferred_element_type=F32,
                )
                for b in range(2):
                    factor = scale_ref[tile * 4 + half * 2 + b] * F32(1.0 / math.sqrt(RB))
                    at = i * 2048 + k * 512 + half * 256 + b * 128
                    rows_ref[:, at : at + 128] = (
                        product[:, b * 128 : b * 128 + 128] * factor
                    ).astype(BF16)
            column = pl.ds(pl.multiple_of(tile * 512, 512), 512)
            own_tiles.append(own_weight[:, column])
            other_tiles.append(other_weight[:, column])
        weight = jnp.concatenate(
            [jnp.concatenate(own_tiles, 1), jnp.concatenate(other_tiles, 1)], 0
        )
        total = lax.dot_general(
            weight,
            rows_ref[:, i * 2048 : i * 2048 + 2048],
            NT,
            preferred_element_type=F32,
        )
        own = total[:32] if own is None else own + total[:32]
        other = total[32:] if other is None else other + total[32:]
    for h in range(4):
        mine, theirs = own[h * 8 : h * 8 + 8], other[h * 8 : h * 8 + 8]
        value = kv_in[h, 0] + jnp.concatenate(
            [jnp.where(place[0] == 0, mine, theirs), jnp.where(place[0] == 0, theirs, mine)], 0
        )
        for i in range(kv_out.shape[1]):
            kv_out[h, i] = value


def decode(hops, copies, place, scales, codes, rotation, own_weight, other_weight, kv_in, after=()):
    def whole(array):
        return pl.BlockSpec(array.shape, lambda i, p, s: (0,) * array.ndim)

    arrays = (*codes, rotation, own_weight, other_weight, kv_in)
    outs = [(128, 2048 * len(hops)), (4, copies, 16, 128)]
    return pl.pallas_call(
        functools.partial(decode_kernel, hops, len(after)),
        grid_spec=pltpu.PrefetchScalarGridSpec(
            num_scalar_prefetch=2,
            grid=(1,),
            in_specs=[
                *(whole(array) for array in arrays),
                *(pl.BlockSpec(memory_space=pl.ANY) for _ in after),
            ],
            out_specs=[
                pl.BlockSpec(outs[0], lambda i, p, s: (0, 0)),
                pl.BlockSpec(outs[1], lambda i, p, s: (0, 0, 0, 0)),
            ],
        ),
        out_shape=[
            pltpu.HBM(outs[0], BF16),
            pltpu.HBM(outs[1], F32),
        ],
        compiler_params=params(16),
        cost_estimate=LIGHT,
        name="decode",
    )(place, scales, *arrays, *after)


def query_kernel(groups, place, *refs):
    rows_refs, refs = refs[: len(groups)], refs[len(groups) :]
    own_weight, other_weight, own_out, other_out, tiles, sems = refs
    parts = [
        (g, i * 4 + k, hop, k)
        for g, hops in enumerate(groups)
        for i, hop in enumerate(hops)
        for k in range(4)
    ]
    copies = []
    for n, (_, _, hop, k) in enumerate(parts):
        row = pl.multiple_of((chip_at(place, -k, -hop) * 2 + place[0]) * 512, 512)
        for side, weight in enumerate((own_weight, other_weight)):
            copies.append(
                pltpu.make_async_copy(
                    weight.at[pl.ds(row, 512), :], tiles.at[n, side], sems.at[n, side]
                )
            )
    for copy in copies:
        copy.start()
    totals = [jnp.zeros(own_out.shape, F32)] * 2
    for n, (g, at, _, _) in enumerate(parts):
        for side in range(2):
            copies[2 * n + side].wait()
            totals[side] += jnp.dot(
                rows_refs[g][:, at * 512 : at * 512 + 512],
                tiles[n, side],
                preferred_element_type=F32,
            )
    own_out[...] = totals[0]
    other_out[...] = totals[1]


def project(groups, place, rows, own_weight, other_weight):
    still = pl.BlockSpec((128, 256), lambda i, p: (0, 0))
    return pl.pallas_call(
        functools.partial(query_kernel, groups),
        grid_spec=pltpu.PrefetchScalarGridSpec(
            num_scalar_prefetch=1,
            grid=(1,),
            in_specs=[pl.BlockSpec(part.shape, lambda i, p: (0, 0)) for part in rows]
            + [pl.BlockSpec(memory_space=pltpu.HBM)] * 2,
            out_specs=[still, still],
            scratch_shapes=[
                pltpu.VMEM((CHIPS, 2, 512, 256), BF16),
                pltpu.SemaphoreType.DMA((CHIPS, 2)),
            ],
        ),
        out_shape=[jax.ShapeDtypeStruct((128, 256), F32)] * 2,
        compiler_params=params(20),
        cost_estimate=pl.CostEstimate(
            flops=2 * 128 * 8192 * 512, bytes_accessed=40 << 20, transcendentals=0
        ),
        name="query",
    )(place, *rows, own_weight, other_weight)


def attend_kernel(
    head_ref, length_ref, own_ref, recv_ref, kv_ref, kv_recv, cos_t, sin_t, cos_q, sin_q, mask_ref, cache_ref, out_ref
):
    score_scale = F32(1.0 / math.sqrt(HD))
    keys, values = [], []
    upper = lax.broadcasted_iota(jnp.int32, (8, 128), 0) < 4
    for chip in range(CHIPS):
        first = kv_ref[chip, 0:8] + kv_recv[chip, 0:8]
        second = kv_ref[chip, 8:16] + kv_recv[chip, 8:16]
        keys.append(jnp.where(upper, first, pltpu.roll(second, 4, 0)))
        values.append(jnp.where(upper, pltpu.roll(first, 4, 0), second))
    keys = jnp.concatenate(keys, 0).astype(BF16).astype(F32)
    values = jnp.concatenate(values, 0).astype(BF16)
    low, high = keys[:64], keys[64:]
    keys = jnp.concatenate(
        [low * cos_t[...] - high * sin_t[...], high * cos_t[...] + low * sin_t[...]], 0
    ).astype(BF16)
    heads = []
    for h in range(2):
        q = own_ref[:, h * 128 : h * 128 + 128] + recv_ref[:, h * 128 : h * 128 + 128]
        q = q * cos_q[...] + pltpu.roll(q, 64, 1) * sin_q[...]
        heads.append(q.astype(BF16))
    fresh = [
        jnp.dot(q, keys, preferred_element_type=F32) * score_scale for q in heads
    ]
    lane = lax.broadcasted_iota(jnp.int32, (32, 128), 1)
    for r in range(8):
        rows = slice(r * 16, r * 16 + 16)
        q = jnp.concatenate([heads[0][rows], heads[1][rows]], 0)
        old = (
            lax.dot_general(q, cache_ref[r, 0, 0], NT, preferred_element_type=F32) * score_scale
        )
        new = jnp.concatenate([fresh[0][rows], fresh[1][rows]], 0)
        mask = jnp.concatenate([mask_ref[rows, :]] * 2, 0)
        old = jnp.where(lane < length_ref[r], old, -jnp.inf)
        new = jnp.where(mask > 0.5, new, -jnp.inf)
        peak = jnp.maximum(
            jnp.max(old, -1, keepdims=True), jnp.max(new, -1, keepdims=True)
        )
        old = jnp.exp(old - peak)
        new = jnp.exp(new - peak)
        total = jnp.sum(old, -1, keepdims=True) + jnp.sum(new, -1, keepdims=True)
        old = (old / total).astype(BF16)
        new = (new / total).astype(BF16)
        mixed = jnp.dot(old, cache_ref[r, 0, 1], preferred_element_type=F32)
        mixed = mixed + lax.dot_general(new, values, NT, preferred_element_type=F32)
        mixed = mixed.astype(BF16)
        out_ref[rows, 0:128] = mixed[:16]
        out_ref[rows, 128:256] = mixed[16:]


def attend(head, lengths, own, recv, kv, kv_recv, cos_t, sin_t, cos_q, sin_q, mask, cache):
    def whole(array):
        return pl.BlockSpec(array.shape, lambda i, h, n: (0,) * array.ndim)

    arrays = (own, recv, kv, kv_recv, cos_t, sin_t, cos_q, sin_q, mask)
    return pl.pallas_call(
        attend_kernel,
        grid_spec=pltpu.PrefetchScalarGridSpec(
            num_scalar_prefetch=2,
            grid=(1,),
            in_specs=[whole(a) for a in arrays]
            + [pl.BlockSpec((8, 1, 2, 128, 128), lambda i, h, n: (0, h[0], 0, 0, 0))],
            out_specs=pl.BlockSpec((128, 256), lambda i, h, n: (0, 0)),
        ),
        out_shape=jax.ShapeDtypeStruct((128, 256), BF16),
        compiler_params=params(6),
        cost_estimate=pl.CostEstimate(
            flops=2 * 256 * 128 * 512, bytes_accessed=2 << 20, transcendentals=65536
        ),
        name="attend",
    )(head, lengths, *arrays, cache)


def partial_kernel(hops, place, mine, theirs, own_weight, other_weight, rotation_ref, *refs):
    outs, (tiles, sems) = refs[: len(hops)], refs[len(hops) :]
    unit = F32(1.0 / math.sqrt(RB))
    parts = [(out, at) for at in range(4) for out in range(len(hops))]
    copies = []
    for i, (out, at) in enumerate(parts):
        column = pl.multiple_of((chip_at(place, hops[out], at) * 2 + place[0]) * 512, 512)
        for side, weight in enumerate((own_weight, other_weight)):
            copies.append(
                pltpu.make_async_copy(
                    weight.at[:, pl.ds(column, 512)], tiles.at[i, side], sems.at[i, side]
                )
            )
    for copy in copies:
        copy.start()
    for i, (out, at) in enumerate(parts):
        copies[2 * i].wait()
        copies[2 * i + 1].wait()
        groups = (
            jnp.dot(mine[...], tiles[i, 0], preferred_element_type=F32),
            jnp.dot(theirs[...], tiles[i, 1], preferred_element_type=F32),
        )
        for b in range(4):
            halves = []
            for group in groups:
                block = group[:, b * 128 : b * 128 + 128]
                coarse = block.astype(BF16)
                fine = (block - coarse.astype(F32)).astype(BF16)
                halves.append(jnp.concatenate([coarse, fine], 1))
            both = lax.dot_general(
                rotation_ref[...],
                jnp.concatenate(halves, 0),
                NT,
                preferred_element_type=F32,
            )
            total = None
            for turned in (both[:, :128], both[:, 128:]):
                scale = jnp.max(jnp.abs(turned), 0, keepdims=True) * unit + TINY
                codes = (turned * (unit / scale)).astype(BF16)
                term = codes.astype(F32) * scale
                total = term if total is None else total + term
            outs[out][at, b * 128 : b * 128 + 128, :] = total.astype(outs[out].dtype)


def partials(hops, place, mine, theirs, own_weight, other_weight, rotation):
    count = 4 * len(hops)
    still = pl.BlockSpec((128, 256), lambda i, p: (0, 0))
    return pl.pallas_call(
        functools.partial(partial_kernel, hops),
        grid_spec=pltpu.PrefetchScalarGridSpec(
            num_scalar_prefetch=1,
            grid=(1,),
            in_specs=[still, still]
            + [pl.BlockSpec(memory_space=pltpu.HBM)] * 2
            + [still],
            out_specs=[pl.BlockSpec((4, 512, 128), lambda i, p: (0, 0, 0)) for _ in hops],
            scratch_shapes=[
                pltpu.VMEM((count, 2, 256, 512), BF16),
                pltpu.SemaphoreType.DMA((count, 2)),
            ],
        ),
        out_shape=[
            jax.ShapeDtypeStruct((4, 512, 128), BF16 if hop else F32) for hop in hops
        ],
        compiler_params=params(6 + 4 * len(hops)),
        cost_estimate=pl.CostEstimate(
            flops=2 * 128 * 2048 * 1024 * len(hops),
            bytes_accessed=len(hops) * 3 << 20,
            transcendentals=0,
        ),
        name="partials",
    )(place, mine, theirs, own_weight, other_weight, rotation)


def on_device(
    in_codes, in_scales, query_weight, kv_weight, out_weight, kv_cache, prefix_len, draft_parent
):
    rank = lax.axis_index(TENSOR)
    core = rank % 2
    head = rank // 8
    along_x = rank // 2 % 4
    place = jnp.stack(
        [core, jnp.where(core == 0, along_x, head), jnp.where(core == 0, head, along_x)]
    )
    signs = hadamard()
    scales = in_scales[0]

    near = jnp.stack([in_codes] + [first_shift(in_codes, k) for k in (1, 2, 3)])
    wq = in_hbm(query_weight[0])
    wq_other = in_hbm(traded(query_weight)[0])
    kv_other = traded(kv_weight)

    near, draft_parent, kv_weight, kv_other, out_weight = lax.optimization_barrier(
        (near, draft_parent, kv_weight, kv_other, out_weight)
    )

    far = {k: second_shift(near, k) for k in (1, 3, 2)}

    def as_rows(weight):
        return weight[0].transpose(2, 1, 3, 0).reshape(32, -1)

    wkv, wkv_other = as_rows(kv_weight), as_rows(kv_other)
    wo = in_hbm(out_weight[0])
    wo_other = in_hbm(traded(out_weight)[0])

    blocks = np.kron(np.eye(2, dtype=np.float32), signs)
    rotation = jnp.asarray(blocks, BF16)

    lengths, ancestry = lax.optimization_barrier((prefix_len, ancestor_table(draft_parent)))
    position = lengths.astype(F32)[:, None] + (jnp.sum(ancestry, -1) - 1.0)
    frequency = jnp.power(ROPE_BASE, -(jnp.arange(64, dtype=F32) / 64))
    angles = position.reshape(128, 1) * frequency
    cosine, sine = jnp.cos(angles), jnp.sin(angles)
    cos_q = jnp.concatenate([cosine, cosine], 1)
    sin_q = jnp.concatenate([-sine, sine], 1)
    block = jnp.eye(8, dtype=F32)
    mask = (ancestry[:, :, None, :] * block[:, None, :, None]).reshape(128, 128)

    cos_t, sin_t = cosine.T, sine.T
    hops = (0, 1, 3, 2)
    rows, kv_part = decode(
        hops,
        4,
        place,
        scales,
        (near, far[1], far[3], far[2]),
        rotation,
        wkv,
        wkv_other,
        jnp.zeros((4, 1, 16, 128), F32),
        (mask, cos_q, sin_q, cos_t, sin_t, wq_other),
    )
    kv = exchanged(kv_part.reshape(CHIPS, 16, 128))
    own, other = project(
        (hops,), place, (in_hbm(rows),), wq, wq_other
    )
    other, kv = lax.optimization_barrier((other, kv))
    recv = traded(other)
    kv_recv = traded(kv)
    attended = attend(
        head.reshape(1), prefix_len, own, recv, kv, kv_recv, cos_t, sin_t, cos_q, sin_q, mask, kv_cache
    )
    theirs = traded(attended)
    twice = jnp.asarray(np.concatenate([signs, signs], 1), BF16)
    sent = {}
    for hops in ((2,), (1, 3), (0,)):
        for hop, piece in zip(hops, partials(hops, place, attended, theirs, wo, wo_other, twice)):
            sent[hop] = piece
    sums = sent[0]
    for k in (2, 1, 3):
        sums = sums + first_shift(sent[k], k).astype(F32)
    summed = sums[0]
    for k in (2, 1, 3):
        summed = summed + second_shift(sums[k].astype(BF16), k).astype(F32)

    here = lax.dynamic_slice_in_dim(scales, rank * 4, 4)
    turned_in = in_codes.T.astype(F32) * jnp.repeat(here, RB)[:, None]
    turned = summed + turned_in
    peak = jnp.max(jnp.abs(turned.reshape(4, RB, 128)), (1, 2))
    next_rows = swapped(turned, "section")
    spread = lax.dynamic_update_slice_in_dim(jnp.zeros((128,), F32), peak, rank * 4, 0)
    everyone = lax.all_to_all(
        jnp.broadcast_to(spread[None, None], (128, 1, 128)),
        ("section", "dp", TENSOR),
        0,
        0,
        tiled=True,
    )
    from_there = lax.dynamic_slice_in_dim(everyone, 64 * (1 - lax.axis_index("section")), 64)
    next_scales = jnp.max(from_there, (0, 1)) + TINY
    scale_here = lax.dynamic_slice_in_dim(next_scales, rank * 4, 4)
    next_codes = (next_rows.T / jnp.repeat(scale_here, RB)[None, :]).astype(BF16)
    return (next_codes, next_scales[None])


def solution(mesh):
    rows = ("section", "dp")
    placed = (
        P(rows, TENSOR),
        P("section", None),
        P("section", None, TENSOR),
        P("section", None, None, None, TENSOR),
        P("section", TENSOR, None),
        P(rows, None, None, None, None),
        P(rows),
        P(rows, None),
    )
    return jax.shard_map(
        on_device,
        mesh=mesh,
        in_specs=placed,
        out_specs=(P(rows, TENSOR), P("section", None)),
        check_vma=False,
    )
```
